256 devices in a mesh: pt: 32 (over y, z), comp: 8 (over x, core).
Axes of the slice: x: 4, y: 4, z: 8, core: 2. Of those that a mesh axis runs over, the one named last changes fastest.
Arguments:
- points: bfloat16 [16384, 1024], P(('pt', 'comp')), may hold values from -64 to 64
- means: bfloat16 [16384, 1024], P('comp'), may hold values from -2 to 2
- log_weights: float32 [16384], P('comp'), may hold values from -3 to 3
- inv_var: float32 [1024], replicated, may hold values from 0.03 to 0.3
Outputs:
- resp: bfloat16 [16384, 16384], P(('pt', 'comp'))
- counts: float32 [16384], P('comp')
- new_means_t: float32 [1024, 16384], P('pt', 'comp')
- loglik: float32 [16384], P(('pt', 'comp'))
The draws below stay inside these ranges and needn't reach their ends.
All inputs are finite; a program needn't handle non-finite values.
Results may differ from the reference program's by a relative error of at most 0.0074.
Values may be sent and summed in bfloat16 or wider, within the bound.
No kernel may reach another device: no remote copies, remote signals or barrier semaphores. Data moves between devices by JAX's collectives and lax.ppermute only.
A program may use at most 128 MiB of HBM per device.

```python
import math
import jax
import jax.numpy as jnp
from jax import lax

D = 1024
K = 16384
ROWS_PT = 512
NPTS = 16384


cluster_count = 256


def base_means(key):
    return 0.3 * jnp.clip(jax.random.normal(jax.random.fold_in(key, 1), (K, D), jnp.float32), -5.0, 5.0)


def draw_means(key, part):
    values = base_means(key)
    return values.astype(jnp.bfloat16)


def draw_points(key, part):
    member = jax.random.randint(jax.random.fold_in(key, 9), (NPTS,), 0, cluster_count)
    centers = jnp.clip(jax.random.normal(jax.random.fold_in(key, 8), (cluster_count, D), jnp.float32), -3.0, 3.0)
    noise = jnp.clip(jax.random.normal(jax.random.fold_in(key, 2), (NPTS, D), jnp.float32), -6.0, 6.0)
    values = centers[member] + noise
    return values.astype(jnp.bfloat16)


def levels(rng, dims, shards, low, high):
    def one(dim, parts):
        steps = jax.random.uniform(jax.random.fold_in(jax.random.fold_in(rng, 6), dim), (parts,), jnp.float32, low / len(shards), high / len(shards))
        return jnp.repeat(jnp.exp(steps), dims[dim] // parts).reshape((-1,) + (1,) * (len(dims) - dim - 1))

    level = one(*shards[0])
    for cut in shards[1:]:
        level = level * one(*cut)
    return level


def centred(rng, shape, width, limit, cuts=(), kind=jnp.bfloat16):
    gain = levels(rng, shape, cuts, -0.22, 0.18) if cuts else 1.0
    values = jax.random.normal(rng, shape, jnp.float32) * width * gain
    return jnp.minimum(jnp.maximum(values, -limit), limit).astype(kind)


def setup_inputs(seed: int = 0) -> dict:
    streams_of = jax.random.split(jax.random.key(seed), 5)
    points = draw_points(jax.random.fold_in(streams_of[4], 71), 0)
    means = draw_means(jax.random.fold_in(streams_of[4], 71), 0)
    log_weights = centred(streams_of[2], (K,), 0.5, 3.0, ((0, 8),), jnp.float32)
    inv_var = jnp.clip(jnp.exp(jax.random.uniform(streams_of[3], (D,), jnp.float32, math.log(0.03), math.log(0.3))), 0.03, 0.3)
    return dict(points=points, means=means, log_weights=log_weights, inv_var=inv_var)


def reference(points, means, log_weights, inv_var):
    means_f = means.astype(jnp.float32)
    scaled = (means_f * inv_var[None, :]).astype(jnp.bfloat16)
    half_norm = 0.5 * jnp.sum(means_f * means_f * inv_var[None, :], axis=1)
    const_term = 0.5 * jnp.sum(jnp.log(inv_var)) - 0.5 * D * math.log(2.0 * math.pi)
    blocks = points.reshape(NPTS // ROWS_PT, ROWS_PT, D)

    def step(carry, block):
        sums_t, counts = carry
        score = lax.dot_general(block, scaled, (((1,), (1,)), ((), ())), preferred_element_type=jnp.float32)
        score = score - half_norm[None, :] + log_weights[None, :]
        peak = jnp.max(score, axis=1)
        total = jnp.sum(jnp.exp(score - peak[:, None]), axis=1)
        lse = peak + jnp.log(total)
        resp = jnp.exp(score - lse[:, None]).astype(jnp.bfloat16)
        counts = counts + jnp.sum(resp.astype(jnp.float32), axis=0)
        sums_t = sums_t + lax.dot_general(block, resp, (((0,), (0,)), ((), ())), preferred_element_type=jnp.float32)
        block_f = block.astype(jnp.float32)
        loglik = lse - 0.5 * jnp.sum(block_f * block_f * inv_var[None, :], axis=1) + const_term
        return (sums_t, counts), (resp, loglik)

    start = (jnp.zeros((D, K), jnp.float32), jnp.zeros((K,), jnp.float32))
    (sums_t, counts), (resp, loglik) = lax.scan(step, start, blocks)
    new_means_t = (sums_t + means_f.T) / (counts[None, :] + 1.0)
    return resp.reshape(NPTS, K), counts, new_means_t, loglik.reshape(NPTS)
```

```python
import functools
import math

import jax
import jax.numpy as jnp
from jax import lax
from jax.experimental import pallas as pl
from jax.experimental.pallas import tpu as pltpu
from jax.sharding import Mesh
from jax.sharding import PartitionSpec as P

BF = jnp.bfloat16
F32 = jnp.float32
VMEM_LIMIT = 48 * 1024 * 1024
VMEM = pltpu.VMEM
SIZES = {"y": 4, "z": 8, "x": 4, "c": 2}


def shift(value, axis, step):
    n = SIZES[axis]
    return lax.ppermute(value, axis, [(i, (i + step) % n) for i in range(n)])


def params():
    return pltpu.CompilerParams(vmem_limit_bytes=VMEM_LIMIT)


def whole():
    return pl.BlockSpec(memory_space=VMEM)


def scalar():
    return pl.BlockSpec(memory_space=pltpu.SMEM)


def place_kernel(at, own, before, after, far, out):
    x = at[0]
    for step, piece in ((0, own), (3, before), (1, after), (2, far)):
        slot = lax.rem(x + step, 4)
        out[pl.ds(pl.multiple_of(slot * 64, 64), 64), :] = piece[...]


def place(at, own, before, after, far):
    return pl.pallas_call(
        place_kernel,
        out_shape=jax.ShapeDtypeStruct((256, 1024), BF),
        in_specs=[scalar()] + [whole()] * 4,
        out_specs=whole(),
        compiler_params=params(),
    )(at, own, before, after, far)


def gather_x(at, own):
    return place(at, own, shift(own, "x", 1), shift(own, "x", -1), shift(own, "x", 2))


def column(row):
    return jnp.transpose(jnp.broadcast_to(row, (128, 128)))[:, 0:1]


def score_kernel(at, own, other, scaled, bias, score, share, rows, peak, total):
    step = pl.program_id(0)
    c = at[1]

    @pl.when(step == 0)
    def _():
        rows[pl.ds(pl.multiple_of(c * 256, 256), 256), :] = own[...]
        rows[pl.ds(pl.multiple_of((1 - c) * 256, 256), 256), :] = other[...]
        peak[...] = jnp.full_like(peak, -jnp.inf)
        total[...] = jnp.zeros_like(total)

    tile = lax.dot_general(
        rows[...], scaled[...], (((1,), (1,)), ((), ())), preferred_element_type=F32
    )
    tile = tile + bias[...]
    score[...] = tile
    top = jnp.maximum(peak[...], jnp.max(tile, axis=1, keepdims=True))
    total[...] = total[...] * jnp.exp(peak[...] - top) + jnp.sum(
        jnp.exp(tile - top), axis=1, keepdims=True
    )
    peak[...] = top

    @pl.when(step == pl.num_programs(0) - 1)
    def _():
        lse = peak[...] + jnp.log(total[...])
        for b in range(4):
            part = jnp.broadcast_to(lse[b * 128 : (b + 1) * 128], (128, 128))
            line = jnp.transpose(part)[0:1, :]
            share[:, b, :] = jnp.broadcast_to(line, (32, 128))


def scores(at, own, other, scaled, bias_row):
    width = 512
    return pl.pallas_call(
        score_kernel,
        grid=(2048 // width,),
        out_shape=(
            jax.ShapeDtypeStruct((512, 2048), F32),
            jax.ShapeDtypeStruct((32, 4, 128), F32),
        ),
        in_specs=[
            scalar(),
            pl.BlockSpec((256, 1024), lambda i: (0, 0)),
            pl.BlockSpec((256, 1024), lambda i: (0, 0)),
            pl.BlockSpec((width, 1024), lambda i: (i, 0)),
            pl.BlockSpec((1, width), lambda i: (0, i)),
        ],
        out_specs=(
            pl.BlockSpec((512, width), lambda i: (0, i)),
            pl.BlockSpec((32, 4, 128), lambda i: (0, 0, 0)),
        ),
        scratch_shapes=[VMEM((512, 1024), BF), VMEM((512, 1), F32), VMEM((512, 1), F32)],
        compiler_params=params(),
        cost_estimate=pl.CostEstimate(
            flops=2 * 512 * 2048 * 1024, bytes_accessed=9 << 20, transcendentals=1 << 20
        ),
    )(at, own, other, scaled, bias_row)


def joined(shares):
    top = jnp.max(shares, axis=0)
    return top + jnp.log(jnp.sum(jnp.exp(shares - top[None]), axis=0))


def resp_kernel(at, shares, score, out):
    step = pl.program_id(0)
    del at
    lse = joined(shares[0, :, pl.ds(step, 1), :])
    out[...] = jnp.exp(score[...] - column(lse)).astype(BF)


def responsibilities(at, shares, score):
    return pl.pallas_call(
        resp_kernel,
        grid_spec=pltpu.PrefetchScalarGridSpec(
            num_scalar_prefetch=1,
            grid=(4,),
            in_specs=[
                pl.BlockSpec((1, 8, 4, 128), lambda i, at: (at[2], 0, 0, 0)),
                pl.BlockSpec((128, 2048), lambda i, at: (i, 0)),
            ],
            out_specs=pl.BlockSpec((128, 2048), lambda i, at: (i, 0)),
        ),
        out_shape=jax.ShapeDtypeStruct((512, 2048), BF),
        compiler_params=params(),
        cost_estimate=pl.CostEstimate(flops=1 << 21, bytes_accessed=6 << 20, transcendentals=1 << 20),
    )(at, shares, score)


def sums_kernel(at, shares, scaled, bias, *refs):
    pieces = refs[:8]
    sums, counts = refs[8:10]
    rows, weights, lse, sems = refs[10:]
    copies = [
        pltpu.make_async_copy(piece, rows.at[pl.ds(i * 256, 256)], sems.at[i])
        for i, piece in enumerate(pieces)
    ]
    for copy in copies:
        copy.start()
    y, c = at[2], at[1]
    for yy in range(4):
        lse[pl.ds(yy * 4, 4), :] = joined(shares[yy])
    count = jnp.zeros((512, 1), F32)
    for i in range(8):
        copies[i].wait()
        there = lax.rem(y + (0, 3, 1, 2)[i // 2], 4)
        core = c if i % 2 == 0 else 1 - c
        line = there * 4 + core * 2
        part = jnp.concatenate([lse[pl.ds(line, 1), :], lse[pl.ds(line + 1, 1), :]], axis=1)
        score = lax.dot_general(
            scaled[...], rows[i * 256 : (i + 1) * 256, :], (((1,), (1,)), ((), ())),
            preferred_element_type=F32,
        )
        weight = jnp.exp(score + bias[...] - part).astype(BF)
        weights[:, i * 256 : (i + 1) * 256] = weight
        count = count + jnp.sum(weight.astype(F32), axis=1, keepdims=True)
    for j in range(4):
        block = lax.dot_general(
            weights[...], rows[:, j * 256 : (j + 1) * 256], (((1,), (0,)), ((), ())),
            preferred_element_type=F32,
        )
        sums[j * 256 : (j + 1) * 256, :] = jnp.transpose(block).astype(BF)
    for b in range(4):
        part = jnp.broadcast_to(count[b * 128 : (b + 1) * 128], (128, 128))
        counts[:, b, :] = jnp.broadcast_to(jnp.transpose(part)[0:1, :], (32, 128))


def partial_sums(at, shares, scaled, bias_col, pieces):
    return pl.pallas_call(
        sums_kernel,
        grid_spec=pltpu.PrefetchScalarGridSpec(
            num_scalar_prefetch=1,
            grid=(1,),
            in_specs=[
                pl.BlockSpec((4, 8, 4, 128), lambda i, at: (0, 0, 0, 0)),
                pl.BlockSpec((512, 1024), lambda i, at: (at[2], 0)),
                pl.BlockSpec((512, 1), lambda i, at: (at[2], 0)),
            ]
            + [pl.BlockSpec(memory_space=pl.ANY)] * 8,
            out_specs=(
                pl.BlockSpec((1024, 512), lambda i, at: (0, 0)),
                pl.BlockSpec((32, 4, 128), lambda i, at: (0, 0, 0)),
            ),
            scratch_shapes=[
                VMEM((2048, 1024), BF),
                VMEM((512, 2048), BF),
                VMEM((16, 128), F32),
                pltpu.SemaphoreType.DMA((8,)),
            ],
        ),
        out_shape=(
            jax.ShapeDtypeStruct((1024, 512), BF),
            jax.ShapeDtypeStruct((32, 4, 128), F32),
        ),
        compiler_params=params(),
        cost_estimate=pl.CostEstimate(
            flops=4 * 512 * 2048 * 1024, bytes_accessed=8 << 20, transcendentals=1 << 20
        ),
    )(at, shares, scaled, bias_col, *pieces)


def body(points, means, log_weights, inv_var):
    x, c, y, z = (lax.axis_index(a) for a in "xcyz")
    at = jnp.stack([x, c, y]).astype(jnp.int32)

    far = shift(points, "y", 2)
    own = gather_x(at, points)
    other = shift(own, "c", 1)

    means_f = means.astype(F32)
    scaled = (means_f * inv_var[None, :]).astype(BF)
    half_norm = 0.5 * jnp.sum(means_f * means_f * inv_var[None, :], axis=1)
    bias = log_weights - half_norm

    score, share = scores(at, own, other, scaled, bias.reshape(1, 2048))

    before = shift(own, "y", 1)
    after = shift(own, "y", -1)
    far = gather_x(at, far)
    pieces = []
    for mine in (before, after, far):
        pieces += [mine, shift(mine, "c", 1)]

    shares = lax.all_to_all(share, ("y", "x", "c"), split_axis=0, concat_axis=0, tiled=True)
    shares = shares.reshape(4, 8, 4, 128)

    resp = responsibilities(at, shares, score)
    resp_rows = lax.all_to_all(resp, ("c", "x"), split_axis=0, concat_axis=0, tiled=True)
    resp_rows = resp_rows.reshape(2, 4, 64, 2048).transpose(2, 1, 0, 3).reshape(64, 16384)

    sums, counts = partial_sums(at, shares, scaled, bias[:, None], [own, other] + pieces)
    counts = lax.all_to_all(counts, ("y", "z"), split_axis=0, concat_axis=0, tiled=True)
    sums = lax.all_to_all(sums, ("y", "z"), split_axis=0, concat_axis=0, tiled=True)
    counts = jnp.sum(counts.reshape(4, 8, 512), axis=1).reshape(2048)
    sums = jnp.sum(sums.reshape(4, 8, 32, 512).astype(F32), axis=1)
    sums = sums.transpose(1, 0, 2).reshape(32, 2048)
    mean_cols = lax.dynamic_slice_in_dim(means, (y * 8 + z) * 32, 32, 1).T.astype(F32)
    new_means_t = (sums + mean_cols) / (counts[None, :] + 1.0)

    lse = joined(lax.dynamic_index_in_dim(shares, y, 0, keepdims=False)).reshape(8, 64)
    own_lse = lax.dynamic_index_in_dim(lse, c * 4 + x, 0, keepdims=False)
    points_f = points.astype(F32)
    const_term = 0.5 * jnp.sum(jnp.log(inv_var)) - 0.5 * 1024 * math.log(2.0 * math.pi)
    loglik = own_lse - 0.5 * jnp.sum(points_f * points_f * inv_var[None, :], axis=1) + const_term
    return (resp_rows, counts, new_means_t, loglik)


def solution(mesh):
    axes = ("y", "z", "x", "c")
    mesh = Mesh(mesh.devices.reshape(4, 8, 4, 2), axes)
    comp, pt = ("x", "c"), ("y", "z")
    return jax.shard_map(
        body,
        mesh=mesh,
        in_specs=(P(axes, None), P(comp, None), P(comp), P()),
        out_specs=(P(axes, None), P(comp), P(pt, comp), P(axes)),
        check_vma=False,
    )
```

```python
import functools
import math

import jax
import jax.numpy as jnp
from jax import lax
from jax.experimental import pallas as pl
from jax.experimental.pallas import tpu as pltpu
from jax.sharding import Mesh
from jax.sharding import PartitionSpec as P

BF = jnp.bfloat16
F32 = jnp.float32
VMEM_LIMIT = 24 * 1024 * 1024
VMEM = pltpu.VMEM
SIZES = {"y": 4, "z": 8, "x": 4, "c": 2}


def shift(value, axis, step):
    n = SIZES[axis]
    return lax.ppermute(value, axis, [(i, (i + step) % n) for i in range(n)])


def swap(value, axis, bit):
    n = SIZES[axis]
    return lax.ppermute(value, axis, [(i, i ^ bit) for i in range(n)])


def params():
    return pltpu.CompilerParams(vmem_limit_bytes=VMEM_LIMIT)


def whole():
    return pl.BlockSpec(memory_space=VMEM)


def scalar():
    return pl.BlockSpec(memory_space=pltpu.SMEM)


def anywhere(n=1):
    return [pl.BlockSpec(memory_space=pl.ANY)] * n


def hbm(n=1):
    return [pl.BlockSpec(memory_space=pltpu.HBM)] * n


def hand_on_kernel(value, *refs):
    refs[-1][...] = value[...]


def hand_on(value, *first):
    return pl.pallas_call(
        hand_on_kernel,
        out_shape=jax.ShapeDtypeStruct(value.shape, value.dtype),
        in_specs=[whole()] + anywhere(len(first)),
        out_specs=whole(),
        compiler_params=params(),
    )(value, *first)


def place_kernel(at, own, before, after, far, *refs):
    out = refs[-1]
    x = at[0]
    for step, piece in ((0, own), (3, before), (1, after), (2, far)):
        slot = lax.rem(x + step, 4)
        out[pl.ds(pl.multiple_of(slot * 64, 64), 64), :] = piece[...]


def gather_x(at, own, ahead):
    parts = (own, shift(own, "x", 1), shift(own, "x", -1), shift(own, "x", 2))
    return pl.pallas_call(
        place_kernel,
        out_shape=jax.ShapeDtypeStruct((256, 1024), BF),
        in_specs=[scalar()] + [whole()] * 4 + anywhere(len(ahead)),
        out_specs=whole(),
        compiler_params=params(),
    )(at, *parts, *ahead)


def column(row):
    return jnp.transpose(jnp.broadcast_to(row, (128, 128)))[:, 0:1]


def line(col):
    return jnp.transpose(jnp.broadcast_to(col, (128, 128)))[0:1, :]


def score_kernel(at, own, other, scaled, bias, score, share, rows, peak, total):
    step = pl.program_id(0)
    c = at[1]

    @pl.when(step == 0)
    def _():
        rows[pl.ds(pl.multiple_of(c * 256, 256), 256), :] = own[...]
        rows[pl.ds(pl.multiple_of((1 - c) * 256, 256), 256), :] = other[...]
        peak[...] = jnp.full_like(peak, -jnp.inf)
        total[...] = jnp.zeros_like(total)

    for r in range(2):
        cut = slice(r * 256, r * 256 + 256)
        tile = lax.dot_general(
            rows[cut, :], scaled[...], (((1,), (1,)), ((), ())), preferred_element_type=F32
        )
        tile = tile + bias[...]
        score[cut, :] = tile
        lanes = [tile[:, i : i + 128] for i in range(0, tile.shape[1], 128)]
        old = peak[cut, :]
        top = functools.reduce(jnp.maximum, lanes, old)
        added = functools.reduce(jnp.add, [jnp.exp(lane - top) for lane in lanes])
        total[cut, :] = total[cut, :] * jnp.exp(old - top) + added
        peak[cut, :] = top

    @pl.when(step == pl.num_programs(0) - 1)
    def _():
        for b in range(4):
            cut = slice(b * 128, b * 128 + 128)
            top = jnp.max(peak[cut, :], axis=1, keepdims=True)
            mass = jnp.sum(total[cut, :] * jnp.exp(peak[cut, :] - top), axis=1, keepdims=True)
            share[:, b, :] = jnp.broadcast_to(line(top + jnp.log(mass)), (32, 128))


def scores(at, own, other, scaled, bias_row):
    width = 512
    return pl.pallas_call(
        score_kernel,
        grid=(2048 // width,),
        out_shape=(
            pltpu.HBM((512, 2048), F32),
            jax.ShapeDtypeStruct((32, 4, 128), F32),
        ),
        in_specs=[
            scalar(),
            pl.BlockSpec((256, 1024), lambda i: (0, 0)),
            pl.BlockSpec((256, 1024), lambda i: (0, 0)),
            pl.BlockSpec((width, 1024), lambda i: (i, 0)),
            pl.BlockSpec((1, width), lambda i: (0, i)),
        ],
        out_specs=(
            pl.BlockSpec((512, width), lambda i: (0, i)),
            pl.BlockSpec((32, 4, 128), lambda i: (0, 0, 0)),
        ),
        scratch_shapes=[VMEM((512, 1024), BF), VMEM((512, 128), F32), VMEM((512, 128), F32)],
        compiler_params=params(),
        cost_estimate=pl.CostEstimate(
            flops=2 * 512 * 2048 * 1024, bytes_accessed=9 << 20, transcendentals=1 << 20
        ),
    )(at, own, other, scaled, bias_row)


def joined(shares):
    top = jnp.max(shares, axis=0)
    return top + jnp.log(jnp.sum(jnp.exp(shares - top[None]), axis=0))


def sums_kernel(at, shares, scaled, bias, *refs):
    pieces = refs[:8]
    sums, counts = refs[8:10]
    rows, weights, lse, sems = refs[10:]
    copies = [
        pltpu.make_async_copy(piece, rows.at[pl.ds(i * 256, 256)], sems.at[i])
        for i, piece in enumerate(pieces)
    ]
    for copy in copies:
        copy.start()
    y, c = at[2], at[1]
    for yy in range(4):
        lse[pl.ds(yy * 4, 4), :] = joined(shares[yy])
    count = jnp.zeros((512, 128), F32)
    for i in range(8):
        there = lax.rem(y + (0, 3, 1, 2)[i // 2], 4)
        core = c if i % 2 == 0 else 1 - c
        at_row = there * 4 + core * 2
        norm = jnp.concatenate([lse[pl.ds(at_row, 1), :], lse[pl.ds(at_row + 1, 1), :]], axis=1)
        cut = slice(i * 256, i * 256 + 256)
        copies[i].wait()
        score = lax.dot_general(
            scaled[...], rows[cut, :], (((1,), (1,)), ((), ())), preferred_element_type=F32
        )
        weight = jnp.exp(score + bias[...] - norm).astype(BF)
        weights[:, cut] = weight
        count = count + weight[:, :128].astype(F32) + weight[:, 128:].astype(F32)
    count = jnp.sum(count, axis=1, keepdims=True)
    counts[...] = jnp.zeros_like(counts)
    for b in range(4):
        counts[pl.ds(y * 4 + b, 1), :] = line(count[b * 128 : b * 128 + 128])
    for j in range(4):
        cut = slice(j * 256, j * 256 + 256)
        block = lax.dot_general(
            weights[...], rows[:, cut], (((1,), (0,)), ((), ())), preferred_element_type=F32
        )
        sums[cut, :] = jnp.transpose(block.astype(BF))


def partial_sums(at, shares, scaled, bias_col, pieces):
    return pl.pallas_call(
        sums_kernel,
        grid_spec=pltpu.PrefetchScalarGridSpec(
            num_scalar_prefetch=1,
            grid=(1,),
            in_specs=[
                pl.BlockSpec((4, 8, 4, 128), lambda i, at: (0, 0, 0, 0)),
                pl.BlockSpec((512, 1024), lambda i, at: (at[2], 0)),
                pl.BlockSpec((512, 1), lambda i, at: (at[2], 0)),
            ]
            + anywhere(8),
            out_specs=(
                pl.BlockSpec((1024, 512), lambda i, at: (0, 0)),
                pl.BlockSpec((16, 128), lambda i, at: (0, 0)),
            ),
            scratch_shapes=[
                VMEM((2048, 1024), BF),
                VMEM((512, 2048), BF),
                VMEM((16, 128), F32),
                pltpu.SemaphoreType.DMA((8,)),
            ],
        ),
        out_shape=(
            pltpu.HBM((1024, 512), BF),
            jax.ShapeDtypeStruct((16, 128), F32),
        ),
        compiler_params=params(),
        cost_estimate=pl.CostEstimate(
            flops=4 * 512 * 2048 * 1024, bytes_accessed=8 << 20, transcendentals=1 << 20
        ),
    )(at, shares, scaled, bias_col, *pieces)


def resp_kernel(at, shares, counts, score, *refs):
    outs, passed, norm, held, sems = refs[:8], refs[8], refs[9], refs[10], refs[11]
    x, c, y = at[0], at[1], at[2]
    copies = []
    for j in range(8):
        core = 1 - c if j < 4 else c
        start = pl.multiple_of(core * 256 + lax.rem(x + j % 4, 4) * 64, 64)
        copies.append(
            (start, pltpu.make_async_copy(score.at[pl.ds(start, 64)], held.at[j], sems.at[j]))
        )
    for _, copy in copies:
        copy.start()
    passed[...] = counts[...]
    lse = joined(shares[y])
    for b in range(4):
        norm[b * 128 : b * 128 + 128, :] = jnp.transpose(
            jnp.broadcast_to(lse[b : b + 1, :], (128, 128))
        )
    for j, (start, copy) in enumerate(copies):
        copy.wait()
        outs[j][...] = jnp.exp(held[j] - norm[pl.ds(start, 64), 0:1]).astype(BF)


def responsibilities(at, shares, counts, score):
    return pl.pallas_call(
        resp_kernel,
        in_specs=[scalar(), whole(), whole()] + hbm(),
        out_specs=[whole()] * 9,
        scratch_shapes=[
            VMEM((512, 128), F32),
            VMEM((8, 64, 2048), F32),
            pltpu.SemaphoreType.DMA((8,)),
        ],
        out_shape=[jax.ShapeDtypeStruct((64, 2048), BF)] * 8
        + [jax.ShapeDtypeStruct((16, 128), F32)],
        compiler_params=params(),
        cost_estimate=pl.CostEstimate(flops=1 << 21, bytes_accessed=6 << 20, transcendentals=1 << 20),
    )(at, shares, counts, pltpu.with_memory_space_constraint(score, pltpu.HBM))


def lay_kernel(at, *refs):
    pieces, out, sems = refs[:8], refs[8], refs[9]
    x, c = at[0], at[1]
    copies = []
    for j in range(8):
        core = 1 - c if j < 4 else c
        comp = lax.rem(x + 4 - j % 4, 4) * 2 + core
        spot = out.at[:, pl.ds(pl.multiple_of(comp * 2048, 2048), 2048)]
        copies.append(pltpu.make_async_copy(pieces[j], spot, sems.at[j]))
    for copy in copies:
        copy.start()
    for copy in copies:
        copy.wait()


def lay_out(at, pieces):
    return pl.pallas_call(
        lay_kernel,
        in_specs=[scalar()] + anywhere(8),
        out_specs=pl.BlockSpec(memory_space=pl.ANY),
        scratch_shapes=[pltpu.SemaphoreType.DMA((8,))],
        out_shape=jax.ShapeDtypeStruct((64, 16384), BF),
        compiler_params=params(),
    )(at, *pieces)


def body(points, means, log_weights, inv_var):
    x, c, y, z = (lax.axis_index(a) for a in "xcyz")
    at = jnp.stack([x, c, y]).astype(jnp.int32)

    far = shift(points, "y", 2)
    means_f = means.astype(F32)
    scaled = (means_f * inv_var[None, :]).astype(BF)
    scaled = pltpu.with_memory_space_constraint(scaled, pltpu.HBM)
    half_norm = 0.5 * jnp.sum(means_f * means_f * inv_var[None, :], axis=1)
    bias = log_weights - half_norm
    bias_row, bias_col = bias.reshape(1, 2048), bias[:, None]

    own = gather_x(at, points, (bias_row, bias_col, far))
    other = shift(own, "c", 1)
    before = shift(own, "y", 1)
    after = shift(own, "y", -1)
    score, share = scores(at, own, other, scaled, bias_row)

    shares = lax.all_to_all(share, ("y", "x", "c"), split_axis=0, concat_axis=0, tiled=True)
    far = gather_x(at, far, (shares,))
    shares = shares.reshape(4, 8, 4, 128)
    pieces = [own, other]
    for mine in (before, after, far):
        pieces += [mine, shift(mine, "c", 1)]

    sums, counts = partial_sums(at, shares, scaled, bias_col, pieces)
    sums = lax.all_to_all(sums, ("y", "z"), split_axis=0, concat_axis=0, tiled=True)

    *blocks, counts = responsibilities(at, shares, counts, score)
    theirs = [swap(b, "c", 1) for b in blocks[:4]]
    held = theirs + list(blocks[4:])
    held = [shift(b, "x", j % 4) if j % 4 else b for j, b in enumerate(held)]
    resp_rows = lay_out(at, held)

    counts = hand_on(counts, *theirs, held[5])
    counts = sum([shift(counts, "z", i) for i in range(1, 8)], counts)
    counts = hand_on(counts, held[1], held[3], held[6], held[7])
    counts = sum([shift(counts, "y", i) for i in range(1, 4)], counts)
    counts = counts.reshape(2048)

    sums = jnp.sum(sums.reshape(4, 8, 32, 512).astype(F32), axis=1)
    sums = sums.transpose(1, 0, 2).reshape(32, 2048)
    mean_cols = lax.dynamic_slice_in_dim(means, (y * 8 + z) * 32, 32, 1).T.astype(F32)
    new_means_t = (sums + mean_cols) / (counts[None, :] + 1.0)

    lse = joined(lax.dynamic_index_in_dim(shares, y, 0, keepdims=False)).reshape(8, 64)
    own_lse = lax.dynamic_index_in_dim(lse, c * 4 + x, 0, keepdims=False)
    points_f = points.astype(F32)
    const_term = 0.5 * jnp.sum(jnp.log(inv_var)) - 0.5 * 1024 * math.log(2.0 * math.pi)
    loglik = own_lse - 0.5 * jnp.sum(points_f * points_f * inv_var[None, :], axis=1) + const_term
    return (resp_rows, counts, new_means_t, loglik)


def solution(mesh):
    axes = ("y", "z", "x", "c")
    mesh = Mesh(mesh.devices.reshape(4, 8, 4, 2), axes)
    comp, pt = ("x", "c"), ("y", "z")
    return jax.shard_map(
        body,
        mesh=mesh,
        in_specs=(P(axes, None), P(comp, None), P(comp), P()),
        out_specs=(P(axes, None), P(comp), P(pt, comp), P(axes)),
        check_vma=False,
    )
```

```python
import functools
import math

import jax
import jax.numpy as jnp
from jax import lax
from jax.experimental import pallas as pl
from jax.experimental.pallas import tpu as pltpu
from jax.sharding import Mesh
from jax.sharding import PartitionSpec as P

BF = jnp.bfloat16
F32 = jnp.float32
VMEM_LIMIT = 24 * 1024 * 1024
VMEM = pltpu.VMEM
SIZES = {"y": 4, "z": 8, "x": 4, "c": 2}


def shift(value, axis, step):
    n = SIZES[axis]
    return lax.ppermute(value, axis, [(i, (i + step) % n) for i in range(n)])


def swap(value, axis, bit):
    n = SIZES[axis]
    return lax.ppermute(value, axis, [(i, i ^ bit) for i in range(n)])


def params():
    return pltpu.CompilerParams(vmem_limit_bytes=VMEM_LIMIT)


def whole():
    return pl.BlockSpec(memory_space=VMEM)


def scalar():
    return pl.BlockSpec(memory_space=pltpu.SMEM)


def anywhere(n=1):
    return [pl.BlockSpec(memory_space=pl.ANY)] * n


def hbm(n=1):
    return [pl.BlockSpec(memory_space=pltpu.HBM)] * n


def place_kernel(at, own, before, after, far, *refs):
    out = refs[-1]
    x = at[0]
    for step, piece in ((0, own), (3, before), (1, after), (2, far)):
        slot = lax.rem(x + step, 4)
        out[pl.ds(pl.multiple_of(slot * 64, 64), 64), :] = piece[...]


def gather_x(at, own, ahead):
    parts = (own, shift(own, "x", 1), shift(own, "x", -1), shift(own, "x", 2))
    return pl.pallas_call(
        place_kernel,
        out_shape=jax.ShapeDtypeStruct((256, 1024), BF),
        in_specs=[scalar()] + [whole()] * 4 + anywhere(len(ahead)),
        out_specs=whole(),
        compiler_params=params(),
    )(at, *parts, *ahead)


def column(row):
    return jnp.transpose(jnp.broadcast_to(row, (128, 128)))[:, 0:1]


def line(col):
    return jnp.transpose(jnp.broadcast_to(col, (128, 128)))[0:1, :]


def score_kernel(at, own, other, scaled, bias, score, share, rows, peak, total):
    step = pl.program_id(0)
    c = at[1]

    @pl.when(step == 0)
    def _():
        rows[pl.ds(pl.multiple_of(c * 256, 256), 256), :] = own[...]
        rows[pl.ds(pl.multiple_of((1 - c) * 256, 256), 256), :] = other[...]
        peak[...] = jnp.full_like(peak, -jnp.inf)
        total[...] = jnp.zeros_like(total)

    for r in range(2):
        cut = slice(r * 256, r * 256 + 256)
        tile = lax.dot_general(
            rows[cut, :], scaled[...], (((1,), (1,)), ((), ())), preferred_element_type=F32
        )
        tile = tile + bias[...]
        score[cut, :] = tile
        lanes = [tile[:, i : i + 128] for i in range(0, tile.shape[1], 128)]
        old = peak[cut, :]
        top = functools.reduce(jnp.maximum, lanes, old)
        added = functools.reduce(jnp.add, [jnp.exp(lane - top) for lane in lanes])
        total[cut, :] = total[cut, :] * jnp.exp(old - top) + added
        peak[cut, :] = top

    @pl.when(step == pl.num_programs(0) - 1)
    def _():
        for b in range(4):
            cut = slice(b * 128, b * 128 + 128)
            top = jnp.max(peak[cut, :], axis=1, keepdims=True)
            mass = jnp.sum(total[cut, :] * jnp.exp(peak[cut, :] - top), axis=1, keepdims=True)
            share[:, b, :] = jnp.broadcast_to(line(top + jnp.log(mass)), (32, 128))


def scores(at, own, other, scaled, bias_row):
    width = 512
    return pl.pallas_call(
        score_kernel,
        grid=(2048 // width,),
        out_shape=(
            pltpu.HBM((512, 2048), F32),
            jax.ShapeDtypeStruct((32, 4, 128), F32),
        ),
        in_specs=[
            scalar(),
            pl.BlockSpec((256, 1024), lambda i: (0, 0)),
            pl.BlockSpec((256, 1024), lambda i: (0, 0)),
            pl.BlockSpec((width, 1024), lambda i: (i, 0)),
            pl.BlockSpec((1, width), lambda i: (0, i)),
        ],
        out_specs=(
            pl.BlockSpec((512, width), lambda i: (0, i)),
            pl.BlockSpec((32, 4, 128), lambda i: (0, 0, 0)),
        ),
        scratch_shapes=[VMEM((512, 1024), BF), VMEM((512, 128), F32), VMEM((512, 128), F32)],
        compiler_params=params(),
        cost_estimate=pl.CostEstimate(
            flops=2 * 512 * 2048 * 1024, bytes_accessed=9 << 20, transcendentals=1 << 20
        ),
    )(at, own, other, scaled, bias_row)


def joined(shares):
    top = jnp.max(shares, axis=0)
    return top + jnp.log(jnp.sum(jnp.exp(shares - top[None]), axis=0))


def sums_kernel(at, shares, scaled, bias, *refs):
    pieces = refs[:8]
    sums = refs[8]
    rows, weights, lse, sems = refs[9:]
    copies = [
        pltpu.make_async_copy(piece, rows.at[pl.ds(i * 256, 256)], sems.at[i])
        for i, piece in enumerate(pieces)
    ]
    for copy in copies:
        copy.start()
    y, c = at[2], at[1]
    for yy in range(4):
        lse[pl.ds(yy * 4, 4), :] = joined(shares[yy])
    count = jnp.zeros((512, 128), F32)
    for i in range(8):
        there = lax.rem(y + (0, 3, 1, 2)[i // 2], 4)
        core = c if i % 2 == 0 else 1 - c
        at_row = there * 4 + core * 2
        norm = jnp.concatenate([lse[pl.ds(at_row, 1), :], lse[pl.ds(at_row + 1, 1), :]], axis=1)
        cut = slice(i * 256, i * 256 + 256)
        copies[i].wait()
        score = lax.dot_general(
            scaled[...], rows[cut, :], (((1,), (1,)), ((), ())), preferred_element_type=F32
        )
        weight = jnp.exp(score + bias[...] - norm).astype(BF)
        weights[:, cut] = weight
        count = count + weight[:, :128].astype(F32) + weight[:, 128:].astype(F32)
    count = jnp.sum(count, axis=1, keepdims=True)
    count = jnp.concatenate([line(count[b : b + 128]) for b in range(0, 512, 128)], axis=1)
    high = count.astype(BF).astype(F32)
    tail = jnp.concatenate([high, count - high, jnp.zeros((6, 512), F32)], axis=0).astype(BF)
    sums[:, 32:40, :] = jnp.broadcast_to(tail[None], (32, 8, 512))
    for j in range(4):
        block = lax.dot_general(
            weights[...],
            rows[:, j * 256 : j * 256 + 256],
            (((1,), (0,)), ((), ())),
            preferred_element_type=F32,
        )
        sums[j * 8 : j * 8 + 8, 0:32, :] = jnp.transpose(block.astype(BF)).reshape(8, 32, 512)


def partial_sums(at, shares, scaled, bias_col, pieces):
    return pl.pallas_call(
        sums_kernel,
        grid_spec=pltpu.PrefetchScalarGridSpec(
            num_scalar_prefetch=1,
            grid=(1,),
            in_specs=[
                pl.BlockSpec((4, 8, 4, 128), lambda i, at: (0, 0, 0, 0)),
                pl.BlockSpec((512, 1024), lambda i, at: (at[2], 0)),
                pl.BlockSpec((512, 1), lambda i, at: (at[2], 0)),
            ]
            + anywhere(8),
            out_specs=pl.BlockSpec((32, 40, 512), lambda i, at: (0, 0, 0)),
            scratch_shapes=[
                VMEM((2048, 1024), BF),
                VMEM((512, 2048), BF),
                VMEM((16, 128), F32),
                pltpu.SemaphoreType.DMA((8,)),
            ],
        ),
        out_shape=pltpu.HBM((32, 40, 512), BF),
        compiler_params=params(),
        cost_estimate=pl.CostEstimate(
            flops=4 * 512 * 2048 * 1024, bytes_accessed=8 << 20, transcendentals=1 << 20
        ),
    )(at, shares, scaled, bias_col, *pieces)


def resp_kernel(at, shares, score, first, *refs):
    del first
    outs, norm, held, sems = refs[:8], refs[8], refs[9], refs[10]
    x, c, y = at[0], at[1], at[2]
    copies = []
    for j in range(8):
        core = 1 - c if j < 4 else c
        start = pl.multiple_of(core * 256 + lax.rem(x + j % 4, 4) * 64, 64)
        copies.append(
            (start, pltpu.make_async_copy(score.at[pl.ds(start, 64)], held.at[j], sems.at[j]))
        )
    for _, copy in copies:
        copy.start()
    lse = joined(shares[y])
    for b in range(4):
        norm[b * 128 : b * 128 + 128, :] = jnp.transpose(
            jnp.broadcast_to(lse[b : b + 1, :], (128, 128))
        )
    for j, (start, copy) in enumerate(copies):
        copy.wait()
        outs[j][...] = jnp.exp(held[j] - norm[pl.ds(start, 64), 0:1]).astype(BF)


def responsibilities(at, shares, score, first):
    return pl.pallas_call(
        resp_kernel,
        in_specs=[scalar(), whole()] + hbm(2),
        out_specs=[whole()] * 8,
        scratch_shapes=[
            VMEM((512, 128), F32),
            VMEM((8, 64, 2048), F32),
            pltpu.SemaphoreType.DMA((8,)),
        ],
        out_shape=[jax.ShapeDtypeStruct((64, 2048), BF)] * 8,
        compiler_params=params(),
        cost_estimate=pl.CostEstimate(flops=1 << 21, bytes_accessed=6 << 20, transcendentals=1 << 20),
    )(at, shares, pltpu.with_memory_space_constraint(score, pltpu.HBM), first)


def lay_kernel(at, *refs):
    pieces, out, sems = refs[:8], refs[8], refs[9]
    x, c = at[0], at[1]
    copies = []
    for j in range(8):
        core = 1 - c if j < 4 else c
        comp = lax.rem(x + 4 - j % 4, 4) * 2 + core
        spot = out.at[:, pl.ds(pl.multiple_of(comp * 2048, 2048), 2048)]
        copies.append(pltpu.make_async_copy(pieces[j], spot, sems.at[j]))
    for copy in copies:
        copy.start()
    for copy in copies:
        copy.wait()


def lay_out(at, pieces):
    return pl.pallas_call(
        lay_kernel,
        in_specs=[scalar()] + anywhere(8),
        out_specs=pl.BlockSpec(memory_space=pl.ANY),
        scratch_shapes=[pltpu.SemaphoreType.DMA((8,))],
        out_shape=jax.ShapeDtypeStruct((64, 16384), BF),
        compiler_params=params(),
    )(at, *pieces)


def body(points, means, log_weights, inv_var):
    x, c, y, z = (lax.axis_index(a) for a in "xcyz")
    at = jnp.stack([x, c, y]).astype(jnp.int32)

    far = shift(points, "y", 2)
    means_f = means.astype(F32)
    scaled = (means_f * inv_var[None, :]).astype(BF)
    scaled = pltpu.with_memory_space_constraint(scaled, pltpu.HBM)
    half_norm = 0.5 * jnp.sum(means_f * means_f * inv_var[None, :], axis=1)
    bias = log_weights - half_norm
    bias_row, bias_col = bias.reshape(1, 2048), bias[:, None]

    own = gather_x(at, points, (bias_row, bias_col, far))
    other = shift(own, "c", 1)
    before = shift(own, "y", 1)
    after = shift(own, "y", -1)
    score, share = scores(at, own, other, scaled, bias_row)

    shares = lax.all_to_all(share, ("y", "x", "c"), split_axis=0, concat_axis=0, tiled=True)
    far = gather_x(at, far, (shares,))
    shares = shares.reshape(4, 8, 4, 128)
    pieces = [own, other]
    for mine in (before, after, far):
        pieces += [mine, shift(mine, "c", 1)]

    sums = partial_sums(at, shares, scaled, bias_col, pieces)
    sent = lax.all_to_all(sums, ("y", "z"), split_axis=0, concat_axis=0, tiled=True)

    blocks = responsibilities(at, shares, score, sums)
    theirs = [swap(b, "c", 1) for b in blocks[:4]]
    held = theirs + list(blocks[4:])
    held = [shift(b, "x", j % 4) if j % 4 else b for j, b in enumerate(held)]
    resp_rows = lay_out(at, held)

    sums = jnp.sum(sent.reshape(4, 8, 40, 512).astype(F32), axis=1)
    counts = (sums[:, 32, :] + sums[:, 33, :]).reshape(2048)
    sums = sums[:, :32, :].transpose(1, 0, 2).reshape(32, 2048)
    mean_cols = lax.dynamic_slice_in_dim(means, (y * 8 + z) * 32, 32, 1).T.astype(F32)
    new_means_t = (sums + mean_cols) / (counts[None, :] + 1.0)

    lse = joined(lax.dynamic_index_in_dim(shares, y, 0, keepdims=False)).reshape(8, 64)
    own_lse = lax.dynamic_index_in_dim(lse, c * 4 + x, 0, keepdims=False)
    points_f = points.astype(F32)
    const_term = 0.5 * jnp.sum(jnp.log(inv_var)) - 0.5 * 1024 * math.log(2.0 * math.pi)
    loglik = own_lse - 0.5 * jnp.sum(points_f * points_f * inv_var[None, :], axis=1) + const_term
    return (resp_rows, counts, new_means_t, loglik)


def solution(mesh):
    axes = ("y", "z", "x", "c")
    mesh = Mesh(mesh.devices.reshape(4, 8, 4, 2), axes)
    comp, pt = ("x", "c"), ("y", "z")
    return jax.shard_map(
        body,
        mesh=mesh,
        in_specs=(P(axes, None), P(comp, None), P(comp), P()),
        out_specs=(P(axes, None), P(comp), P(pt, comp), P(axes)),
        check_vma=False,
    )
```

```python
import functools
import math

import jax
import jax.numpy as jnp
from jax import lax
from jax.experimental import pallas as pl
from jax.experimental.pallas import tpu as pltpu
from jax.sharding import Mesh
from jax.sharding import PartitionSpec as P

BF = jnp.bfloat16
F32 = jnp.float32
VMEM_LIMIT = 24 * 1024 * 1024
VMEM = pltpu.VMEM
SIZES = {"y": 4, "z": 8, "x": 4, "c": 2}


def shift(value, axis, step):
    n = SIZES[axis]
    return lax.ppermute(value, axis, [(i, (i + step) % n) for i in range(n)])


def still(value):
    return pltpu.with_memory_space_constraint(value, pltpu.HBM)


def params():
    return pltpu.CompilerParams(vmem_limit_bytes=VMEM_LIMIT)


def whole():
    return pl.BlockSpec(memory_space=VMEM)


def scalar():
    return pl.BlockSpec(memory_space=pltpu.SMEM)


def anywhere(n=1):
    return [pl.BlockSpec(memory_space=pl.ANY)] * n


def hbm(n=1):
    return [pl.BlockSpec(memory_space=pltpu.HBM)] * n


def prepare_kernel(means, inv_var, weights, scaled, row, col):
    values = means[...].astype(F32)
    product = values * inv_var[...]
    scaled[...] = product.astype(BF)
    square = values * product
    norm = functools.reduce(jnp.add, [square[:, i : i + 128] for i in range(0, 1024, 128)])
    norm = 0.5 * jnp.sum(norm, axis=1, keepdims=True)
    for i in range(0, 256, 128):
        part = weights[:, i : i + 128] - line(norm[i : i + 128])
        row[:, i : i + 128] = part
        col[i : i + 128, :] = column(part)


def prepare(means, inv_var, log_weights):
    return pl.pallas_call(
        prepare_kernel,
        grid=(8,),
        in_specs=[
            pl.BlockSpec((256, 1024), lambda i: (i, 0)),
            pl.BlockSpec((1, 1024), lambda i: (0, 0)),
            pl.BlockSpec((1, 256), lambda i: (0, i)),
        ],
        out_specs=(
            pl.BlockSpec((256, 1024), lambda i: (i, 0)),
            pl.BlockSpec((1, 256), lambda i: (0, i)),
            pl.BlockSpec((256, 1), lambda i: (i, 0)),
        ),
        out_shape=(
            pltpu.HBM((2048, 1024), BF),
            jax.ShapeDtypeStruct((1, 2048), F32),
            jax.ShapeDtypeStruct((2048, 1), F32),
        ),
        compiler_params=params(),
        cost_estimate=pl.CostEstimate(flops=6 << 21, bytes_accessed=8 << 20, transcendentals=0),
    )(still(means), inv_var.reshape(1, 1024), log_weights.reshape(1, 2048))


def place_kernel(at, own, before, after, far, *refs):
    out = refs[-1]
    x = at[0]
    for step, piece in ((0, own), (3, before), (1, after), (2, far)):
        slot = lax.rem(x + step, 4)
        out[pl.ds(pl.multiple_of(slot * 64, 64), 64), :] = piece[...]


def gather_x(at, own, ahead, there=()):
    parts = (own, shift(own, "x", 1), shift(own, "x", -1), shift(own, "x", 2))
    return pl.pallas_call(
        place_kernel,
        out_shape=jax.ShapeDtypeStruct((256, 1024), BF),
        in_specs=[scalar()] + [whole()] * 4 + hbm(len(ahead)) + anywhere(len(there)),
        out_specs=whole(),
        compiler_params=params(),
    )(at, *parts, *(still(a) for a in ahead), *there)


def column(row):
    return jnp.transpose(jnp.broadcast_to(row, (128, 128)))[:, 0:1]


def line(col):
    return jnp.transpose(jnp.broadcast_to(col, (128, 128)))[0:1, :]


def score_kernel(at, own, other, scaled, bias, score, share, rows, peak, total):
    step = pl.program_id(0)
    c = at[1]

    @pl.when(step == 0)
    def _():
        rows[pl.ds(pl.multiple_of(c * 256, 256), 256), :] = own[...]
        rows[pl.ds(pl.multiple_of((1 - c) * 256, 256), 256), :] = other[...]
        peak[...] = jnp.full_like(peak, -jnp.inf)
        total[...] = jnp.zeros_like(total)

    for r in range(2):
        cut = slice(r * 256, r * 256 + 256)
        tile = lax.dot_general(
            rows[cut, :], scaled[...], (((1,), (1,)), ((), ())), preferred_element_type=F32
        )
        tile = tile + bias[...]
        score[cut, :] = tile
        lanes = [tile[:, i : i + 128] for i in range(0, tile.shape[1], 128)]
        old = peak[cut, :]
        top = functools.reduce(jnp.maximum, lanes, old)
        added = functools.reduce(jnp.add, [jnp.exp(lane - top) for lane in lanes])
        total[cut, :] = total[cut, :] * jnp.exp(old - top) + added
        peak[cut, :] = top

    @pl.when(step == pl.num_programs(0) - 1)
    def _():
        for b in range(4):
            cut = slice(b * 128, b * 128 + 128)
            top = jnp.max(peak[cut, :], axis=1, keepdims=True)
            mass = jnp.sum(total[cut, :] * jnp.exp(peak[cut, :] - top), axis=1, keepdims=True)
            share[:, b, :] = jnp.broadcast_to(line(top + jnp.log(mass)), (32, 128))


def scores(at, own, other, scaled, bias_row):
    width = 512
    return pl.pallas_call(
        score_kernel,
        grid=(2048 // width,),
        out_shape=(
            pltpu.HBM((512, 2048), F32),
            jax.ShapeDtypeStruct((32, 4, 128), F32),
        ),
        in_specs=[
            scalar(),
            pl.BlockSpec((256, 1024), lambda i: (0, 0)),
            pl.BlockSpec((256, 1024), lambda i: (0, 0)),
            pl.BlockSpec((width, 1024), lambda i: (i, 0)),
            pl.BlockSpec((1, width), lambda i: (0, i)),
        ],
        out_specs=(
            pl.BlockSpec((512, width), lambda i: (0, i)),
            pl.BlockSpec((32, 4, 128), lambda i: (0, 0, 0)),
        ),
        scratch_shapes=[VMEM((512, 1024), BF), VMEM((512, 128), F32), VMEM((512, 128), F32)],
        compiler_params=params(),
        cost_estimate=pl.CostEstimate(
            flops=2 * 512 * 2048 * 1024, bytes_accessed=9 << 20, transcendentals=1 << 20
        ),
    )(at, own, other, still(scaled), bias_row)


def joined(shares):
    top = jnp.max(shares, axis=0)
    return top + jnp.log(jnp.sum(jnp.exp(shares - top[None]), axis=0))


def sums_kernel(at, shares, scaled, bias, *refs):
    pieces = refs[:8]
    sums = refs[8]
    rows, weights, lse, sems = refs[9:]
    copies = [
        pltpu.make_async_copy(piece, rows.at[pl.ds(i * 256, 256)], sems.at[i])
        for i, piece in enumerate(pieces)
    ]
    for copy in copies:
        copy.start()
    y, c = at[2], at[1]
    for yy in range(4):
        lse[pl.ds(yy * 4, 4), :] = joined(shares[yy])
    count = jnp.zeros((512, 128), F32)
    for i in range(8):
        there = lax.rem(y + (0, 3, 1, 2)[i // 2], 4)
        core = c if i % 2 == 0 else 1 - c
        at_row = there * 4 + core * 2
        norm = jnp.concatenate([lse[pl.ds(at_row, 1), :], lse[pl.ds(at_row + 1, 1), :]], axis=1)
        cut = slice(i * 256, i * 256 + 256)
        copies[i].wait()
        score = lax.dot_general(
            scaled[...], rows[cut, :], (((1,), (1,)), ((), ())), preferred_element_type=F32
        )
        weight = jnp.exp(score + bias[...] - norm).astype(BF)
        weights[:, cut] = weight
        count = count + weight[:, :128].astype(F32) + weight[:, 128:].astype(F32)
    count = jnp.sum(count, axis=1, keepdims=True)
    count = jnp.concatenate([line(count[b : b + 128]) for b in range(0, 512, 128)], axis=1)
    high = count.astype(BF).astype(F32)
    tail = jnp.concatenate([high, count - high, jnp.zeros((6, 512), F32)], axis=0).astype(BF)
    sums[:, 32:40, :] = jnp.broadcast_to(tail[None], (32, 8, 512))
    for j in range(4):
        block = lax.dot_general(
            weights[...],
            rows[:, j * 256 : j * 256 + 256],
            (((1,), (0,)), ((), ())),
            preferred_element_type=F32,
        )
        sums[j * 8 : j * 8 + 8, 0:32, :] = jnp.transpose(block.astype(BF)).reshape(8, 32, 512)


def partial_sums(at, shares, scaled, bias_col, pieces):
    return pl.pallas_call(
        sums_kernel,
        grid_spec=pltpu.PrefetchScalarGridSpec(
            num_scalar_prefetch=1,
            grid=(1,),
            in_specs=[
                pl.BlockSpec((4, 8, 4, 128), lambda i, at: (0, 0, 0, 0)),
                pl.BlockSpec((512, 1024), lambda i, at: (at[2], 0)),
                pl.BlockSpec((512, 1), lambda i, at: (at[2], 0)),
            ]
            + anywhere(8),
            out_specs=pl.BlockSpec((32, 40, 512), lambda i, at: (0, 0, 0)),
            scratch_shapes=[
                VMEM((2048, 1024), BF),
                VMEM((512, 2048), BF),
                VMEM((16, 128), F32),
                pltpu.SemaphoreType.DMA((8,)),
            ],
        ),
        out_shape=pltpu.HBM((32, 40, 512), BF),
        compiler_params=params(),
        cost_estimate=pl.CostEstimate(
            flops=4 * 512 * 2048 * 1024, bytes_accessed=8 << 20, transcendentals=1 << 20
        ),
    )(at, shares, still(scaled), bias_col, *pieces)


def resp_kernel(at, shares, score, sums, *refs):
    del sums
    outs, norm, held, sems = refs[:5], refs[6], refs[7], refs[8]
    x, c, y = at[0], at[1], at[2]
    copies = []
    for j in range(8):
        core = 1 - c if j < 4 else c
        start = pl.multiple_of(core * 256 + lax.rem(x + j % 4, 4) * 64, 64)
        copies.append(
            (start, pltpu.make_async_copy(score.at[pl.ds(start, 64)], held.at[j], sems.at[j]))
        )
    for _, copy in copies:
        copy.start()
    lse = joined(shares[y])
    for b in range(4):
        norm[b * 128 : b * 128 + 128, :] = jnp.transpose(
            jnp.broadcast_to(lse[b : b + 1, :], (128, 128))
        )
    for j, (start, copy) in enumerate(copies):
        copy.wait()
        block = jnp.exp(held[j] - norm[pl.ds(start, 64), 0:1]).astype(BF)
        if j % 4 == 0:
            outs[j // 4][...] = block
        else:
            outs[1 + j % 4][j // 4 * 64 : j // 4 * 64 + 64, :] = block


def responsibilities(at, shares, score, sums):
    return pl.pallas_call(
        resp_kernel,
        in_specs=[scalar(), whole()] + hbm(2),
        out_specs=[whole()] * 5 + hbm(),
        input_output_aliases={3: 5},
        scratch_shapes=[
            VMEM((512, 128), F32),
            VMEM((8, 64, 2048), F32),
            pltpu.SemaphoreType.DMA((8,)),
        ],
        out_shape=[jax.ShapeDtypeStruct((64, 2048), BF)] * 2
        + [jax.ShapeDtypeStruct((128, 2048), BF)] * 3
        + [pltpu.HBM((32, 40, 512), BF)],
        compiler_params=params(),
        cost_estimate=pl.CostEstimate(flops=1 << 21, bytes_accessed=6 << 20, transcendentals=1 << 20),
    )(at, shares, still(score), sums)


def cut_kernel(at, means, ahead, out, turned):
    del ahead
    for i in range(0, 2048, 128):
        turned[:, i : i + 128] = jnp.transpose(means[i : i + 128, :].astype(F32))
    out[...] = turned[pl.ds(pl.multiple_of(lax.rem(at[3], 4) * 32, 32), 32), :]


def mean_columns(at, means, ahead):
    return pl.pallas_call(
        cut_kernel,
        grid_spec=pltpu.PrefetchScalarGridSpec(
            num_scalar_prefetch=1,
            grid=(1,),
            in_specs=[pl.BlockSpec((2048, 128), lambda i, at: (0, at[3] // 4))] + anywhere(),
            out_specs=pl.BlockSpec((32, 2048), lambda i, at: (0, 0)),
            scratch_shapes=[VMEM((128, 2048), F32)],
        ),
        out_shape=pltpu.HBM((32, 2048), F32),
        compiler_params=params(),
    )(at, still(means), ahead)


def lay_kernel(at, *refs):
    pieces, out, sems = refs[:8], refs[8], refs[9]
    x, c = at[0], at[1]
    copies = []
    for j in range(8):
        core = 1 - c if j < 4 else c
        comp = lax.rem(x + 4 - j % 4, 4) * 2 + core
        spot = out.at[:, pl.ds(pl.multiple_of(comp * 2048, 2048), 2048)]
        piece = pieces[j].at[pl.ds(64, 64)] if j > 4 else pieces[j]
        copies.append(pltpu.make_async_copy(piece, spot, sems.at[j]))
    for copy in copies:
        copy.start()
    for copy in copies:
        copy.wait()


def lay_out(at, pieces):
    return pl.pallas_call(
        lay_kernel,
        in_specs=[scalar()] + anywhere(8),
        out_specs=pl.BlockSpec(memory_space=pl.ANY),
        scratch_shapes=[pltpu.SemaphoreType.DMA((8,))],
        out_shape=jax.ShapeDtypeStruct((64, 16384), BF),
        compiler_params=params(),
    )(at, *pieces)


def body(points, means, log_weights, inv_var):
    x, c, y, z = (lax.axis_index(a) for a in "xcyz")
    at = jnp.stack([x, c, y, y * 8 + z]).astype(jnp.int32)

    far = shift(points, "y", 2)
    scaled, bias_row, bias_col = prepare(means, inv_var, log_weights)

    own = gather_x(at, points, (scaled,), (far,))
    other = shift(own, "c", 1)
    before = shift(own, "y", 1)
    after = shift(own, "y", -1)
    score, share = scores(at, own, other, scaled, bias_row)

    shares = lax.all_to_all(share, ("y", "x", "c"), split_axis=0, concat_axis=0, tiled=True)
    mean_cols = mean_columns(at, means, share)
    far = gather_x(at, far, (mean_cols,), (shares,))
    shares = shares.reshape(4, 8, 4, 128)
    pieces = [own, other]
    for mine in (before, after, far):
        pieces += [mine, shift(mine, "c", 1)]

    sums = partial_sums(at, shares, scaled, bias_col, pieces)
    *blocks, sums = responsibilities(at, shares, score, sums)
    pairs = [shift(b, "x", j + 1) for j, b in enumerate(blocks[2:])]
    theirs = [shift(b, "c", 1) for b in [blocks[0]] + [pair[:64] for pair in pairs]]
    held = theirs + [blocks[1]] + pairs
    sent = lax.all_to_all(sums, ("y", "z"), split_axis=0, concat_axis=0, tiled=True)
    resp_rows = lay_out(at, held)

    sums = jnp.sum(sent.reshape(4, 8, 40, 512).astype(F32), axis=1)
    counts = (sums[:, 32, :] + sums[:, 33, :]).reshape(2048)
    sums = sums[:, :32, :].transpose(1, 0, 2).reshape(32, 2048)
    new_means_t = (sums + mean_cols) / (counts[None, :] + 1.0)

    lse = joined(lax.dynamic_index_in_dim(shares, y, 0, keepdims=False)).reshape(8, 64)
    own_lse = lax.dynamic_index_in_dim(lse, c * 4 + x, 0, keepdims=False)
    points_f = points.astype(F32)
    const_term = 0.5 * jnp.sum(jnp.log(inv_var)) - 0.5 * 1024 * math.log(2.0 * math.pi)
    loglik = own_lse - 0.5 * jnp.sum(points_f * points_f * inv_var[None, :], axis=1) + const_term
    return (resp_rows, counts, new_means_t, loglik)


def solution(mesh):
    axes = ("y", "z", "x", "c")
    mesh = Mesh(mesh.devices.reshape(4, 8, 4, 2), axes)
    comp, pt = ("x", "c"), ("y", "z")
    return jax.shard_map(
        body,
        mesh=mesh,
        in_specs=(P(axes, None), P(comp, None), P(comp), P()),
        out_specs=(P(axes, None), P(comp), P(pt, comp), P(axes)),
        check_vma=False,
    )
```

```python
import functools
import math

import jax
import jax.numpy as jnp
from jax import lax
from jax.experimental import pallas as pl
from jax.experimental.pallas import tpu as pltpu
from jax.sharding import Mesh
from jax.sharding import PartitionSpec as P

BF = jnp.bfloat16
F32 = jnp.float32
VMEM_LIMIT = 24 * 1024 * 1024
VMEM = pltpu.VMEM
SIZES = {"y": 4, "x": 4, "c": 2}


def shift(value, axis, step):
    n = SIZES[axis]
    return lax.ppermute(value, axis, [(i, (i + step) % n) for i in range(n)])


def still(value):
    return pltpu.with_memory_space_constraint(value, pltpu.HBM)


def params():
    return pltpu.CompilerParams(vmem_limit_bytes=VMEM_LIMIT)


def whole():
    return pl.BlockSpec(memory_space=VMEM)


def scalar():
    return pl.BlockSpec(memory_space=pltpu.SMEM)


def anywhere(n=1):
    return [pl.BlockSpec(memory_space=pl.ANY)] * n


def hbm(n=1):
    return [pl.BlockSpec(memory_space=pltpu.HBM)] * n


def prepare_kernel(means, inv_var, weights, scaled, row):
    values = means[...].astype(F32)
    product = values * inv_var[...]
    scaled[...] = product.astype(BF)
    square = values * product
    norm = functools.reduce(jnp.add, [square[:, i : i + 128] for i in range(0, 1024, 128)])
    norm = 0.5 * jnp.sum(norm, axis=1, keepdims=True)
    for i in range(0, 512, 128):
        row[:, i : i + 128] = weights[:, i : i + 128] - line(norm[i : i + 128])


def prepare(means, inv_var, log_weights):
    return pl.pallas_call(
        prepare_kernel,
        grid=(4,),
        in_specs=[
            pl.BlockSpec((512, 1024), lambda i: (i, 0)),
            pl.BlockSpec((1, 1024), lambda i: (0, 0)),
            pl.BlockSpec((1, 512), lambda i: (0, i)),
        ],
        out_specs=(
            pl.BlockSpec((512, 1024), lambda i: (i, 0)),
            pl.BlockSpec((1, 512), lambda i: (0, i)),
        ),
        out_shape=(
            pltpu.HBM((2048, 1024), BF),
            jax.ShapeDtypeStruct((1, 2048), F32),
        ),
        compiler_params=params(),
        cost_estimate=pl.CostEstimate(flops=6 << 21, bytes_accessed=8 << 20, transcendentals=0),
    )(still(means), inv_var.reshape(1, 1024), log_weights.reshape(1, 2048))


def place_kernel(at, own, before, after, far, *refs):
    out = refs[-1]
    x = at[0]
    for step, piece in ((0, own), (3, before), (1, after), (2, far)):
        slot = lax.rem(x + step, 4)
        out[pl.ds(pl.multiple_of(slot * 64, 64), 64), :] = piece[...]


def gather_x(at, own, ahead, there=()):
    parts = (own, shift(own, "x", 1), shift(own, "x", -1), shift(own, "x", 2))
    return pl.pallas_call(
        place_kernel,
        out_shape=jax.ShapeDtypeStruct((256, 1024), BF),
        in_specs=[scalar()] + [whole()] * 4 + hbm(len(ahead)) + anywhere(len(there)),
        out_specs=whole(),
        compiler_params=params(),
    )(at, *parts, *(still(a) for a in ahead), *there)


def column(row):
    return jnp.transpose(jnp.broadcast_to(row, (128, 128)))[:, 0:1]


def line(col):
    return jnp.transpose(jnp.broadcast_to(col, (128, 128)))[0:1, :]


def score_kernel(at, own, other, scaled, bias, score, share, rows, peak, total):
    step = pl.program_id(0)
    c = at[1]

    @pl.when(step == 0)
    def _():
        rows[pl.ds(pl.multiple_of(c * 256, 256), 256), :] = own[...]
        rows[pl.ds(pl.multiple_of((1 - c) * 256, 256), 256), :] = other[...]
        peak[...] = jnp.full_like(peak, -jnp.inf)
        total[...] = jnp.zeros_like(total)

    for r in range(2):
        cut = slice(r * 256, r * 256 + 256)
        tile = lax.dot_general(
            rows[cut, :], scaled[...], (((1,), (1,)), ((), ())), preferred_element_type=F32
        )
        tile = tile + bias[...]
        score[cut, :] = tile
        lanes = [tile[:, i : i + 128] for i in range(0, tile.shape[1], 128)]
        old = peak[cut, :]
        top = functools.reduce(jnp.maximum, lanes, old)
        added = functools.reduce(jnp.add, [jnp.exp(lane - top) for lane in lanes])
        total[cut, :] = total[cut, :] * jnp.exp(old - top) + added
        peak[cut, :] = top

    @pl.when(step == pl.num_programs(0) - 1)
    def _():
        for b in range(4):
            cut = slice(b * 128, b * 128 + 128)
            top = jnp.max(peak[cut, :], axis=1, keepdims=True)
            mass = jnp.sum(total[cut, :] * jnp.exp(peak[cut, :] - top), axis=1, keepdims=True)
            share[:, b, :] = jnp.broadcast_to(line(top + jnp.log(mass)), (32, 128))


def scores(at, own, other, scaled, bias_row):
    width = 512
    return pl.pallas_call(
        score_kernel,
        grid=(2048 // width,),
        out_shape=(
            pltpu.HBM((512, 2048), F32),
            jax.ShapeDtypeStruct((32, 4, 128), F32),
        ),
        in_specs=[
            scalar(),
            pl.BlockSpec((256, 1024), lambda i: (0, 0)),
            pl.BlockSpec((256, 1024), lambda i: (0, 0)),
            pl.BlockSpec((width, 1024), lambda i: (i, 0)),
            pl.BlockSpec((1, width), lambda i: (0, i)),
        ],
        out_specs=(
            pl.BlockSpec((512, width), lambda i: (0, i)),
            pl.BlockSpec((32, 4, 128), lambda i: (0, 0, 0)),
        ),
        scratch_shapes=[VMEM((512, 1024), BF), VMEM((512, 128), F32), VMEM((512, 128), F32)],
        compiler_params=params(),
        cost_estimate=pl.CostEstimate(
            flops=2 * 512 * 2048 * 1024, bytes_accessed=9 << 20, transcendentals=1 << 20
        ),
    )(at, own, other, still(scaled), bias_row)


def joined(shares):
    top = jnp.max(shares, axis=0)
    return top + jnp.log(jnp.sum(jnp.exp(shares - top[None]), axis=0))


def split_count(count):
    high = count.astype(BF).astype(F32)
    return jnp.concatenate([high, count - high, jnp.zeros((6, 512), F32)], axis=0).astype(BF)


def add_kernel(kept, got_a, got_b, *refs):
    out = refs[-1]
    other = jnp.concatenate([got_a[...], got_b[...]], axis=2).astype(F32)
    mine = kept[...].astype(F32)
    out[:, 0:32, :] = (mine[:, 0:32, :] + other[:, 0:32, :]).astype(BF)
    tails = mine[0, 32:34, :] + other[0, 32:34, :]
    count = tails[0:1, :] + tails[1:2, :]
    out[:, 32:40, :] = jnp.broadcast_to(split_count(count)[None], (4, 8, 512))


def added(kept, got_a, got_b, *first):
    return pl.pallas_call(
        add_kernel,
        grid=(4,),
        in_specs=[
            pl.BlockSpec((4, 40, 512), lambda i: (i, 0, 0)),
            pl.BlockSpec((4, 40, 256), lambda i: (i, 0, 0)),
            pl.BlockSpec((4, 40, 256), lambda i: (i, 0, 0)),
        ]
        + anywhere(len(first)),
        out_specs=pl.BlockSpec((4, 40, 512), lambda i: (i, 0, 0)),
        out_shape=pltpu.HBM((16, 40, 512), BF),
        compiler_params=params(),
    )(still(kept), got_a, got_b, *first)


def sums_kernel(at, shares, scaled, bias, *refs):
    pieces = refs[:8]
    kept, away_a, away_b = refs[9:12]
    rows, weights, lse, wide, sems = refs[12:]
    copies = [
        pltpu.make_async_copy(piece, rows.at[pl.ds(i * 256, 256)], sems.at[i])
        for i, piece in enumerate(pieces)
    ]
    for copy in copies:
        copy.start()
    y, c = at[2], at[1]
    for yy in range(4):
        lse[pl.ds(yy * 4, 4), :] = joined(shares[yy])
    for b in range(0, 512, 128):
        wide[b : b + 128, :] = jnp.transpose(jnp.broadcast_to(bias[:, b : b + 128], (128, 128)))
    shift_up = jnp.concatenate([wide[...], wide[...]], axis=1)
    count = jnp.zeros((512, 128), F32)
    for i in range(8):
        there = lax.rem(y + (0, 3, 1, 2)[i // 2], 4)
        core = c if i % 2 == 0 else 1 - c
        at_row = there * 4 + core * 2
        norm = jnp.concatenate([lse[pl.ds(at_row, 1), :], lse[pl.ds(at_row + 1, 1), :]], axis=1)
        cut = slice(i * 256, i * 256 + 256)
        copies[i].wait()
        score = lax.dot_general(
            scaled[...], rows[cut, :], (((1,), (1,)), ((), ())), preferred_element_type=F32
        )
        weight = jnp.exp(score + shift_up - norm).astype(BF)
        weights[:, cut] = weight
        count = count + weight[:, :128].astype(F32) + weight[:, 128:].astype(F32)
    count = jnp.sum(count, axis=1, keepdims=True)
    count = jnp.concatenate([line(count[b : b + 128]) for b in range(0, 512, 128)], axis=1)
    tail = jnp.broadcast_to(split_count(count)[None], (16, 8, 512))
    kept[:, 32:40, :] = tail
    away_a[:, 32:40, :] = tail[:, :, :256]
    away_b[:, 32:40, :] = tail[:, :, 256:]
    even = at[4] == 0
    for j in range(4):
        block = lax.dot_general(
            weights[...],
            rows[:, j * 256 : j * 256 + 256],
            (((1,), (0,)), ((), ())),
            preferred_element_type=F32,
        )
        block = jnp.transpose(block.astype(BF))
        for h in range(4):
            first = block[h * 64 : h * 64 + 32, :]
            second = block[h * 64 + 32 : h * 64 + 64, :]
            kept[j * 4 + h, 0:32, :] = jnp.where(even, first, second)
            other = jnp.where(even, second, first)
            away_a[j * 4 + h, 0:32, :] = other[:, :256]
            away_b[j * 4 + h, 0:32, :] = other[:, 256:]


def partial_sums(at, shares, scaled, bias_row, pieces, first):
    return pl.pallas_call(
        sums_kernel,
        grid_spec=pltpu.PrefetchScalarGridSpec(
            num_scalar_prefetch=1,
            grid=(1,),
            in_specs=[
                pl.BlockSpec((4, 8, 4, 128), lambda i, at: (0, 0, 0, 0)),
                pl.BlockSpec((512, 1024), lambda i, at: (at[2], 0)),
                pl.BlockSpec((1, 512), lambda i, at: (0, at[2])),
            ]
            + anywhere(9),
            out_specs=[
                pl.BlockSpec((16, 40, width), lambda i, at: (0, 0, 0)) for width in (512, 256, 256)
            ],
            scratch_shapes=[
                VMEM((2048, 1024), BF),
                VMEM((512, 2048), BF),
                VMEM((16, 128), F32),
                VMEM((512, 128), F32),
                pltpu.SemaphoreType.DMA((8,)),
            ],
        ),
        out_shape=[pltpu.HBM((16, 40, width), BF) for width in (512, 256, 256)],
        compiler_params=params(),
        cost_estimate=pl.CostEstimate(
            flops=4 * 512 * 2048 * 1024, bytes_accessed=8 << 20, transcendentals=1 << 20
        ),
    )(at, shares, still(scaled), bias_row, *pieces, first)


def resp_kernel(at, shares, score, *refs):
    outs, norm, held, sems = refs[:5], refs[5], refs[6], refs[7]
    x, c, y = at[0], at[1], at[2]
    copies = []
    for j in range(8):
        core = 1 - c if j < 4 else c
        start = pl.multiple_of(core * 256 + lax.rem(x + j % 4, 4) * 64, 64)
        copies.append(
            (start, pltpu.make_async_copy(score.at[pl.ds(start, 64)], held.at[j], sems.at[j]))
        )
    for _, copy in copies:
        copy.start()
    lse = joined(shares[y])
    for b in range(4):
        norm[b * 128 : b * 128 + 128, :] = jnp.transpose(
            jnp.broadcast_to(lse[b : b + 1, :], (128, 128))
        )
    for j, (start, copy) in enumerate(copies):
        copy.wait()
        block = jnp.exp(held[j] - norm[pl.ds(start, 64), 0:1]).astype(BF)
        if j % 4 == 0:
            outs[j // 4][...] = block
        else:
            outs[1 + j % 4][j // 4 * 64 : j // 4 * 64 + 64, :] = block


def responsibilities(at, shares, score):
    return pl.pallas_call(
        resp_kernel,
        in_specs=[scalar(), whole()] + hbm(),
        out_specs=[whole()] * 5,
        scratch_shapes=[
            VMEM((512, 128), F32),
            VMEM((8, 64, 2048), F32),
            pltpu.SemaphoreType.DMA((8,)),
        ],
        out_shape=[jax.ShapeDtypeStruct((64, 2048), BF)] * 2
        + [jax.ShapeDtypeStruct((128, 2048), BF)] * 3,
        compiler_params=params(),
        cost_estimate=pl.CostEstimate(flops=1 << 21, bytes_accessed=6 << 20, transcendentals=1 << 20),
    )(at, shares, still(score))


def cut_kernel(at, means, ahead, out, turned):
    del ahead
    for i in range(0, 2048, 128):
        turned[:, i : i + 128] = jnp.transpose(means[i : i + 128, :].astype(F32))
    out[...] = turned[pl.ds(pl.multiple_of(lax.rem(at[3], 4) * 32, 32), 32), :]


def mean_columns(at, means, ahead):
    return pl.pallas_call(
        cut_kernel,
        grid_spec=pltpu.PrefetchScalarGridSpec(
            num_scalar_prefetch=1,
            grid=(1,),
            in_specs=[pl.BlockSpec((2048, 128), lambda i, at: (0, at[3] // 4))] + anywhere(),
            out_specs=pl.BlockSpec((32, 2048), lambda i, at: (0, 0)),
            scratch_shapes=[VMEM((128, 2048), F32)],
        ),
        out_shape=pltpu.HBM((32, 2048), F32),
        compiler_params=params(),
    )(at, still(means), ahead)


def lay_kernel(at, *refs):
    pieces, out, sems = refs[:8], refs[8], refs[9]
    x, c = at[0], at[1]
    copies = []
    for j in range(8):
        core = 1 - c if j < 4 else c
        comp = lax.rem(x + 4 - j % 4, 4) * 2 + core
        spot = out.at[:, pl.ds(pl.multiple_of(comp * 2048, 2048), 2048)]
        piece = pieces[j].at[pl.ds(64, 64)] if j > 4 else pieces[j]
        copies.append(pltpu.make_async_copy(piece, spot, sems.at[j]))
    for copy in copies:
        copy.start()
    for copy in copies:
        copy.wait()


def lay_out(at, pieces):
    return pl.pallas_call(
        lay_kernel,
        in_specs=[scalar()] + anywhere(8),
        out_specs=pl.BlockSpec(memory_space=pl.ANY),
        scratch_shapes=[pltpu.SemaphoreType.DMA((8,))],
        out_shape=jax.ShapeDtypeStruct((64, 16384), BF),
        compiler_params=params(),
        cost_estimate=pl.CostEstimate(flops=0, bytes_accessed=4 << 20, transcendentals=0),
    )(at, *pieces)


def body(points, means, log_weights, inv_var):
    x, c, y, h, l = (lax.axis_index(a) for a in "xcyhl")
    at = jnp.stack([x, c, y, y * 8 + h * 2 + l, l]).astype(jnp.int32)

    far = shift(points, "y", 2)
    scaled, bias_row = prepare(means, inv_var, log_weights)

    own = gather_x(at, points, (scaled,), (far,))
    other = shift(own, "c", 1)
    before = shift(own, "y", 1)
    after = shift(own, "y", -1)
    score, share = scores(at, own, other, scaled, bias_row)

    shares = lax.all_to_all(share, ("y", "x", "c"), split_axis=0, concat_axis=0, tiled=True)
    mean_cols = mean_columns(at, means, share)
    far = gather_x(at, far, (mean_cols,), (shares,))
    shares = shares.reshape(4, 8, 4, 128)
    pieces = [own, other]
    for mine in (before, after, far):
        pieces += [mine, shift(mine, "c", 1)]

    blocks = responsibilities(at, shares, score)
    pairs = [shift(b, "x", j + 1) for j, b in enumerate(blocks[2:])]
    kept, away_a, away_b = partial_sums(at, shares, scaled, bias_row, pieces, blocks[0])
    near = [(z, z ^ 1) for z in range(8)]
    got_a = lax.ppermute(away_a, ("h", "l"), near)
    near = [(z, (z + (1 if z % 2 else 7)) % 8) for z in range(8)]
    got_b = lax.ppermute(away_b, ("h", "l"), near)
    sums = added(kept, got_a, got_b, *pairs)
    sent = lax.all_to_all(sums, ("y", "h"), split_axis=0, concat_axis=0, tiled=True)
    theirs = [shift(b, "c", 1) for b in [blocks[0]] + [pair[:64] for pair in pairs]]
    held = theirs + [blocks[1]] + pairs
    resp_rows = lay_out(at, held)

    sums = jnp.sum(sent.reshape(4, 4, 40, 512).astype(F32), axis=1)
    counts = (sums[:, 32, :] + sums[:, 33, :]).reshape(2048)
    sums = sums[:, :32, :].transpose(1, 0, 2).reshape(32, 2048)
    new_means_t = (sums + mean_cols) / (counts[None, :] + 1.0)

    lse = joined(lax.dynamic_index_in_dim(shares, y, 0, keepdims=False)).reshape(8, 64)
    own_lse = lax.dynamic_index_in_dim(lse, c * 4 + x, 0, keepdims=False)
    points_f = points.astype(F32)
    const_term = 0.5 * jnp.sum(jnp.log(inv_var)) - 0.5 * 1024 * math.log(2.0 * math.pi)
    loglik = own_lse - 0.5 * jnp.sum(points_f * points_f * inv_var[None, :], axis=1) + const_term
    return (resp_rows, counts, new_means_t, loglik)


def solution(mesh):
    axes = ("y", "h", "l", "x", "c")
    mesh = Mesh(mesh.devices.reshape(4, 4, 2, 4, 2), axes)
    comp, pt = ("x", "c"), ("y", "h", "l")
    return jax.shard_map(
        body,
        mesh=mesh,
        in_specs=(P(axes, None), P(comp, None), P(comp), P()),
        out_specs=(P(axes, None), P(comp), P(pt, comp), P(axes)),
        check_vma=False,
    )
```

```python
import functools
import math

import jax
import jax.numpy as jnp
from jax import lax
from jax.experimental import pallas as pl
from jax.experimental.pallas import tpu as pltpu
from jax.sharding import Mesh
from jax.sharding import PartitionSpec as P

BF = jnp.bfloat16
F32 = jnp.float32
VMEM_LIMIT = 24 * 1024 * 1024
VMEM = pltpu.VMEM
SIZES = {"y": 4, "z": 8, "x": 4, "c": 2}


def shift(value, axis, step):
    n = SIZES[axis]
    return lax.ppermute(value, axis, [(i, (i + step) % n) for i in range(n)])


def still(value):
    return pltpu.with_memory_space_constraint(value, pltpu.HBM)


def params():
    return pltpu.CompilerParams(vmem_limit_bytes=VMEM_LIMIT)


def whole():
    return pl.BlockSpec(memory_space=VMEM)


def scalar():
    return pl.BlockSpec(memory_space=pltpu.SMEM)


def anywhere(n=1):
    return [pl.BlockSpec(memory_space=pl.ANY)] * n


def hbm(n=1):
    return [pl.BlockSpec(memory_space=pltpu.HBM)] * n


def prepare_kernel(means, inv_var, weights, scaled, row):
    values = means[...].astype(F32)
    product = values * inv_var[...]
    scaled[...] = product.astype(BF)
    square = values * product
    norm = functools.reduce(jnp.add, [square[:, i : i + 128] for i in range(0, 1024, 128)])
    norm = 0.5 * jnp.sum(norm, axis=1, keepdims=True)
    for i in range(0, 512, 128):
        row[:, i : i + 128] = weights[:, i : i + 128] - line(norm[i : i + 128])


def prepare(means, inv_var, log_weights):
    return pl.pallas_call(
        prepare_kernel,
        grid=(4,),
        in_specs=[
            pl.BlockSpec((512, 1024), lambda i: (i, 0)),
            pl.BlockSpec((1, 1024), lambda i: (0, 0)),
            pl.BlockSpec((1, 512), lambda i: (0, i)),
        ],
        out_specs=(
            pl.BlockSpec((512, 1024), lambda i: (i, 0)),
            pl.BlockSpec((1, 512), lambda i: (0, i)),
        ),
        out_shape=(
            pltpu.HBM((2048, 1024), BF),
            jax.ShapeDtypeStruct((1, 2048), F32),
        ),
        compiler_params=params(),
        cost_estimate=pl.CostEstimate(flops=6 << 21, bytes_accessed=8 << 20, transcendentals=0),
    )(still(means), still(inv_var.reshape(1, 1024)), still(log_weights.reshape(1, 2048)))


def place_kernel(at, own, before, after, far, *refs):
    out = refs[-1]
    x = at[0]
    for step, piece in ((0, own), (3, before), (1, after), (2, far)):
        slot = lax.rem(x + step, 4)
        out[pl.ds(pl.multiple_of(slot * 64, 64), 64), :] = piece[...]


def gather_x(at, own, ahead, there=()):
    parts = (own, shift(own, "x", 1), shift(own, "x", -1), shift(own, "x", 2))
    return pl.pallas_call(
        place_kernel,
        out_shape=jax.ShapeDtypeStruct((256, 1024), BF),
        in_specs=[scalar()] + [whole()] * 4 + hbm(len(ahead)) + anywhere(len(there)),
        out_specs=whole(),
        compiler_params=params(),
    )(at, *parts, *(still(a) for a in ahead), *there)


def column(row):
    return jnp.transpose(jnp.broadcast_to(row, (128, 128)))[:, 0:1]


def line(col):
    return jnp.transpose(jnp.broadcast_to(col, (128, 128)))[0:1, :]


def score_kernel(at, own, other, scaled, bias, score, share, rows, peak, total):
    step = pl.program_id(0)
    c = at[1]

    @pl.when(step == 0)
    def _():
        rows[pl.ds(pl.multiple_of(c * 256, 256), 256), :] = own[...]
        rows[pl.ds(pl.multiple_of((1 - c) * 256, 256), 256), :] = other[...]
        peak[...] = jnp.full_like(peak, -jnp.inf)
        total[...] = jnp.zeros_like(total)

    for r in range(2):
        cut = slice(r * 256, r * 256 + 256)
        tile = lax.dot_general(
            rows[cut, :], scaled[...], (((1,), (1,)), ((), ())), preferred_element_type=F32
        )
        tile = tile + bias[...]
        score[cut, :] = tile
        lanes = [tile[:, i : i + 128] for i in range(0, tile.shape[1], 128)]
        old = peak[cut, :]
        top = functools.reduce(jnp.maximum, lanes, old)
        added = functools.reduce(jnp.add, [jnp.exp(lane - top) for lane in lanes])
        total[cut, :] = total[cut, :] * jnp.exp(old - top) + added
        peak[cut, :] = top

    @pl.when(step == pl.num_programs(0) - 1)
    def _():
        for b in range(4):
            cut = slice(b * 128, b * 128 + 128)
            top = jnp.max(peak[cut, :], axis=1, keepdims=True)
            mass = jnp.sum(total[cut, :] * jnp.exp(peak[cut, :] - top), axis=1, keepdims=True)
            share[:, b, :] = jnp.broadcast_to(line(top + jnp.log(mass)), (32, 128))


def scores(at, own, other, scaled, bias_row):
    width = 512
    return pl.pallas_call(
        score_kernel,
        grid=(2048 // width,),
        out_shape=(
            pltpu.HBM((512, 2048), F32),
            jax.ShapeDtypeStruct((32, 4, 128), F32),
        ),
        in_specs=[
            scalar(),
            pl.BlockSpec((256, 1024), lambda i: (0, 0)),
            pl.BlockSpec((256, 1024), lambda i: (0, 0)),
            pl.BlockSpec((width, 1024), lambda i: (i, 0)),
            pl.BlockSpec((1, width), lambda i: (0, i)),
        ],
        out_specs=(
            pl.BlockSpec((512, width), lambda i: (0, i)),
            pl.BlockSpec((32, 4, 128), lambda i: (0, 0, 0)),
        ),
        scratch_shapes=[VMEM((512, 1024), BF), VMEM((512, 128), F32), VMEM((512, 128), F32)],
        compiler_params=params(),
        cost_estimate=pl.CostEstimate(
            flops=2 * 512 * 2048 * 1024, bytes_accessed=9 << 20, transcendentals=1 << 20
        ),
    )(at, own, other, still(scaled), bias_row)


def joined(shares):
    top = jnp.max(shares, axis=0)
    return top + jnp.log(jnp.sum(jnp.exp(shares - top[None]), axis=0))


def sums_kernel(at, shares, scaled, bias, *refs):
    pieces = refs[:8]
    sums = refs[8]
    rows, weights, lse, wide, sems = refs[9:]
    copies = [
        pltpu.make_async_copy(piece, rows.at[pl.ds(i * 256, 256)], sems.at[i])
        for i, piece in enumerate(pieces)
    ]
    for copy in copies:
        copy.start()
    y, c = at[2], at[1]
    for yy in range(4):
        lse[pl.ds(yy * 4, 4), :] = joined(shares[yy])
    for b in range(0, 512, 128):
        wide[b : b + 128, :] = jnp.transpose(jnp.broadcast_to(bias[:, b : b + 128], (128, 128)))
    shift_up = jnp.concatenate([wide[...], wide[...]], axis=1)
    count = jnp.zeros((512, 128), F32)
    for i in range(8):
        there = lax.rem(y + (0, 3, 1, 2)[i // 2], 4)
        core = c if i % 2 == 0 else 1 - c
        at_row = there * 4 + core * 2
        norm = jnp.concatenate([lse[pl.ds(at_row, 1), :], lse[pl.ds(at_row + 1, 1), :]], axis=1)
        cut = slice(i * 256, i * 256 + 256)
        copies[i].wait()
        score = lax.dot_general(
            scaled[...], rows[cut, :], (((1,), (1,)), ((), ())), preferred_element_type=F32
        )
        weight = jnp.exp(score + shift_up - norm).astype(BF)
        weights[:, cut] = weight
        count = count + weight[:, :128].astype(F32) + weight[:, 128:].astype(F32)
    count = jnp.sum(count, axis=1, keepdims=True)
    count = jnp.concatenate([line(count[b : b + 128]) for b in range(0, 512, 128)], axis=1)
    digits = []
    for _ in range(8):
        digit = jnp.floor(count * (1.0 / 1024.0))
        digits.append(digit)
        count = (count - digit * 1024.0) * 32.0
    tail = jnp.concatenate(digits, axis=0).astype(BF)
    sums[:, :, 32:40, :] = jnp.broadcast_to(tail[None, None], (8, 4, 8, 512))
    for j in range(4):
        block = lax.dot_general(
            weights[...],
            rows[:, j * 256 : j * 256 + 256],
            (((1,), (0,)), ((), ())),
            preferred_element_type=F32,
        )
        block = jnp.transpose(block.astype(BF))
        sums[:, j, 0:32, :] = block.reshape(8, 32, 512)


def partial_sums(at, shares, scaled, bias_row, pieces):
    return pl.pallas_call(
        sums_kernel,
        grid_spec=pltpu.PrefetchScalarGridSpec(
            num_scalar_prefetch=1,
            grid=(1,),
            in_specs=[
                pl.BlockSpec((4, 8, 4, 128), lambda i, at: (0, 0, 0, 0)),
                pl.BlockSpec((512, 1024), lambda i, at: (at[2], 0)),
                pl.BlockSpec((1, 512), lambda i, at: (0, at[2])),
            ]
            + anywhere(8),
            out_specs=pl.BlockSpec((8, 4, 40, 512), lambda i, at: (0, 0, 0, 0)),
            scratch_shapes=[
                VMEM((2048, 1024), BF),
                VMEM((512, 2048), BF),
                VMEM((16, 128), F32),
                VMEM((512, 128), F32),
                pltpu.SemaphoreType.DMA((8,)),
            ],
        ),
        out_shape=pltpu.HBM((8, 4, 40, 512), BF),
        compiler_params=params(),
        cost_estimate=pl.CostEstimate(
            flops=4 * 512 * 2048 * 1024, bytes_accessed=8 << 20, transcendentals=1 << 20
        ),
    )(at, shares, still(scaled), bias_row, *pieces)


def resp_kernel(at, shares, score, first, *refs):
    del first
    outs, norm, held, sems = refs[:5], refs[5], refs[6], refs[7]
    x, c, y = at[0], at[1], at[2]
    copies = []
    for j in range(8):
        core = 1 - c if j < 4 else c
        start = pl.multiple_of(core * 256 + lax.rem(x + j % 4, 4) * 64, 64)
        copies.append(
            (start, pltpu.make_async_copy(score.at[pl.ds(start, 64)], held.at[j], sems.at[j]))
        )
    for _, copy in copies:
        copy.start()
    lse = joined(shares[y])
    for b in range(4):
        norm[b * 128 : b * 128 + 128, :] = jnp.transpose(
            jnp.broadcast_to(lse[b : b + 1, :], (128, 128))
        )
    for j, (start, copy) in enumerate(copies):
        copy.wait()
        block = jnp.exp(held[j] - norm[pl.ds(start, 64), 0:1]).astype(BF)
        if j % 4 == 0:
            outs[j // 4][...] = block
        else:
            outs[1 + j % 4][j // 4 * 64 : j // 4 * 64 + 64, :] = block


def responsibilities(at, shares, score, first):
    return pl.pallas_call(
        resp_kernel,
        in_specs=[scalar(), whole()] + hbm(2),
        out_specs=[whole()] * 5,
        scratch_shapes=[
            VMEM((512, 128), F32),
            VMEM((8, 64, 2048), F32),
            pltpu.SemaphoreType.DMA((8,)),
        ],
        out_shape=[jax.ShapeDtypeStruct((64, 2048), BF)] * 2
        + [jax.ShapeDtypeStruct((128, 2048), BF)] * 3,
        compiler_params=params(),
        cost_estimate=pl.CostEstimate(flops=1 << 21, bytes_accessed=6 << 20, transcendentals=1 << 20),
    )(at, shares, still(score), still(first))


def cut_kernel(at, means, ahead, out, turned):
    del ahead
    for i in range(0, 2048, 128):
        turned[:, i : i + 128] = jnp.transpose(means[i : i + 128, :].astype(F32))
    out[...] = turned[pl.ds(pl.multiple_of(lax.rem(at[3], 4) * 32, 32), 32), :]


def mean_columns(at, means, ahead):
    return pl.pallas_call(
        cut_kernel,
        grid_spec=pltpu.PrefetchScalarGridSpec(
            num_scalar_prefetch=1,
            grid=(1,),
            in_specs=[pl.BlockSpec((2048, 128), lambda i, at: (0, at[3] // 4))] + anywhere(),
            out_specs=pl.BlockSpec((32, 2048), lambda i, at: (0, 0)),
            scratch_shapes=[VMEM((128, 2048), F32)],
        ),
        out_shape=pltpu.HBM((32, 2048), F32),
        compiler_params=params(),
    )(at, still(means), ahead)


def lay_kernel(at, *refs):
    pieces, out, sems = refs[:8], refs[8], refs[9]
    x, c = at[0], at[1]
    copies = []
    for j in range(8):
        core = 1 - c if j < 4 else c
        comp = lax.rem(x + 4 - j % 4, 4) * 2 + core
        spot = out.at[:, pl.ds(pl.multiple_of(comp * 2048, 2048), 2048)]
        piece = pieces[j].at[pl.ds(64, 64)] if j > 4 else pieces[j]
        copies.append(pltpu.make_async_copy(piece, spot, sems.at[j]))
    for copy in copies:
        copy.start()
    for copy in copies:
        copy.wait()


def lay_out(at, pieces):
    return pl.pallas_call(
        lay_kernel,
        in_specs=[scalar()] + anywhere(8),
        out_specs=pl.BlockSpec(memory_space=pl.ANY),
        scratch_shapes=[pltpu.SemaphoreType.DMA((8,))],
        out_shape=jax.ShapeDtypeStruct((64, 16384), BF),
        compiler_params=params(),
    )(at, *pieces)


def body(points, means, log_weights, inv_var):
    x, c, y, z = (lax.axis_index(a) for a in "xcyz")
    at = jnp.stack([x, c, y, y * 8 + z]).astype(jnp.int32)

    far = shift(points, "y", 2)
    scaled, bias_row = prepare(means, inv_var, log_weights)

    own = gather_x(at, points, (scaled,), (far,))
    other = shift(own, "c", 1)
    before = shift(own, "y", 1)
    after = shift(own, "y", -1)
    score, share = scores(at, own, other, scaled, bias_row)

    shares = lax.all_to_all(share, ("y", "x", "c"), split_axis=0, concat_axis=0, tiled=True)
    mean_cols = mean_columns(at, means, share)
    far = gather_x(at, far, (mean_cols,), (shares,))
    shares = shares.reshape(4, 8, 4, 128)
    pieces = [own, other]
    for mine in (before, after, far):
        pieces += [mine, shift(mine, "c", 1)]

    sums = partial_sums(at, shares, scaled, bias_row, pieces)
    blocks = responsibilities(at, shares, score, sums)
    pairs = [shift(b, "x", j + 1) for j, b in enumerate(blocks[2:])]
    theirs = [shift(b, "c", 1) for b in [blocks[0]] + [pair[:64] for pair in pairs]]
    held = theirs + [blocks[1]] + pairs
    sums = lax.psum_scatter(sums.reshape(1280, 512), "z", scatter_dimension=0, tiled=True)
    sent = lax.all_to_all(sums, "y", split_axis=0, concat_axis=0, tiled=True)
    resp_rows = lay_out(at, held)

    sent = sent.reshape(4, 40, 512).astype(F32)
    counts = sum(sent[:, 32 + i, :] * (32.0 ** (2 - i)) for i in range(8)).reshape(2048)
    sums = sent[:, :32, :].transpose(1, 0, 2).reshape(32, 2048)
    new_means_t = (sums + mean_cols) / (counts[None, :] + 1.0)

    lse = joined(lax.dynamic_index_in_dim(shares, y, 0, keepdims=False)).reshape(8, 64)
    own_lse = lax.dynamic_index_in_dim(lse, c * 4 + x, 0, keepdims=False)
    points_f = points.astype(F32)
    const_term = 0.5 * jnp.sum(jnp.log(inv_var)) - 0.5 * 1024 * math.log(2.0 * math.pi)
    loglik = own_lse - 0.5 * jnp.sum(points_f * points_f * inv_var[None, :], axis=1) + const_term
    return (resp_rows, counts, new_means_t, loglik)


def solution(mesh):
    axes = ("y", "z", "x", "c")
    mesh = Mesh(mesh.devices.reshape(4, 8, 4, 2), axes)
    comp, pt = ("x", "c"), ("y", "z")
    return jax.shard_map(
        body,
        mesh=mesh,
        in_specs=(P(axes, None), P(comp, None), P(comp), P()),
        out_specs=(P(axes, None), P(comp), P(pt, comp), P(axes)),
        check_vma=False,
    )
```

```python
import functools
import math

import jax
import jax.numpy as jnp
from jax import lax
from jax.experimental import pallas as pl
from jax.experimental.pallas import tpu as pltpu
from jax.sharding import Mesh
from jax.sharding import PartitionSpec as P

BF = jnp.bfloat16
F32 = jnp.float32
VMEM_LIMIT = 24 * 1024 * 1024
VMEM = pltpu.VMEM
SIZES = {"y": 4, "x": 4, "c": 2}


def shift(value, axis, step):
    n = SIZES[axis]
    return lax.ppermute(value, axis, [(i, (i + step) % n) for i in range(n)])


def swap(value, bit):
    return lax.ppermute(value, ("h", "l"), [(z, z ^ bit) for z in range(8)])


def still(value):
    return pltpu.with_memory_space_constraint(value, pltpu.HBM)


def params():
    return pltpu.CompilerParams(vmem_limit_bytes=VMEM_LIMIT)


def whole():
    return pl.BlockSpec(memory_space=VMEM)


def scalar():
    return pl.BlockSpec(memory_space=pltpu.SMEM)


def anywhere(n=1):
    return [pl.BlockSpec(memory_space=pl.ANY)] * n


def hbm(n=1):
    return [pl.BlockSpec(memory_space=pltpu.HBM)] * n


def prepare_kernel(means, inv_var, weights, scaled, row):
    values = means[...].astype(F32)
    product = values * inv_var[...]
    scaled[...] = product.astype(BF)
    square = values * product
    norm = functools.reduce(jnp.add, [square[:, i : i + 128] for i in range(0, 1024, 128)])
    norm = 0.5 * jnp.sum(norm, axis=1, keepdims=True)
    for i in range(0, 512, 128):
        row[:, i : i + 128] = weights[:, i : i + 128] - line(norm[i : i + 128])


def prepare(means, inv_var, log_weights):
    return pl.pallas_call(
        prepare_kernel,
        grid=(4,),
        in_specs=[
            pl.BlockSpec((512, 1024), lambda i: (i, 0)),
            pl.BlockSpec((1, 1024), lambda i: (0, 0)),
            pl.BlockSpec((1, 512), lambda i: (0, i)),
        ],
        out_specs=(
            pl.BlockSpec((512, 1024), lambda i: (i, 0)),
            pl.BlockSpec((1, 512), lambda i: (0, i)),
        ),
        out_shape=(
            pltpu.HBM((2048, 1024), BF),
            jax.ShapeDtypeStruct((1, 2048), F32),
        ),
        compiler_params=params(),
        cost_estimate=pl.CostEstimate(flops=6 << 21, bytes_accessed=8 << 20, transcendentals=0),
    )(still(means), still(inv_var.reshape(1, 1024)), still(log_weights.reshape(1, 2048)))


def place_kernel(at, own, before, after, far, *refs):
    out = refs[-1]
    x = at[0]
    for step, piece in ((0, own), (3, before), (1, after), (2, far)):
        slot = lax.rem(x + step, 4)
        out[pl.ds(pl.multiple_of(slot * 64, 64), 64), :] = piece[...]


def gather_x(at, own, ahead, there=()):
    parts = (own, shift(own, "x", 1), shift(own, "x", -1), shift(own, "x", 2))
    return pl.pallas_call(
        place_kernel,
        out_shape=jax.ShapeDtypeStruct((256, 1024), BF),
        in_specs=[scalar()] + [whole()] * 4 + hbm(len(ahead)) + anywhere(len(there)),
        out_specs=whole(),
        compiler_params=params(),
    )(at, *parts, *(still(a) for a in ahead), *there)


def column(row):
    return jnp.transpose(jnp.broadcast_to(row, (128, 128)))[:, 0:1]


def line(col):
    return jnp.transpose(jnp.broadcast_to(col, (128, 128)))[0:1, :]


def score_kernel(at, own, other, scaled, bias, score, share, rows, peak, total):
    step = pl.program_id(0)
    c = at[1]

    @pl.when(step == 0)
    def _():
        rows[pl.ds(pl.multiple_of(c * 256, 256), 256), :] = own[...]
        rows[pl.ds(pl.multiple_of((1 - c) * 256, 256), 256), :] = other[...]
        peak[...] = jnp.full_like(peak, -jnp.inf)
        total[...] = jnp.zeros_like(total)

    for r in range(2):
        cut = slice(r * 256, r * 256 + 256)
        tile = lax.dot_general(
            rows[cut, :], scaled[...], (((1,), (1,)), ((), ())), preferred_element_type=F32
        )
        tile = tile + bias[...]
        score[cut, :] = tile
        lanes = [tile[:, i : i + 128] for i in range(0, tile.shape[1], 128)]
        old = peak[cut, :]
        top = functools.reduce(jnp.maximum, lanes, old)
        added = functools.reduce(jnp.add, [jnp.exp(lane - top) for lane in lanes])
        total[cut, :] = total[cut, :] * jnp.exp(old - top) + added
        peak[cut, :] = top

    @pl.when(step == pl.num_programs(0) - 1)
    def _():
        for b in range(4):
            cut = slice(b * 128, b * 128 + 128)
            top = jnp.max(peak[cut, :], axis=1, keepdims=True)
            mass = jnp.sum(total[cut, :] * jnp.exp(peak[cut, :] - top), axis=1, keepdims=True)
            share[:, b, :] = jnp.broadcast_to(line(top + jnp.log(mass)), (32, 128))


def scores(at, own, other, scaled, bias_row):
    width = 512
    return pl.pallas_call(
        score_kernel,
        grid=(2048 // width,),
        out_shape=(
            pltpu.HBM((512, 2048), F32),
            jax.ShapeDtypeStruct((32, 4, 128), F32),
        ),
        in_specs=[
            scalar(),
            pl.BlockSpec((256, 1024), lambda i: (0, 0)),
            pl.BlockSpec((256, 1024), lambda i: (0, 0)),
            pl.BlockSpec((width, 1024), lambda i: (i, 0)),
            pl.BlockSpec((1, width), lambda i: (0, i)),
        ],
        out_specs=(
            pl.BlockSpec((512, width), lambda i: (0, i)),
            pl.BlockSpec((32, 4, 128), lambda i: (0, 0, 0)),
        ),
        scratch_shapes=[VMEM((512, 1024), BF), VMEM((512, 128), F32), VMEM((512, 128), F32)],
        compiler_params=params(),
        cost_estimate=pl.CostEstimate(
            flops=2 * 512 * 2048 * 1024, bytes_accessed=9 << 20, transcendentals=1 << 20
        ),
    )(at, own, other, still(scaled), bias_row)


def joined(shares):
    top = jnp.max(shares, axis=0)
    return top + jnp.log(jnp.sum(jnp.exp(shares - top[None]), axis=0))


def hold_kernel(*refs):
    del refs


def hold(value, *first):
    return pl.pallas_call(
        hold_kernel,
        out_shape=pltpu.HBM(value.shape, value.dtype),
        in_specs=hbm() + anywhere(len(first)),
        out_specs=pl.BlockSpec(memory_space=pltpu.HBM),
        input_output_aliases={0: 0},
        compiler_params=params(),
    )(value, *first)


def sums_kernel(at, shares, scaled, bias, *refs):
    pieces = refs[:8]
    sums, counts = refs[9:11]
    rows, weights, lse, wide, sems = refs[11:]
    copies = [
        pltpu.make_async_copy(piece, rows.at[pl.ds(i * 256, 256)], sems.at[i])
        for i, piece in enumerate(pieces)
    ]
    for copy in copies:
        copy.start()
    y, c = at[2], at[1]
    for yy in range(4):
        lse[pl.ds(yy * 4, 4), :] = joined(shares[yy])
    for b in range(0, 512, 128):
        wide[b : b + 128, :] = jnp.transpose(jnp.broadcast_to(bias[:, b : b + 128], (128, 128)))
    shift_up = jnp.concatenate([wide[...], wide[...]], axis=1)
    count = jnp.zeros((512, 128), F32)
    for i in range(8):
        there = lax.rem(y + (0, 3, 1, 2)[i // 2], 4)
        core = c if i % 2 == 0 else 1 - c
        at_row = there * 4 + core * 2
        norm = jnp.concatenate([lse[pl.ds(at_row, 1), :], lse[pl.ds(at_row + 1, 1), :]], axis=1)
        cut = slice(i * 256, i * 256 + 256)
        copies[i].wait()
        score = lax.dot_general(
            scaled[...], rows[cut, :], (((1,), (1,)), ((), ())), preferred_element_type=F32
        )
        weight = jnp.exp(score + shift_up - norm).astype(BF)
        weights[:, cut] = weight
        count = count + weight[:, :128].astype(F32) + weight[:, 128:].astype(F32)
    count = jnp.sum(count, axis=1, keepdims=True)
    counts[...] = jnp.zeros_like(counts)
    for b in range(4):
        counts[pl.ds(y * 4 + b, 1), :] = line(count[b * 128 : b * 128 + 128])
    for j in range(4):
        block = lax.dot_general(
            weights[...],
            rows[:, j * 256 : j * 256 + 256],
            (((1,), (0,)), ((), ())),
            preferred_element_type=F32,
        )
        sums[j * 256 : j * 256 + 256, :] = jnp.transpose(block.astype(BF))


def partial_sums(at, shares, scaled, bias_row, pieces, first):
    return pl.pallas_call(
        sums_kernel,
        grid_spec=pltpu.PrefetchScalarGridSpec(
            num_scalar_prefetch=1,
            grid=(1,),
            in_specs=[
                pl.BlockSpec((4, 8, 4, 128), lambda i, at: (0, 0, 0, 0)),
                pl.BlockSpec((512, 1024), lambda i, at: (at[2], 0)),
                pl.BlockSpec((1, 512), lambda i, at: (0, at[2])),
            ]
            + anywhere(9),
            out_specs=(
                pl.BlockSpec((1024, 512), lambda i, at: (0, 0)),
                pl.BlockSpec((16, 128), lambda i, at: (0, 0)),
            ),
            scratch_shapes=[
                VMEM((2048, 1024), BF),
                VMEM((512, 2048), BF),
                VMEM((16, 128), F32),
                VMEM((512, 128), F32),
                pltpu.SemaphoreType.DMA((8,)),
            ],
        ),
        out_shape=(pltpu.HBM((1024, 512), BF), jax.ShapeDtypeStruct((16, 128), F32)),
        compiler_params=params(),
        cost_estimate=pl.CostEstimate(
            flops=4 * 512 * 2048 * 1024, bytes_accessed=8 << 20, transcendentals=1 << 20
        ),
    )(at, shares, still(scaled), bias_row, *pieces, first)


def resp_kernel(at, shares, score, *refs):
    outs, norm, held, sems, across = refs[:5], refs[5], refs[6], refs[7], refs[8]
    outs, out_across = (*outs[:3], across, outs[4]), outs[3]
    x, c, y = at[0], at[1], at[2]
    copies = []
    for j in range(8):
        core = 1 - c if j < 4 else c
        start = pl.multiple_of(core * 256 + lax.rem(x + j % 4, 4) * 64, 64)
        copies.append(
            (start, pltpu.make_async_copy(score.at[pl.ds(start, 64)], held.at[j], sems.at[j]))
        )
    for _, copy in copies:
        copy.start()
    lse = joined(shares[y])
    for b in range(4):
        norm[b * 128 : b * 128 + 128, :] = jnp.transpose(
            jnp.broadcast_to(lse[b : b + 1, :], (128, 128))
        )
    for j, (start, copy) in enumerate(copies):
        copy.wait()
        block = jnp.exp(held[j] - norm[pl.ds(start, 64), 0:1]).astype(BF)
        if j % 4 == 0:
            outs[j // 4][...] = block
        else:
            outs[1 + j % 4][j // 4 * 64 : j // 4 * 64 + 64, :] = block
    copy = pltpu.make_async_copy(across, out_across, sems.at[0])
    copy.start()
    copy.wait()


def responsibilities(at, shares, score):
    return pl.pallas_call(
        resp_kernel,
        in_specs=[scalar(), whole()] + hbm(),
        out_specs=[whole()] * 3 + hbm() + [whole()],
        scratch_shapes=[
            VMEM((512, 128), F32),
            VMEM((8, 64, 2048), F32),
            pltpu.SemaphoreType.DMA((8,)),
            VMEM((128, 2048), BF),
        ],
        out_shape=[jax.ShapeDtypeStruct((64, 2048), BF)] * 2
        + [jax.ShapeDtypeStruct((128, 2048), BF), pltpu.HBM((128, 2048), BF), jax.ShapeDtypeStruct((128, 2048), BF)],
        compiler_params=params(),
        cost_estimate=pl.CostEstimate(flops=1 << 21, bytes_accessed=6 << 20, transcendentals=1 << 20),
    )(at, shares, still(score))


def cut_kernel(at, means, ahead, out, turned):
    del ahead
    for i in range(0, 2048, 128):
        turned[:, i : i + 128] = jnp.transpose(means[i : i + 128, :].astype(F32))
    out[...] = turned[pl.ds(pl.multiple_of(lax.rem(at[3], 4) * 32, 32), 32), :]


def mean_columns(at, means, ahead):
    return pl.pallas_call(
        cut_kernel,
        grid_spec=pltpu.PrefetchScalarGridSpec(
            num_scalar_prefetch=1,
            grid=(1,),
            in_specs=[pl.BlockSpec((2048, 128), lambda i, at: (0, at[3] // 4))] + anywhere(),
            out_specs=pl.BlockSpec((32, 2048), lambda i, at: (0, 0)),
            scratch_shapes=[VMEM((128, 2048), F32)],
        ),
        out_shape=pltpu.HBM((32, 2048), F32),
        compiler_params=params(),
    )(at, still(means), ahead)


def lay_kernel(at, *refs):
    pieces, out, sems = refs[:8], refs[8], refs[9]
    x, c = at[0], at[1]
    copies = []
    for j in range(8):
        core = 1 - c if j < 4 else c
        comp = lax.rem(x + 4 - j % 4, 4) * 2 + core
        spot = out.at[:, pl.ds(pl.multiple_of(comp * 2048, 2048), 2048)]
        piece = pieces[j].at[pl.ds(64, 64)] if j > 4 else pieces[j]
        copies.append(pltpu.make_async_copy(piece, spot, sems.at[j]))
    for copy in copies:
        copy.start()
    for copy in copies:
        copy.wait()


def lay_out(at, pieces):
    return pl.pallas_call(
        lay_kernel,
        in_specs=[scalar()] + anywhere(8),
        out_specs=pl.BlockSpec(memory_space=pl.ANY),
        scratch_shapes=[pltpu.SemaphoreType.DMA((8,))],
        out_shape=jax.ShapeDtypeStruct((64, 16384), BF),
        compiler_params=params(),
        cost_estimate=pl.CostEstimate(flops=0, bytes_accessed=4 << 20, transcendentals=0),
    )(at, *pieces)


def body(points, means, log_weights, inv_var):
    x, c, y, h, l = (lax.axis_index(a) for a in "xcyhl")
    at = jnp.stack([x, c, y, y * 8 + h * 2 + l, l]).astype(jnp.int32)

    far = shift(points, "y", 2)
    scaled, bias_row = prepare(means, inv_var, log_weights)

    own = gather_x(at, points, (scaled,), (far,))
    other = shift(own, "c", 1)
    before = shift(own, "y", 1)
    after = shift(own, "y", -1)
    score, share = scores(at, own, other, scaled, bias_row)

    shares = lax.all_to_all(share, ("y", "x", "c"), split_axis=0, concat_axis=0, tiled=True)
    mean_cols = mean_columns(at, means, share)
    far = gather_x(at, far, (mean_cols,), (shares,))
    shares = shares.reshape(4, 8, 4, 128)
    pieces = [own, other]
    for mine in (before, after, far):
        pieces += [mine, shift(mine, "c", 1)]

    blocks = responsibilities(at, shares, score)
    ahead, behind = shift(blocks[2], "x", 1), shift(blocks[4], "x", 3)
    sums, counts = partial_sums(at, shares, scaled, bias_row, pieces, blocks[0])
    pairs = [ahead, shift(hold(blocks[3], counts), "x", 2), behind]
    sums = hold(sums, ahead, behind)
    sent = lax.all_to_all(sums, ("y", "h", "l"), split_axis=0, concat_axis=0, tiled=True)
    theirs = [shift(b, "c", 1) for b in [blocks[0]] + [pair[:64] for pair in pairs]]
    held = theirs + [blocks[1]] + pairs
    resp_rows = lay_out(at, held)

    counts = counts + swap(counts, 1)
    counts = counts + swap(counts, 2)
    counts = counts + swap(counts, 4)
    counts = sum([shift(counts, "y", i) for i in range(1, 4)], counts).reshape(2048)
    sums = jnp.sum(sent.reshape(4, 8, 32, 512).astype(F32), axis=1)
    sums = sums.transpose(1, 0, 2).reshape(32, 2048)
    new_means_t = (sums + mean_cols) / (counts[None, :] + 1.0)

    lse = joined(lax.dynamic_index_in_dim(shares, y, 0, keepdims=False)).reshape(8, 64)
    own_lse = lax.dynamic_index_in_dim(lse, c * 4 + x, 0, keepdims=False)
    points_f = points.astype(F32)
    const_term = 0.5 * jnp.sum(jnp.log(inv_var)) - 0.5 * 1024 * math.log(2.0 * math.pi)
    loglik = own_lse - 0.5 * jnp.sum(points_f * points_f * inv_var[None, :], axis=1) + const_term
    return (resp_rows, counts, new_means_t, loglik)


def solution(mesh):
    axes = ("y", "h", "l", "x", "c")
    mesh = Mesh(mesh.devices.reshape(4, 4, 2, 4, 2), axes)
    comp, pt = ("x", "c"), ("y", "h", "l")
    return jax.shard_map(
        body,
        mesh=mesh,
        in_specs=(P(axes, None), P(comp, None), P(comp), P()),
        out_specs=(P(axes, None), P(comp), P(pt, comp), P(axes)),
        check_vma=False,
    )
```

```python
import functools
import math

import jax
import jax.numpy as jnp
from jax import lax
from jax.experimental import pallas as pl
from jax.experimental.pallas import tpu as pltpu
from jax.sharding import Mesh
from jax.sharding import PartitionSpec as P

BF = jnp.bfloat16
F32 = jnp.float32
VMEM_LIMIT = 24 * 1024 * 1024
VMEM = pltpu.VMEM
SIZES = {"y": 4, "x": 4, "c": 2}


def shift(value, axis, step):
    n = SIZES[axis]
    return lax.ppermute(value, axis, [(i, (i + step) % n) for i in range(n)])


def still(value):
    return pltpu.with_memory_space_constraint(value, pltpu.HBM)


def params():
    return pltpu.CompilerParams(vmem_limit_bytes=VMEM_LIMIT)


def whole():
    return pl.BlockSpec(memory_space=VMEM)


def scalar():
    return pl.BlockSpec(memory_space=pltpu.SMEM)


def anywhere(n=1):
    return [pl.BlockSpec(memory_space=pl.ANY)] * n


def hbm(n=1):
    return [pl.BlockSpec(memory_space=pltpu.HBM)] * n


def prepare_kernel(means, inv_var, weights, scaled, row):
    values = means[...].astype(F32)
    product = values * inv_var[...]
    scaled[...] = product.astype(BF)
    square = values * product
    norm = functools.reduce(jnp.add, [square[:, i : i + 128] for i in range(0, 1024, 128)])
    norm = 0.5 * jnp.sum(norm, axis=1, keepdims=True)
    for i in range(0, 512, 128):
        row[:, i : i + 128] = weights[:, i : i + 128] - line(norm[i : i + 128])


def prepare(means, inv_var, log_weights):
    return pl.pallas_call(
        prepare_kernel,
        grid=(4,),
        in_specs=[
            pl.BlockSpec((512, 1024), lambda i: (i, 0)),
            pl.BlockSpec((1, 1024), lambda i: (0, 0)),
            pl.BlockSpec((1, 512), lambda i: (0, i)),
        ],
        out_specs=(
            pl.BlockSpec((512, 1024), lambda i: (i, 0)),
            pl.BlockSpec((1, 512), lambda i: (0, i)),
        ),
        out_shape=(
            pltpu.HBM((2048, 1024), BF),
            jax.ShapeDtypeStruct((1, 2048), F32),
        ),
        compiler_params=params(),
        cost_estimate=pl.CostEstimate(flops=6 << 21, bytes_accessed=8 << 20, transcendentals=0),
    )(still(means), still(inv_var.reshape(1, 1024)), still(log_weights.reshape(1, 2048)))


def place_kernel(at, own, before, after, far, *refs):
    out = refs[-1]
    x = at[0]
    for step, piece in ((0, own), (3, before), (1, after), (2, far)):
        slot = lax.rem(x + step, 4)
        out[pl.ds(pl.multiple_of(slot * 64, 64), 64), :] = piece[...]


def gather_x(at, own, ahead, there=()):
    parts = (own, shift(own, "x", 1), shift(own, "x", -1), shift(own, "x", 2))
    return pl.pallas_call(
        place_kernel,
        out_shape=jax.ShapeDtypeStruct((256, 1024), BF),
        in_specs=[scalar()] + [whole()] * 4 + hbm(len(ahead)) + anywhere(len(there)),
        out_specs=whole(),
        compiler_params=params(),
    )(at, *parts, *(still(a) for a in ahead), *there)


def column(row):
    return jnp.transpose(jnp.broadcast_to(row, (128, 128)))[:, 0:1]


def line(col):
    return jnp.transpose(jnp.broadcast_to(col, (128, 128)))[0:1, :]


def score_kernel(at, own, other, scaled, bias, score, share, rows, peak, total):
    step = pl.program_id(0)
    c = at[1]

    @pl.when(step == 0)
    def _():
        rows[pl.ds(pl.multiple_of(c * 256, 256), 256), :] = own[...]
        rows[pl.ds(pl.multiple_of((1 - c) * 256, 256), 256), :] = other[...]
        peak[...] = jnp.full_like(peak, -jnp.inf)
        total[...] = jnp.zeros_like(total)

    for r in range(2):
        cut = slice(r * 256, r * 256 + 256)
        tile = lax.dot_general(
            rows[cut, :], scaled[...], (((1,), (1,)), ((), ())), preferred_element_type=F32
        )
        tile = tile + bias[...]
        score[cut, :] = tile
        lanes = [tile[:, i : i + 128] for i in range(0, tile.shape[1], 128)]
        old = peak[cut, :]
        top = functools.reduce(jnp.maximum, lanes, old)
        added = functools.reduce(jnp.add, [jnp.exp(lane - top) for lane in lanes])
        total[cut, :] = total[cut, :] * jnp.exp(old - top) + added
        peak[cut, :] = top

    @pl.when(step == pl.num_programs(0) - 1)
    def _():
        for b in range(4):
            cut = slice(b * 128, b * 128 + 128)
            top = jnp.max(peak[cut, :], axis=1, keepdims=True)
            mass = jnp.sum(total[cut, :] * jnp.exp(peak[cut, :] - top), axis=1, keepdims=True)
            share[:, b, :] = jnp.broadcast_to(line(top + jnp.log(mass)), (32, 128))


def scores(at, own, other, scaled, bias_row):
    width = 512
    return pl.pallas_call(
        score_kernel,
        grid=(2048 // width,),
        out_shape=(
            pltpu.HBM((512, 2048), F32),
            jax.ShapeDtypeStruct((32, 4, 128), F32),
        ),
        in_specs=[
            scalar(),
            pl.BlockSpec((256, 1024), lambda i: (0, 0)),
            pl.BlockSpec((256, 1024), lambda i: (0, 0)),
            pl.BlockSpec((width, 1024), lambda i: (i, 0)),
            pl.BlockSpec((1, width), lambda i: (0, i)),
        ],
        out_specs=(
            pl.BlockSpec((512, width), lambda i: (0, i)),
            pl.BlockSpec((32, 4, 128), lambda i: (0, 0, 0)),
        ),
        scratch_shapes=[VMEM((512, 1024), BF), VMEM((512, 128), F32), VMEM((512, 128), F32)],
        compiler_params=params(),
        cost_estimate=pl.CostEstimate(
            flops=2 * 512 * 2048 * 1024, bytes_accessed=9 << 20, transcendentals=1 << 20
        ),
    )(at, own, other, still(scaled), bias_row)


def joined(shares):
    top = jnp.max(shares, axis=0)
    return top + jnp.log(jnp.sum(jnp.exp(shares - top[None]), axis=0))


def hold_kernel(*refs):
    del refs


def hold(value, *first):
    return pl.pallas_call(
        hold_kernel,
        out_shape=pltpu.HBM(value.shape, value.dtype),
        in_specs=hbm() + anywhere(len(first)),
        out_specs=pl.BlockSpec(memory_space=pltpu.HBM),
        input_output_aliases={0: 0},
        compiler_params=params(),
    )(value, *first)


def sums_kernel(at, shares, scaled, bias, *refs):
    pieces = refs[:8]
    sums = refs[9]
    rows, weights, lse, wide, sems = refs[10:]
    copies = [
        pltpu.make_async_copy(piece, rows.at[pl.ds(i * 256, 256)], sems.at[i])
        for i, piece in enumerate(pieces)
    ]
    for copy in copies:
        copy.start()
    y, c = at[2], at[1]
    for yy in range(4):
        lse[pl.ds(yy * 4, 4), :] = joined(shares[yy])
    for b in range(0, 512, 128):
        wide[b : b + 128, :] = jnp.transpose(jnp.broadcast_to(bias[:, b : b + 128], (128, 128)))
    shift_up = jnp.concatenate([wide[...], wide[...]], axis=1)
    count = jnp.zeros((512, 128), F32)
    for i in range(8):
        there = lax.rem(y + (0, 3, 1, 2)[i // 2], 4)
        core = c if i % 2 == 0 else 1 - c
        at_row = there * 4 + core * 2
        norm = jnp.concatenate([lse[pl.ds(at_row, 1), :], lse[pl.ds(at_row + 1, 1), :]], axis=1)
        cut = slice(i * 256, i * 256 + 256)
        copies[i].wait()
        score = lax.dot_general(
            scaled[...], rows[cut, :], (((1,), (1,)), ((), ())), preferred_element_type=F32
        )
        weight = jnp.exp(score + shift_up - norm).astype(BF)
        weights[:, cut] = weight
        count = count + weight[:, :128].astype(F32) + weight[:, 128:].astype(F32)
    count = jnp.sum(count, axis=1, keepdims=True)
    lines = jnp.concatenate([line(count[b : b + 128]) for b in range(0, 512, 128)], axis=0)
    high = lines.astype(BF).astype(F32)
    tail = jnp.concatenate([high, lines - high], axis=0).astype(BF)
    sums[:, 128:136, :] = jnp.broadcast_to(tail[None], (32, 8, 128))
    for j in range(4):
        block = lax.dot_general(
            weights[...],
            rows[:, j * 256 : j * 256 + 256],
            (((1,), (0,)), ((), ())),
            preferred_element_type=F32,
        )
        block = jnp.transpose(block.astype(BF))
        for q in range(4):
            part = block[:, q * 128 : q * 128 + 128].reshape(8, 32, 128)
            sums[j * 8 : j * 8 + 8, q * 32 : q * 32 + 32, :] = part


def partial_sums(at, shares, scaled, bias_row, pieces, first):
    return pl.pallas_call(
        sums_kernel,
        grid_spec=pltpu.PrefetchScalarGridSpec(
            num_scalar_prefetch=1,
            grid=(1,),
            in_specs=[
                pl.BlockSpec((4, 8, 4, 128), lambda i, at: (0, 0, 0, 0)),
                pl.BlockSpec((512, 1024), lambda i, at: (at[2], 0)),
                pl.BlockSpec((1, 512), lambda i, at: (0, at[2])),
            ]
            + anywhere(9),
            out_specs=pl.BlockSpec((32, 136, 128), lambda i, at: (0, 0, 0)),
            scratch_shapes=[
                VMEM((2048, 1024), BF),
                VMEM((512, 2048), BF),
                VMEM((16, 128), F32),
                VMEM((512, 128), F32),
                pltpu.SemaphoreType.DMA((8,)),
            ],
        ),
        out_shape=pltpu.HBM((32, 136, 128), BF),
        compiler_params=params(),
        cost_estimate=pl.CostEstimate(
            flops=4 * 512 * 2048 * 1024, bytes_accessed=8 << 20, transcendentals=1 << 20
        ),
    )(at, shares, still(scaled), bias_row, *pieces, first)


def resp_kernel(at, shares, score, *refs):
    outs, norm, held, sems, across = refs[:5], refs[5], refs[6], refs[7], refs[8]
    outs, out_across = (*outs[:3], across, outs[4]), outs[3]
    x, c, y = at[0], at[1], at[2]
    copies = []
    for j in range(8):
        core = 1 - c if j < 4 else c
        start = pl.multiple_of(core * 256 + lax.rem(x + j % 4, 4) * 64, 64)
        copies.append(
            (start, pltpu.make_async_copy(score.at[pl.ds(start, 64)], held.at[j], sems.at[j]))
        )
    for _, copy in copies:
        copy.start()
    lse = joined(shares[y])
    for b in range(4):
        norm[b * 128 : b * 128 + 128, :] = jnp.transpose(
            jnp.broadcast_to(lse[b : b + 1, :], (128, 128))
        )
    for j, (start, copy) in enumerate(copies):
        copy.wait()
        block = jnp.exp(held[j] - norm[pl.ds(start, 64), 0:1]).astype(BF)
        if j % 4 == 0:
            outs[j // 4][...] = block
        else:
            outs[1 + j % 4][j // 4 * 64 : j // 4 * 64 + 64, :] = block
    copy = pltpu.make_async_copy(across, out_across, sems.at[0])
    copy.start()
    copy.wait()


def responsibilities(at, shares, score):
    return pl.pallas_call(
        resp_kernel,
        in_specs=[scalar(), whole()] + hbm(),
        out_specs=[whole()] * 3 + hbm() + [whole()],
        scratch_shapes=[
            VMEM((512, 128), F32),
            VMEM((8, 64, 2048), F32),
            pltpu.SemaphoreType.DMA((8,)),
            VMEM((128, 2048), BF),
        ],
        out_shape=[jax.ShapeDtypeStruct((64, 2048), BF)] * 2
        + [jax.ShapeDtypeStruct((128, 2048), BF), pltpu.HBM((128, 2048), BF), jax.ShapeDtypeStruct((128, 2048), BF)],
        compiler_params=params(),
        cost_estimate=pl.CostEstimate(flops=1 << 21, bytes_accessed=6 << 20, transcendentals=1 << 20),
    )(at, shares, still(score))


def cut_kernel(at, means, ahead, out, turned):
    del ahead
    for i in range(0, 2048, 128):
        turned[:, i : i + 128] = jnp.transpose(means[i : i + 128, :].astype(F32))
    out[...] = turned[pl.ds(pl.multiple_of(lax.rem(at[3], 4) * 32, 32), 32), :]


def mean_columns(at, means, ahead):
    return pl.pallas_call(
        cut_kernel,
        grid_spec=pltpu.PrefetchScalarGridSpec(
            num_scalar_prefetch=1,
            grid=(1,),
            in_specs=[pl.BlockSpec((2048, 128), lambda i, at: (0, at[3] // 4))] + anywhere(),
            out_specs=pl.BlockSpec((32, 2048), lambda i, at: (0, 0)),
            scratch_shapes=[VMEM((128, 2048), F32)],
        ),
        out_shape=pltpu.HBM((32, 2048), F32),
        compiler_params=params(),
    )(at, still(means), ahead)


def finish_kernel(sent, means, new, counts):
    for y in range(4):
        total = sent[y * 8, :, :].astype(F32)
        for z in range(1, 8):
            total = total + sent[y * 8 + z, :, :].astype(F32)
        count = total[128:132, :] + total[132:136, :]
        counts[y * 4 : y * 4 + 4, :] = count
        for q in range(4):
            cut = slice(y * 512 + q * 128, y * 512 + q * 128 + 128)
            part = total[q * 32 : q * 32 + 32, :] + means[:, cut]
            new[:, cut] = part / (count[q : q + 1, :] + 1.0)


def finish(sent, mean_cols):
    return pl.pallas_call(
        finish_kernel,
        grid=(1,),
        in_specs=[
            pl.BlockSpec((32, 136, 128), lambda i: (0, 0, 0)),
            pl.BlockSpec((32, 2048), lambda i: (0, 0)),
        ],
        out_specs=[
            pl.BlockSpec((32, 2048), lambda i: (0, 0)),
            pl.BlockSpec((16, 128), lambda i: (0, 0)),
        ],
        out_shape=[
            jax.ShapeDtypeStruct((32, 2048), F32),
            jax.ShapeDtypeStruct((16, 128), F32),
        ],
        compiler_params=params(),
    )(sent, still(mean_cols))


def lay_kernel(at, *refs):
    pieces, out, sems = refs[:8], refs[8], refs[9]
    x, c = at[0], at[1]
    copies = []
    for j in range(8):
        core = 1 - c if j < 4 else c
        comp = lax.rem(x + 4 - j % 4, 4) * 2 + core
        spot = out.at[:, pl.ds(pl.multiple_of(comp * 2048, 2048), 2048)]
        piece = pieces[j].at[pl.ds(64, 64)] if j > 4 else pieces[j]
        copies.append(pltpu.make_async_copy(piece, spot, sems.at[j]))
    for copy in copies:
        copy.start()
    for copy in copies:
        copy.wait()


def lay_out(at, pieces):
    return pl.pallas_call(
        lay_kernel,
        in_specs=[scalar()] + anywhere(8),
        out_specs=pl.BlockSpec(memory_space=pl.ANY),
        scratch_shapes=[pltpu.SemaphoreType.DMA((8,))],
        out_shape=jax.ShapeDtypeStruct((64, 16384), BF),
        compiler_params=params(),
        cost_estimate=pl.CostEstimate(flops=0, bytes_accessed=4 << 20, transcendentals=0),
    )(at, *pieces)


def body(points, means, log_weights, inv_var):
    x, c, y, h, l = (lax.axis_index(a) for a in "xcyhl")
    at = jnp.stack([x, c, y, y * 8 + h * 2 + l, l]).astype(jnp.int32)

    far = shift(points, "y", 2)
    scaled, bias_row = prepare(means, inv_var, log_weights)

    own = gather_x(at, points, (scaled,), (far,))
    other = shift(own, "c", 1)
    before = shift(own, "y", 1)
    after = shift(own, "y", -1)
    score, share = scores(at, own, other, scaled, bias_row)

    shares = lax.all_to_all(share, ("y", "x", "c"), split_axis=0, concat_axis=0, tiled=True)
    mean_cols = mean_columns(at, means, share)
    far = gather_x(at, far, (mean_cols,), (shares,))
    shares = shares.reshape(4, 8, 4, 128)
    pieces = [own, other]
    for mine in (before, after, far):
        pieces += [mine, shift(mine, "c", 1)]

    blocks = responsibilities(at, shares, score)
    ahead, behind = shift(blocks[2], "x", 1), shift(blocks[4], "x", 3)
    sums = partial_sums(at, shares, scaled, bias_row, pieces, blocks[0])
    sums = hold(sums, ahead, behind)
    pairs = [ahead, shift(hold(blocks[3], still(sums)), "x", 2), behind]
    sent = lax.all_to_all(sums, ("y", "h", "l"), split_axis=0, concat_axis=0, tiled=True)
    theirs = [shift(b, "c", 1) for b in [blocks[0]] + [pair[:64] for pair in pairs]]
    held = theirs + [blocks[1]] + pairs
    resp_rows = lay_out(at, held)

    new_means_t, counts = finish(sent, mean_cols)
    counts = counts.reshape(2048)

    lse = joined(lax.dynamic_index_in_dim(shares, y, 0, keepdims=False)).reshape(8, 64)
    own_lse = lax.dynamic_index_in_dim(lse, c * 4 + x, 0, keepdims=False)
    points_f = points.astype(F32)
    const_term = 0.5 * jnp.sum(jnp.log(inv_var)) - 0.5 * 1024 * math.log(2.0 * math.pi)
    loglik = own_lse - 0.5 * jnp.sum(points_f * points_f * inv_var[None, :], axis=1) + const_term
    return (resp_rows, counts, new_means_t, loglik)


def solution(mesh):
    axes = ("y", "h", "l", "x", "c")
    mesh = Mesh(mesh.devices.reshape(4, 4, 2, 4, 2), axes)
    comp, pt = ("x", "c"), ("y", "h", "l")
    return jax.shard_map(
        body,
        mesh=mesh,
        in_specs=(P(axes, None), P(comp, None), P(comp), P()),
        out_specs=(P(axes, None), P(comp), P(pt, comp), P(axes)),
        check_vma=False,
    )
```

```python
import functools
import math

import jax
import jax.numpy as jnp
from jax import lax
from jax.experimental import pallas as pl
from jax.experimental.pallas import tpu as pltpu
from jax.sharding import Mesh
from jax.sharding import PartitionSpec as P

BF = jnp.bfloat16
F32 = jnp.float32
VMEM_LIMIT = 24 * 1024 * 1024
VMEM = pltpu.VMEM
SIZES = {"y": 4, "x": 4, "c": 2}


def shift(value, axis, step):
    n = SIZES[axis]
    return lax.ppermute(value, axis, [(i, (i + step) % n) for i in range(n)])


def still(value):
    return pltpu.with_memory_space_constraint(value, pltpu.HBM)


def params():
    return pltpu.CompilerParams(vmem_limit_bytes=VMEM_LIMIT)


def whole():
    return pl.BlockSpec(memory_space=VMEM)


def scalar():
    return pl.BlockSpec(memory_space=pltpu.SMEM)


def anywhere(n=1):
    return [pl.BlockSpec(memory_space=pl.ANY)] * n


def hbm(n=1):
    return [pl.BlockSpec(memory_space=pltpu.HBM)] * n


def prepare_kernel(means, inv_var, weights, scaled, row):
    values = means[...].astype(F32)
    product = values * inv_var[...]
    scaled[...] = product.astype(BF)
    square = values * product
    norm = functools.reduce(jnp.add, [square[:, i : i + 128] for i in range(0, 1024, 128)])
    norm = 0.5 * jnp.sum(norm, axis=1, keepdims=True)
    for i in range(0, 512, 128):
        row[:, i : i + 128] = weights[:, i : i + 128] - line(norm[i : i + 128])


def prepare(means, inv_var, log_weights):
    return pl.pallas_call(
        prepare_kernel,
        grid=(4,),
        in_specs=[
            pl.BlockSpec((512, 1024), lambda i: (i, 0)),
            pl.BlockSpec((1, 1024), lambda i: (0, 0)),
            pl.BlockSpec((1, 512), lambda i: (0, i)),
        ],
        out_specs=(
            pl.BlockSpec((512, 1024), lambda i: (i, 0)),
            pl.BlockSpec((1, 512), lambda i: (0, i)),
        ),
        out_shape=(
            pltpu.HBM((2048, 1024), BF),
            jax.ShapeDtypeStruct((1, 2048), F32),
        ),
        compiler_params=params(),
        cost_estimate=pl.CostEstimate(flops=6 << 21, bytes_accessed=8 << 20, transcendentals=0),
    )(still(means), still(inv_var.reshape(1, 1024)), still(log_weights.reshape(1, 2048)))


def place_kernel(at, own, before, after, far, *refs):
    out = refs[-1]
    x = at[0]
    for step, piece in ((0, own), (3, before), (1, after), (2, far)):
        slot = lax.rem(x + step, 4)
        out[pl.ds(pl.multiple_of(slot * 64, 64), 64), :] = piece[...]


def gather_x(at, own, ahead, there=()):
    parts = (own, shift(own, "x", 1), shift(own, "x", -1), shift(own, "x", 2))
    return pl.pallas_call(
        place_kernel,
        out_shape=jax.ShapeDtypeStruct((256, 1024), BF),
        in_specs=[scalar()] + [whole()] * 4 + hbm(len(ahead)) + anywhere(len(there)),
        out_specs=whole(),
        compiler_params=params(),
    )(at, *parts, *(still(a) for a in ahead), *there)


def column(row):
    return jnp.transpose(jnp.broadcast_to(row, (128, 128)))[:, 0:1]


def line(col):
    return jnp.transpose(jnp.broadcast_to(col, (128, 128)))[0:1, :]


def score_kernel(at, own, other, scaled, bias, score, share, rows, peak, total):
    step = pl.program_id(0)
    c = at[1]

    @pl.when(step == 0)
    def _():
        rows[pl.ds(pl.multiple_of(c * 256, 256), 256), :] = own[...]
        rows[pl.ds(pl.multiple_of((1 - c) * 256, 256), 256), :] = other[...]
        peak[...] = jnp.full_like(peak, -jnp.inf)
        total[...] = jnp.zeros_like(total)

    for r in range(2):
        cut = slice(r * 256, r * 256 + 256)
        tile = lax.dot_general(
            rows[cut, :], scaled[...], (((1,), (1,)), ((), ())), preferred_element_type=F32
        )
        tile = tile + bias[...]
        score[cut, :] = tile
        lanes = [tile[:, i : i + 128] for i in range(0, tile.shape[1], 128)]
        old = peak[cut, :]
        top = functools.reduce(jnp.maximum, lanes, old)
        added = functools.reduce(jnp.add, [jnp.exp(lane - top) for lane in lanes])
        total[cut, :] = total[cut, :] * jnp.exp(old - top) + added
        peak[cut, :] = top

    @pl.when(step == pl.num_programs(0) - 1)
    def _():
        for b in range(4):
            cut = slice(b * 128, b * 128 + 128)
            top = jnp.max(peak[cut, :], axis=1, keepdims=True)
            mass = jnp.sum(total[cut, :] * jnp.exp(peak[cut, :] - top), axis=1, keepdims=True)
            share[:, b, :] = jnp.broadcast_to(line(top + jnp.log(mass)), (32, 128))


def scores(at, own, other, scaled, bias_row):
    width = 512
    return pl.pallas_call(
        score_kernel,
        grid=(2048 // width,),
        out_shape=(
            pltpu.HBM((512, 2048), F32),
            jax.ShapeDtypeStruct((32, 4, 128), F32),
        ),
        in_specs=[
            scalar(),
            pl.BlockSpec((256, 1024), lambda i: (0, 0)),
            pl.BlockSpec((256, 1024), lambda i: (0, 0)),
            pl.BlockSpec((width, 1024), lambda i: (i, 0)),
            pl.BlockSpec((1, width), lambda i: (0, i)),
        ],
        out_specs=(
            pl.BlockSpec((512, width), lambda i: (0, i)),
            pl.BlockSpec((32, 4, 128), lambda i: (0, 0, 0)),
        ),
        scratch_shapes=[VMEM((512, 1024), BF), VMEM((512, 128), F32), VMEM((512, 128), F32)],
        compiler_params=params(),
        cost_estimate=pl.CostEstimate(
            flops=2 * 512 * 2048 * 1024, bytes_accessed=9 << 20, transcendentals=1 << 20
        ),
    )(at, own, other, still(scaled), bias_row)


def joined(shares):
    top = jnp.max(shares, axis=0)
    return top + jnp.log(jnp.sum(jnp.exp(shares - top[None]), axis=0))


def hold_kernel(*refs):
    del refs


def hold(value, *first):
    return pl.pallas_call(
        hold_kernel,
        out_shape=pltpu.HBM(value.shape, value.dtype),
        in_specs=hbm() + anywhere(len(first)),
        out_specs=pl.BlockSpec(memory_space=pltpu.HBM),
        input_output_aliases={0: 0},
        compiler_params=params(),
    )(value, *first)


def sums_kernel(at, shares, scaled, bias, *refs):
    pieces = refs[:8]
    sums = refs[9]
    rows, weights, lse, wide, sems = refs[10:]
    copies = [
        pltpu.make_async_copy(piece, rows.at[pl.ds(i * 256, 256)], sems.at[i])
        for i, piece in enumerate(pieces)
    ]
    for copy in copies:
        copy.start()
    y, c = at[2], at[1]
    for yy in range(4):
        lse[pl.ds(yy * 4, 4), :] = joined(shares[yy])
    for b in range(0, 512, 128):
        wide[b : b + 128, :] = jnp.transpose(jnp.broadcast_to(bias[:, b : b + 128], (128, 128)))
    shift_up = jnp.concatenate([wide[...], wide[...]], axis=1)
    count = jnp.zeros((512, 128), F32)
    for i in range(8):
        there = lax.rem(y + (0, 3, 1, 2)[i // 2], 4)
        core = c if i % 2 == 0 else 1 - c
        at_row = there * 4 + core * 2
        norm = jnp.concatenate([lse[pl.ds(at_row, 1), :], lse[pl.ds(at_row + 1, 1), :]], axis=1)
        cut = slice(i * 256, i * 256 + 256)
        copies[i].wait()
        score = lax.dot_general(
            scaled[...], rows[cut, :], (((1,), (1,)), ((), ())), preferred_element_type=F32
        )
        weight = jnp.exp(score + shift_up - norm).astype(BF)
        weights[:, cut] = weight
        count = count + weight[:, :128].astype(F32) + weight[:, 128:].astype(F32)
    count = jnp.sum(count, axis=1, keepdims=True)
    lines = jnp.concatenate([line(count[b : b + 128]) for b in range(0, 512, 128)], axis=0)
    high = lines.astype(BF).astype(F32)
    tail = jnp.concatenate([high, lines - high], axis=0).astype(BF)
    sums[:, 128:136, :] = jnp.broadcast_to(tail[None], (32, 8, 128))
    for j in range(4):
        block = lax.dot_general(
            weights[...],
            rows[:, j * 256 : j * 256 + 256],
            (((1,), (0,)), ((), ())),
            preferred_element_type=F32,
        )
        block = jnp.transpose(block.astype(BF))
        for q in range(4):
            part = block[:, q * 128 : q * 128 + 128].reshape(8, 32, 128)
            sums[j * 8 : j * 8 + 8, q * 32 : q * 32 + 32, :] = part


def partial_sums(at, shares, scaled, bias_row, pieces, first):
    return pl.pallas_call(
        sums_kernel,
        grid_spec=pltpu.PrefetchScalarGridSpec(
            num_scalar_prefetch=1,
            grid=(1,),
            in_specs=[
                pl.BlockSpec((4, 8, 4, 128), lambda i, at: (0, 0, 0, 0)),
                pl.BlockSpec((512, 1024), lambda i, at: (at[2], 0)),
                pl.BlockSpec((1, 512), lambda i, at: (0, at[2])),
            ]
            + anywhere(9),
            out_specs=pl.BlockSpec((32, 136, 128), lambda i, at: (0, 0, 0)),
            scratch_shapes=[
                VMEM((2048, 1024), BF),
                VMEM((512, 2048), BF),
                VMEM((16, 128), F32),
                VMEM((512, 128), F32),
                pltpu.SemaphoreType.DMA((8,)),
            ],
        ),
        out_shape=pltpu.HBM((32, 136, 128), BF),
        compiler_params=params(),
        cost_estimate=pl.CostEstimate(
            flops=4 * 512 * 2048 * 1024, bytes_accessed=8 << 20, transcendentals=1 << 20
        ),
    )(at, shares, still(scaled), bias_row, *pieces, first)


def resp_kernel(at, shares, score, *refs):
    outs, norm, held, sems, across = refs[:5], refs[5], refs[6], refs[7], refs[8]
    outs, out_across = (*outs[:3], across, outs[4]), outs[3]
    x, c, y = at[0], at[1], at[2]
    copies = []
    for j in range(8):
        core = 1 - c if j < 4 else c
        start = pl.multiple_of(core * 256 + lax.rem(x + j % 4, 4) * 64, 64)
        copies.append(
            (start, pltpu.make_async_copy(score.at[pl.ds(start, 64)], held.at[j], sems.at[j]))
        )
    for _, copy in copies:
        copy.start()
    lse = joined(shares[y])
    for b in range(4):
        norm[b * 128 : b * 128 + 128, :] = jnp.transpose(
            jnp.broadcast_to(lse[b : b + 1, :], (128, 128))
        )
    for j, (start, copy) in enumerate(copies):
        copy.wait()
        block = jnp.exp(held[j] - norm[pl.ds(start, 64), 0:1]).astype(BF)
        if j % 4 == 0:
            outs[j // 4][...] = block
        else:
            outs[1 + j % 4][j // 4 * 64 : j // 4 * 64 + 64, :] = block
    copy = pltpu.make_async_copy(across, out_across, sems.at[0])
    copy.start()
    copy.wait()


def responsibilities(at, shares, score):
    return pl.pallas_call(
        resp_kernel,
        in_specs=[scalar(), whole()] + hbm(),
        out_specs=[whole()] * 3 + hbm() + [whole()],
        scratch_shapes=[
            VMEM((512, 128), F32),
            VMEM((8, 64, 2048), F32),
            pltpu.SemaphoreType.DMA((8,)),
            VMEM((128, 2048), BF),
        ],
        out_shape=[jax.ShapeDtypeStruct((64, 2048), BF)] * 2
        + [jax.ShapeDtypeStruct((128, 2048), BF), pltpu.HBM((128, 2048), BF), jax.ShapeDtypeStruct((128, 2048), BF)],
        compiler_params=params(),
        cost_estimate=pl.CostEstimate(flops=1 << 21, bytes_accessed=6 << 20, transcendentals=1 << 20),
    )(at, shares, still(score))


def cut_kernel(at, means, ahead, out, turned):
    del ahead
    for i in range(0, 2048, 128):
        turned[:, i : i + 128] = jnp.transpose(means[i : i + 128, :].astype(F32))
    out[...] = turned[pl.ds(pl.multiple_of(lax.rem(at[3], 4) * 32, 32), 32), :]


def mean_columns(at, means, ahead):
    return pl.pallas_call(
        cut_kernel,
        grid_spec=pltpu.PrefetchScalarGridSpec(
            num_scalar_prefetch=1,
            grid=(1,),
            in_specs=[pl.BlockSpec((2048, 128), lambda i, at: (0, at[3] // 4))] + anywhere(),
            out_specs=pl.BlockSpec((32, 2048), lambda i, at: (0, 0)),
            scratch_shapes=[VMEM((128, 2048), F32)],
        ),
        out_shape=pltpu.HBM((32, 2048), F32),
        compiler_params=params(),
    )(at, still(means), ahead)


def finish_kernel(sent, means, new, counts):
    for y in range(4):
        total = sent[y * 8, :, :].astype(F32)
        for z in range(1, 8):
            total = total + sent[y * 8 + z, :, :].astype(F32)
        count = total[128:132, :] + total[132:136, :]
        counts[y * 4 : y * 4 + 4, :] = count
        for q in range(4):
            cut = slice(y * 512 + q * 128, y * 512 + q * 128 + 128)
            part = total[q * 32 : q * 32 + 32, :] + means[:, cut]
            new[:, cut] = part / (count[q : q + 1, :] + 1.0)


def finish(sent, mean_cols):
    return pl.pallas_call(
        finish_kernel,
        grid=(1,),
        in_specs=[
            pl.BlockSpec((32, 136, 128), lambda i: (0, 0, 0)),
            pl.BlockSpec((32, 2048), lambda i: (0, 0)),
        ],
        out_specs=[
            pl.BlockSpec((32, 2048), lambda i: (0, 0)),
            pl.BlockSpec((16, 128), lambda i: (0, 0)),
        ],
        out_shape=[
            jax.ShapeDtypeStruct((32, 2048), F32),
            jax.ShapeDtypeStruct((16, 128), F32),
        ],
        compiler_params=params(),
    )(sent, still(mean_cols))


def lay_kernel(at, *refs):
    pieces, out, sems = refs[:8], refs[8], refs[9]
    x, c = at[0], at[1]
    copies = []
    for j in range(8):
        core = 1 - c if j < 4 else c
        comp = lax.rem(x + 4 - j % 4, 4) * 2 + core
        spot = out.at[:, pl.ds(pl.multiple_of(comp * 2048, 2048), 2048)]
        piece = pieces[j].at[pl.ds(64, 64)] if j > 4 else pieces[j]
        copies.append(pltpu.make_async_copy(piece, spot, sems.at[j]))
    for copy in copies:
        copy.start()
    for copy in copies:
        copy.wait()


def lay_out(at, pieces):
    return pl.pallas_call(
        lay_kernel,
        in_specs=[scalar()] + [whole()] * 8,
        out_specs=pl.BlockSpec(memory_space=pl.ANY),
        scratch_shapes=[pltpu.SemaphoreType.DMA((8,))],
        out_shape=jax.ShapeDtypeStruct((64, 16384), BF),
        compiler_params=params(),
        cost_estimate=pl.CostEstimate(flops=0, bytes_accessed=4 << 20, transcendentals=0),
    )(at, *pieces)


def body(points, means, log_weights, inv_var):
    x, c, y, h, l = (lax.axis_index(a) for a in "xcyhl")
    at = jnp.stack([x, c, y, y * 8 + h * 2 + l, l]).astype(jnp.int32)

    far = shift(points, "y", 2)
    scaled, bias_row = prepare(means, inv_var, log_weights)

    own = gather_x(at, points, (scaled,), (far,))
    other = shift(own, "c", 1)
    before = shift(own, "y", 1)
    after = shift(own, "y", -1)
    score, share = scores(at, own, other, scaled, bias_row)

    shares = lax.all_to_all(share, ("y", "x", "c"), split_axis=0, concat_axis=0, tiled=True)
    mean_cols = mean_columns(at, means, share)
    far = gather_x(at, far, (mean_cols,), (shares,))
    shares = shares.reshape(4, 8, 4, 128)
    pieces = [own, other]
    for mine in (before, after, far):
        pieces += [mine, shift(mine, "c", 1)]

    blocks = responsibilities(at, shares, score)
    ahead, behind = shift(blocks[2], "x", 1), shift(blocks[4], "x", 3)
    sums = partial_sums(at, shares, scaled, bias_row, pieces, blocks[0])
    sums = hold(sums, ahead, behind)
    pairs = [ahead, shift(hold(blocks[3], still(sums)), "x", 2), behind]
    sent = lax.all_to_all(sums, ("y", "h", "l"), split_axis=0, concat_axis=0, tiled=True)
    theirs = [shift(b, "c", 1) for b in [blocks[0]] + [pair[:64] for pair in pairs]]
    held = theirs + [blocks[1]] + pairs
    resp_rows = lay_out(at, held)

    new_means_t, counts = finish(sent, mean_cols)
    counts = counts.reshape(2048)

    lse = joined(lax.dynamic_index_in_dim(shares, y, 0, keepdims=False)).reshape(8, 64)
    own_lse = lax.dynamic_index_in_dim(lse, c * 4 + x, 0, keepdims=False)
    points_f = points.astype(F32)
    const_term = 0.5 * jnp.sum(jnp.log(inv_var)) - 0.5 * 1024 * math.log(2.0 * math.pi)
    loglik = own_lse - 0.5 * jnp.sum(points_f * points_f * inv_var[None, :], axis=1) + const_term
    return (resp_rows, counts, new_means_t, loglik)


def solution(mesh):
    axes = ("y", "h", "l", "x", "c")
    mesh = Mesh(mesh.devices.reshape(4, 4, 2, 4, 2), axes)
    comp, pt = ("x", "c"), ("y", "h", "l")
    return jax.shard_map(
        body,
        mesh=mesh,
        in_specs=(P(axes, None), P(comp, None), P(comp), P()),
        out_specs=(P(axes, None), P(comp), P(pt, comp), P(axes)),
        check_vma=False,
    )
```

```python
import functools
import math

import jax
import jax.numpy as jnp
from jax import lax
from jax.experimental import pallas as pl
from jax.experimental.pallas import tpu as pltpu
from jax.sharding import Mesh
from jax.sharding import PartitionSpec as P

BF = jnp.bfloat16
F32 = jnp.float32
VMEM_LIMIT = 24 * 1024 * 1024
VMEM = pltpu.VMEM
SIZES = {"y": 4, "x": 4, "c": 2}


def shift(value, axis, step):
    n = SIZES[axis]
    return lax.ppermute(value, axis, [(i, (i + step) % n) for i in range(n)])


def still(value):
    return pltpu.with_memory_space_constraint(value, pltpu.HBM)


def params():
    return pltpu.CompilerParams(vmem_limit_bytes=VMEM_LIMIT)


def whole():
    return pl.BlockSpec(memory_space=VMEM)


def scalar():
    return pl.BlockSpec(memory_space=pltpu.SMEM)


def anywhere(n=1):
    return [pl.BlockSpec(memory_space=pl.ANY)] * n


def hbm(n=1):
    return [pl.BlockSpec(memory_space=pltpu.HBM)] * n


def prepare_kernel(means, inv_var, weights, scaled, row):
    values = means[...].astype(F32)
    product = values * inv_var[...]
    scaled[...] = product.astype(BF)
    square = values * product
    norm = functools.reduce(jnp.add, [square[:, i : i + 128] for i in range(0, 1024, 128)])
    norm = 0.5 * jnp.sum(norm, axis=1, keepdims=True)
    for i in range(0, 512, 128):
        row[:, i : i + 128] = weights[:, i : i + 128] - line(norm[i : i + 128])


def prepare(means, inv_var, log_weights):
    return pl.pallas_call(
        prepare_kernel,
        grid=(4,),
        in_specs=[
            pl.BlockSpec((512, 1024), lambda i: (i, 0)),
            pl.BlockSpec((1, 1024), lambda i: (0, 0)),
            pl.BlockSpec((1, 512), lambda i: (0, i)),
        ],
        out_specs=(
            pl.BlockSpec((512, 1024), lambda i: (i, 0)),
            pl.BlockSpec((1, 512), lambda i: (0, i)),
        ),
        out_shape=(
            pltpu.HBM((2048, 1024), BF),
            jax.ShapeDtypeStruct((1, 2048), F32),
        ),
        compiler_params=params(),
        cost_estimate=pl.CostEstimate(flops=6 << 21, bytes_accessed=8 << 20, transcendentals=0),
    )(still(means), still(inv_var.reshape(1, 1024)), still(log_weights.reshape(1, 2048)))


def place_kernel(at, own, before, after, far, *refs):
    out = refs[-1]
    x = at[0]
    for step, piece in ((0, own), (3, before), (1, after), (2, far)):
        slot = lax.rem(x + step, 4)
        out[pl.ds(pl.multiple_of(slot * 64, 64), 64), :] = piece[...]


def gather_x(at, own, ahead, there=()):
    parts = (own, shift(own, "x", 1), shift(own, "x", -1), shift(own, "x", 2))
    return pl.pallas_call(
        place_kernel,
        out_shape=jax.ShapeDtypeStruct((256, 1024), BF),
        in_specs=[scalar()] + [whole()] * 4 + hbm(len(ahead)) + anywhere(len(there)),
        out_specs=whole(),
        compiler_params=params(),
    )(at, *parts, *(still(a) for a in ahead), *there)


def column(row):
    return jnp.transpose(jnp.broadcast_to(row, (128, 128)))[:, 0:1]


def line(col):
    return jnp.transpose(jnp.broadcast_to(col, (128, 128)))[0:1, :]


def score_kernel(at, own, other, scaled, bias, score, share, rows, peak, total):
    step = pl.program_id(0)
    c = at[1]

    @pl.when(step == 0)
    def _():
        rows[pl.ds(pl.multiple_of(c * 256, 256), 256), :] = own[...]
        rows[pl.ds(pl.multiple_of((1 - c) * 256, 256), 256), :] = other[...]
        peak[...] = jnp.full_like(peak, -jnp.inf)
        total[...] = jnp.zeros_like(total)

    for r in range(2):
        cut = slice(r * 256, r * 256 + 256)
        tile = lax.dot_general(
            rows[cut, :], scaled[...], (((1,), (1,)), ((), ())), preferred_element_type=F32
        )
        tile = tile + bias[...]
        score[cut, :] = tile
        lanes = [tile[:, i : i + 128] for i in range(0, tile.shape[1], 128)]
        old = peak[cut, :]
        top = functools.reduce(jnp.maximum, lanes, old)
        added = functools.reduce(jnp.add, [jnp.exp(lane - top) for lane in lanes])
        total[cut, :] = total[cut, :] * jnp.exp(old - top) + added
        peak[cut, :] = top

    @pl.when(step == pl.num_programs(0) - 1)
    def _():
        for b in range(4):
            cut = slice(b * 128, b * 128 + 128)
            top = jnp.max(peak[cut, :], axis=1, keepdims=True)
            mass = jnp.sum(total[cut, :] * jnp.exp(peak[cut, :] - top), axis=1, keepdims=True)
            share[:, b, :] = jnp.broadcast_to(line(top + jnp.log(mass)), (32, 128))


def scores(at, own, other, scaled, bias_row):
    width = 512
    return pl.pallas_call(
        score_kernel,
        grid=(2048 // width,),
        out_shape=(
            pltpu.HBM((512, 2048), F32),
            jax.ShapeDtypeStruct((32, 4, 128), F32),
        ),
        in_specs=[
            scalar(),
            pl.BlockSpec((256, 1024), lambda i: (0, 0)),
            pl.BlockSpec((256, 1024), lambda i: (0, 0)),
            pl.BlockSpec((width, 1024), lambda i: (i, 0)),
            pl.BlockSpec((1, width), lambda i: (0, i)),
        ],
        out_specs=(
            pl.BlockSpec((512, width), lambda i: (0, i)),
            pl.BlockSpec((32, 4, 128), lambda i: (0, 0, 0)),
        ),
        scratch_shapes=[VMEM((512, 1024), BF), VMEM((512, 128), F32), VMEM((512, 128), F32)],
        compiler_params=params(),
        cost_estimate=pl.CostEstimate(
            flops=2 * 512 * 2048 * 1024, bytes_accessed=9 << 20, transcendentals=1 << 20
        ),
    )(at, own, other, still(scaled), bias_row)


def joined(shares):
    top = jnp.max(shares, axis=0)
    return top + jnp.log(jnp.sum(jnp.exp(shares - top[None]), axis=0))


def hold_kernel(*refs):
    del refs


def hold(value, *first):
    return pl.pallas_call(
        hold_kernel,
        out_shape=pltpu.HBM(value.shape, value.dtype),
        in_specs=hbm() + anywhere(len(first)),
        out_specs=pl.BlockSpec(memory_space=pltpu.HBM),
        input_output_aliases={0: 0},
        compiler_params=params(),
    )(value, *first)


def sums_kernel(at, shares, scaled, bias, *refs):
    pieces = refs[:8]
    sums = refs[9]
    rows, weights, lse, norms, sems = refs[10:]
    copies = [
        pltpu.make_async_copy(piece, rows.at[pl.ds(i * 256, 256)], sems.at[i])
        for i, piece in enumerate(pieces)
    ]
    for copy in copies:
        copy.start()
    y, c = at[2], at[1]
    for yy in range(4):
        lse[pl.ds(yy * 4, 4), :] = joined(shares[yy])
    parts = []
    for i in range(8):
        there = lax.rem(y + (0, 3, 1, 2)[i // 2], 4)
        core = c if i % 2 == 0 else 1 - c
        line_at = there * 4 + core * 2
        parts += [lse[pl.ds(line_at, 1), :], lse[pl.ds(line_at + 1, 1), :]]
    norms[...] = jnp.transpose(jnp.concatenate(parts + [jnp.zeros((112, 128), F32)], axis=0))
    count = jnp.zeros((8, 512), F32)
    for g in range(2):
        for copy in copies[g * 4 : g * 4 + 4]:
            copy.wait()
        score = lax.dot_general(
            rows[g * 1024 : g * 1024 + 1024, :],
            scaled[...],
            (((1,), (1,)), ((), ())),
            preferred_element_type=F32,
        )
        for q in range(8):
            j = g * 8 + q
            shifted = score[q * 128 : q * 128 + 128, :] + (bias[...] - norms[:, j : j + 1])
            weight = jnp.exp(shifted).astype(BF)
            weights[j * 128 : j * 128 + 128, :] = weight
            weight = weight.astype(F32)
            count = count + functools.reduce(
                jnp.add, [weight[t : t + 8, :] for t in range(0, 128, 8)]
            )
    count = jnp.sum(count, axis=0, keepdims=True)
    lines = jnp.concatenate([count[:, b : b + 128] for b in range(0, 512, 128)], axis=0)
    high = lines.astype(BF).astype(F32)
    tail = jnp.concatenate([high, lines - high], axis=0).astype(BF)
    sums[:, 128:136, :] = jnp.broadcast_to(tail[None], (32, 8, 128))
    block = lax.dot_general(
        rows[...], weights[...], (((0,), (0,)), ((), ())), preferred_element_type=F32
    ).astype(BF)
    for q in range(4):
        part = block[:, q * 128 : q * 128 + 128].reshape(32, 32, 128)
        sums[:, q * 32 : q * 32 + 32, :] = part


def partial_sums(at, shares, scaled, bias_row, pieces, first):
    return pl.pallas_call(
        sums_kernel,
        grid_spec=pltpu.PrefetchScalarGridSpec(
            num_scalar_prefetch=1,
            grid=(1,),
            in_specs=[
                pl.BlockSpec((4, 8, 4, 128), lambda i, at: (0, 0, 0, 0)),
                pl.BlockSpec((512, 1024), lambda i, at: (at[2], 0)),
                pl.BlockSpec((1, 512), lambda i, at: (0, at[2])),
            ]
            + anywhere(9),
            out_specs=pl.BlockSpec((32, 136, 128), lambda i, at: (0, 0, 0)),
            scratch_shapes=[
                VMEM((2048, 1024), BF),
                VMEM((2048, 512), BF),
                VMEM((16, 128), F32),
                VMEM((128, 128), F32),
                pltpu.SemaphoreType.DMA((8,)),
            ],
        ),
        out_shape=pltpu.HBM((32, 136, 128), BF),
        compiler_params=params(),
        cost_estimate=pl.CostEstimate(
            flops=4 * 512 * 2048 * 1024, bytes_accessed=8 << 20, transcendentals=1 << 20
        ),
    )(at, shares, still(scaled), bias_row, *pieces, first)


def resp_kernel(at, shares, score, *refs):
    outs, norm, held, sems, across = refs[:5], refs[5], refs[6], refs[7], refs[8]
    outs, out_across = (*outs[:3], across, outs[4]), outs[3]
    x, c, y = at[0], at[1], at[2]
    copies = []
    for j in range(8):
        core = 1 - c if j < 4 else c
        start = pl.multiple_of(core * 256 + lax.rem(x + j % 4, 4) * 64, 64)
        copies.append(
            (start, pltpu.make_async_copy(score.at[pl.ds(start, 64)], held.at[j], sems.at[j]))
        )
    for _, copy in copies:
        copy.start()
    lse = joined(shares[y])
    for b in range(4):
        norm[b * 128 : b * 128 + 128, :] = jnp.transpose(
            jnp.broadcast_to(lse[b : b + 1, :], (128, 128))
        )
    for j, (start, copy) in enumerate(copies):
        copy.wait()
        block = jnp.exp(held[j] - norm[pl.ds(start, 64), 0:1]).astype(BF)
        if j % 4 == 0:
            outs[j // 4][...] = block
        else:
            outs[1 + j % 4][j // 4 * 64 : j // 4 * 64 + 64, :] = block
    copy = pltpu.make_async_copy(across, out_across, sems.at[0])
    copy.start()
    copy.wait()


def responsibilities(at, shares, score):
    return pl.pallas_call(
        resp_kernel,
        in_specs=[scalar(), whole()] + hbm(),
        out_specs=[whole()] * 3 + hbm() + [whole()],
        scratch_shapes=[
            VMEM((512, 128), F32),
            VMEM((8, 64, 2048), F32),
            pltpu.SemaphoreType.DMA((8,)),
            VMEM((128, 2048), BF),
        ],
        out_shape=[jax.ShapeDtypeStruct((64, 2048), BF)] * 2
        + [jax.ShapeDtypeStruct((128, 2048), BF), pltpu.HBM((128, 2048), BF), jax.ShapeDtypeStruct((128, 2048), BF)],
        compiler_params=params(),
        cost_estimate=pl.CostEstimate(flops=1 << 21, bytes_accessed=6 << 20, transcendentals=1 << 20),
    )(at, shares, still(score))


def cut_kernel(at, means, ahead, out, turned):
    del ahead
    for i in range(0, 2048, 128):
        turned[:, i : i + 128] = jnp.transpose(means[i : i + 128, :].astype(F32))
    out[...] = turned[pl.ds(pl.multiple_of(lax.rem(at[3], 4) * 32, 32), 32), :]


def mean_columns(at, means, ahead):
    return pl.pallas_call(
        cut_kernel,
        grid_spec=pltpu.PrefetchScalarGridSpec(
            num_scalar_prefetch=1,
            grid=(1,),
            in_specs=[pl.BlockSpec((2048, 128), lambda i, at: (0, at[3] // 4))] + anywhere(),
            out_specs=pl.BlockSpec((32, 2048), lambda i, at: (0, 0)),
            scratch_shapes=[VMEM((128, 2048), F32)],
        ),
        out_shape=pltpu.HBM((32, 2048), F32),
        compiler_params=params(),
    )(at, still(means), ahead)


def finish_kernel(sent, means, new, counts):
    for y in range(4):
        total = sent[y * 8, :, :].astype(F32)
        for z in range(1, 8):
            total = total + sent[y * 8 + z, :, :].astype(F32)
        count = total[128:132, :] + total[132:136, :]
        counts[y * 4 : y * 4 + 4, :] = count
        for q in range(4):
            cut = slice(y * 512 + q * 128, y * 512 + q * 128 + 128)
            part = total[q * 32 : q * 32 + 32, :] + means[:, cut]
            new[:, cut] = part / (count[q : q + 1, :] + 1.0)


def finish(sent, mean_cols):
    return pl.pallas_call(
        finish_kernel,
        grid=(1,),
        in_specs=[
            pl.BlockSpec((32, 136, 128), lambda i: (0, 0, 0)),
            pl.BlockSpec((32, 2048), lambda i: (0, 0)),
        ],
        out_specs=[
            pl.BlockSpec((32, 2048), lambda i: (0, 0)),
            pl.BlockSpec((16, 128), lambda i: (0, 0)),
        ],
        out_shape=[
            jax.ShapeDtypeStruct((32, 2048), F32),
            jax.ShapeDtypeStruct((16, 128), F32),
        ],
        compiler_params=params(),
    )(sent, still(mean_cols))


def lay_kernel(at, *refs):
    pieces, out, sems = refs[:8], refs[8], refs[9]
    x, c = at[0], at[1]
    copies = []
    for j in range(8):
        core = 1 - c if j < 4 else c
        comp = lax.rem(x + 4 - j % 4, 4) * 2 + core
        spot = out.at[:, pl.ds(pl.multiple_of(comp * 2048, 2048), 2048)]
        piece = pieces[j].at[pl.ds(64, 64)] if j > 4 else pieces[j]
        copies.append(pltpu.make_async_copy(piece, spot, sems.at[j]))
    for copy in copies:
        copy.start()
    for copy in copies:
        copy.wait()


def lay_out(at, pieces):
    return pl.pallas_call(
        lay_kernel,
        in_specs=[scalar()] + [whole()] * 8,
        out_specs=pl.BlockSpec(memory_space=pl.ANY),
        scratch_shapes=[pltpu.SemaphoreType.DMA((8,))],
        out_shape=jax.ShapeDtypeStruct((64, 16384), BF),
        compiler_params=params(),
        cost_estimate=pl.CostEstimate(flops=0, bytes_accessed=4 << 20, transcendentals=0),
    )(at, *pieces)


def body(points, means, log_weights, inv_var):
    x, c, y, h, l = (lax.axis_index(a) for a in "xcyhl")
    at = jnp.stack([x, c, y, y * 8 + h * 2 + l, l]).astype(jnp.int32)

    far = shift(points, "y", 2)
    scaled, bias_row = prepare(means, inv_var, log_weights)

    own = gather_x(at, points, (scaled,), (far,))
    other = shift(own, "c", 1)
    before = shift(own, "y", 1)
    after = shift(own, "y", -1)
    score, share = scores(at, own, other, scaled, bias_row)

    shares = lax.all_to_all(share, ("y", "x", "c"), split_axis=0, concat_axis=0, tiled=True)
    mean_cols = mean_columns(at, means, share)
    far = gather_x(at, far, (mean_cols,), (shares,))
    shares = shares.reshape(4, 8, 4, 128)
    pieces = [own, other]
    for mine in (before, after, far):
        pieces += [mine, shift(mine, "c", 1)]

    blocks = responsibilities(at, shares, score)
    ahead, behind = shift(blocks[2], "x", 1), shift(blocks[4], "x", 3)
    sums = partial_sums(at, shares, scaled, bias_row, pieces, blocks[0])
    sums = hold(sums, ahead)
    pairs = [ahead, shift(hold(blocks[3], still(sums)), "x", 2), behind]
    sent = lax.all_to_all(sums, ("y", "h", "l"), split_axis=0, concat_axis=0, tiled=True)
    theirs = [shift(b, "c", 1) for b in [blocks[0]] + [pair[:64] for pair in pairs]]
    held = theirs + [blocks[1]] + pairs
    resp_rows = lay_out(at, held)

    new_means_t, counts = finish(sent, mean_cols)
    counts = counts.reshape(2048)

    lse = joined(lax.dynamic_index_in_dim(shares, y, 0, keepdims=False)).reshape(8, 64)
    own_lse = lax.dynamic_index_in_dim(lse, c * 4 + x, 0, keepdims=False)
    points_f = points.astype(F32)
    const_term = 0.5 * jnp.sum(jnp.log(inv_var)) - 0.5 * 1024 * math.log(2.0 * math.pi)
    loglik = own_lse - 0.5 * jnp.sum(points_f * points_f * inv_var[None, :], axis=1) + const_term
    return (resp_rows, counts, new_means_t, loglik)


def solution(mesh):
    axes = ("y", "h", "l", "x", "c")
    mesh = Mesh(mesh.devices.reshape(4, 4, 2, 4, 2), axes)
    comp, pt = ("x", "c"), ("y", "h", "l")
    return jax.shard_map(
        body,
        mesh=mesh,
        in_specs=(P(axes, None), P(comp, None), P(comp), P()),
        out_specs=(P(axes, None), P(comp), P(pt, comp), P(axes)),
        check_vma=False,
    )
```

```python
import functools
import math

import jax
import jax.numpy as jnp
from jax import lax
from jax.experimental import pallas as pl
from jax.experimental.pallas import tpu as pltpu
from jax.sharding import Mesh
from jax.sharding import PartitionSpec as P

BF = jnp.bfloat16
F32 = jnp.float32
VMEM_LIMIT = 24 * 1024 * 1024
VMEM = pltpu.VMEM
SIZES = {"y": 4, "x": 4, "c": 2}


def shift(value, axis, step):
    n = SIZES[axis]
    return lax.ppermute(value, axis, [(i, (i + step) % n) for i in range(n)])


def still(value):
    return pltpu.with_memory_space_constraint(value, pltpu.HBM)


def params():
    return pltpu.CompilerParams(vmem_limit_bytes=VMEM_LIMIT)


def whole():
    return pl.BlockSpec(memory_space=VMEM)


def scalar():
    return pl.BlockSpec(memory_space=pltpu.SMEM)


def anywhere(n=1):
    return [pl.BlockSpec(memory_space=pl.ANY)] * n


def hbm(n=1):
    return [pl.BlockSpec(memory_space=pltpu.HBM)] * n


def prepare_kernel(means, inv_var, weights, scaled, row):
    values = means[...].astype(F32)
    product = values * inv_var[...]
    scaled[...] = product.astype(BF)
    square = values * product
    norm = functools.reduce(jnp.add, [square[:, i : i + 128] for i in range(0, 1024, 128)])
    norm = 0.5 * jnp.sum(norm, axis=1, keepdims=True)
    for i in range(0, 512, 128):
        row[:, i : i + 128] = weights[:, i : i + 128] - line(norm[i : i + 128])


def prepare(means, inv_var, log_weights):
    return pl.pallas_call(
        prepare_kernel,
        grid=(4,),
        in_specs=[
            pl.BlockSpec((512, 1024), lambda i: (i, 0)),
            pl.BlockSpec((1, 1024), lambda i: (0, 0)),
            pl.BlockSpec((1, 512), lambda i: (0, i)),
        ],
        out_specs=(
            pl.BlockSpec((512, 1024), lambda i: (i, 0)),
            pl.BlockSpec((1, 512), lambda i: (0, i)),
        ),
        out_shape=(
            pltpu.HBM((2048, 1024), BF),
            jax.ShapeDtypeStruct((1, 2048), F32),
        ),
        compiler_params=params(),
        cost_estimate=pl.CostEstimate(flops=6 << 21, bytes_accessed=8 << 20, transcendentals=0),
    )(still(means), still(inv_var.reshape(1, 1024)), still(log_weights.reshape(1, 2048)))


def place_kernel(at, own, before, after, far, *refs):
    out = refs[-1]
    x = at[0]
    for step, piece in ((0, own), (3, before), (1, after), (2, far)):
        slot = lax.rem(x + step, 4)
        out[pl.ds(pl.multiple_of(slot * 64, 64), 64), :] = piece[...]


def gather_x(at, own, ahead, there=()):
    parts = (own, shift(own, "x", 1), shift(own, "x", -1), shift(own, "x", 2))
    return pl.pallas_call(
        place_kernel,
        out_shape=jax.ShapeDtypeStruct((256, 1024), BF),
        in_specs=[scalar()] + [whole()] * 4 + hbm(len(ahead)) + anywhere(len(there)),
        out_specs=whole(),
        compiler_params=params(),
    )(at, *parts, *(still(a) for a in ahead), *there)


def column(row):
    return jnp.transpose(jnp.broadcast_to(row, (128, 128)))[:, 0:1]


def line(col):
    return jnp.transpose(jnp.broadcast_to(col, (128, 128)))[0:1, :]


def score_kernel(at, own, other, scaled, bias, score, share, rows, peak, total):
    step = pl.program_id(0)
    c = at[1]

    @pl.when(step == 0)
    def _():
        rows[pl.ds(pl.multiple_of(c * 256, 256), 256), :] = own[...]
        rows[pl.ds(pl.multiple_of((1 - c) * 256, 256), 256), :] = other[...]
        peak[...] = jnp.full_like(peak, -jnp.inf)
        total[...] = jnp.zeros_like(total)

    for r in range(2):
        cut = slice(r * 256, r * 256 + 256)
        tile = lax.dot_general(
            rows[cut, :], scaled[...], (((1,), (1,)), ((), ())), preferred_element_type=F32
        )
        tile = tile + bias[...]
        score[cut, :] = tile
        lanes = [tile[:, i : i + 128] for i in range(0, tile.shape[1], 128)]
        old = peak[cut, :]
        top = functools.reduce(jnp.maximum, lanes, old)
        added = functools.reduce(jnp.add, [jnp.exp(lane - top) for lane in lanes])
        total[cut, :] = total[cut, :] * jnp.exp(old - top) + added
        peak[cut, :] = top

    @pl.when(step == pl.num_programs(0) - 1)
    def _():
        for b in range(4):
            cut = slice(b * 128, b * 128 + 128)
            top = jnp.max(peak[cut, :], axis=1, keepdims=True)
            mass = jnp.sum(total[cut, :] * jnp.exp(peak[cut, :] - top), axis=1, keepdims=True)
            share[:, b, :] = jnp.broadcast_to(line(top + jnp.log(mass)), (32, 128))


def scores(at, own, other, scaled, bias_row):
    width = 512
    return pl.pallas_call(
        score_kernel,
        grid=(2048 // width,),
        out_shape=(
            pltpu.HBM((512, 2048), F32),
            jax.ShapeDtypeStruct((32, 4, 128), F32),
        ),
        in_specs=[
            scalar(),
            pl.BlockSpec((256, 1024), lambda i: (0, 0)),
            pl.BlockSpec((256, 1024), lambda i: (0, 0)),
            pl.BlockSpec((width, 1024), lambda i: (i, 0)),
            pl.BlockSpec((1, width), lambda i: (0, i)),
        ],
        out_specs=(
            pl.BlockSpec((512, width), lambda i: (0, i)),
            pl.BlockSpec((32, 4, 128), lambda i: (0, 0, 0)),
        ),
        scratch_shapes=[VMEM((512, 1024), BF), VMEM((512, 128), F32), VMEM((512, 128), F32)],
        compiler_params=params(),
        cost_estimate=pl.CostEstimate(
            flops=2 * 512 * 2048 * 1024, bytes_accessed=9 << 20, transcendentals=1 << 20
        ),
    )(at, own, other, still(scaled), bias_row)


def joined(shares):
    top = jnp.max(shares, axis=0)
    return top + jnp.log(jnp.sum(jnp.exp(shares - top[None]), axis=0))


def hold_kernel(*refs):
    del refs


def hold(value, *first):
    return pl.pallas_call(
        hold_kernel,
        out_shape=pltpu.HBM(value.shape, value.dtype),
        in_specs=hbm() + anywhere(len(first)),
        out_specs=pl.BlockSpec(memory_space=pltpu.HBM),
        input_output_aliases={0: 0},
        compiler_params=params(),
    )(value, *first)


def sums_kernel(at, shares, scaled, bias, *refs):
    pieces = refs[:8]
    sums = refs[9]
    rows, weights, lse, norms, sems = refs[10:]
    copies = [
        pltpu.make_async_copy(piece, rows.at[pl.ds(i * 256, 256)], sems.at[i])
        for i, piece in enumerate(pieces)
    ]
    for copy in copies:
        copy.start()
    y, c = at[2], at[1]
    for yy in range(4):
        lse[pl.ds(yy * 4, 4), :] = joined(shares[yy])
    parts = []
    for i in range(8):
        there = lax.rem(y + (0, 3, 1, 2)[i // 2], 4)
        core = c if i % 2 == 0 else 1 - c
        line_at = there * 4 + core * 2
        parts += [lse[pl.ds(line_at, 1), :], lse[pl.ds(line_at + 1, 1), :]]
    norms[...] = jnp.transpose(jnp.concatenate(parts + [jnp.zeros((112, 128), F32)], axis=0))
    count = jnp.zeros((8, 512), F32)
    for g in range(2):
        for copy in copies[g * 4 : g * 4 + 4]:
            copy.wait()
        score = lax.dot_general(
            rows[g * 1024 : g * 1024 + 1024, :],
            scaled[...],
            (((1,), (1,)), ((), ())),
            preferred_element_type=F32,
        )
        for q in range(8):
            j = g * 8 + q
            shifted = score[q * 128 : q * 128 + 128, :] + (bias[...] - norms[:, j : j + 1])
            weight = jnp.exp(shifted).astype(BF)
            weights[j * 128 : j * 128 + 128, :] = weight
            weight = weight.astype(F32)
            count = count + functools.reduce(
                jnp.add, [weight[t : t + 8, :] for t in range(0, 128, 8)]
            )
    count = jnp.sum(count, axis=0, keepdims=True)
    lines = jnp.concatenate([count[:, b : b + 128] for b in range(0, 512, 128)], axis=0)
    high = lines.astype(BF).astype(F32)
    tail = jnp.concatenate([high, lines - high], axis=0).astype(BF)
    sums[:, 128:136, :] = jnp.broadcast_to(tail[None], (32, 8, 128))
    block = lax.dot_general(
        rows[...], weights[...], (((0,), (0,)), ((), ())), preferred_element_type=F32
    ).astype(BF)
    for q in range(4):
        part = block[:, q * 128 : q * 128 + 128].reshape(32, 32, 128)
        sums[:, q * 32 : q * 32 + 32, :] = part


def partial_sums(at, shares, scaled, bias_row, pieces, first):
    return pl.pallas_call(
        sums_kernel,
        grid_spec=pltpu.PrefetchScalarGridSpec(
            num_scalar_prefetch=1,
            grid=(1,),
            in_specs=[
                pl.BlockSpec((4, 8, 4, 128), lambda i, at: (0, 0, 0, 0)),
                pl.BlockSpec((512, 1024), lambda i, at: (at[2], 0)),
                pl.BlockSpec((1, 512), lambda i, at: (0, at[2])),
            ]
            + anywhere(9),
            out_specs=pl.BlockSpec((32, 136, 128), lambda i, at: (0, 0, 0)),
            scratch_shapes=[
                VMEM((2048, 1024), BF),
                VMEM((2048, 512), BF),
                VMEM((16, 128), F32),
                VMEM((128, 128), F32),
                pltpu.SemaphoreType.DMA((8,)),
            ],
        ),
        out_shape=pltpu.HBM((32, 136, 128), BF),
        compiler_params=params(),
        cost_estimate=pl.CostEstimate(
            flops=4 * 512 * 2048 * 1024, bytes_accessed=8 << 20, transcendentals=1 << 20
        ),
    )(at, shares, still(scaled), bias_row, *pieces, first)


def resp_kernel(at, shares, score, *refs):
    outs, out_across = refs[:6], refs[6]
    norm, held, sems, across = refs[7:]
    x, c, y = at[0], at[1], at[2]
    copies = []
    for j in range(8):
        core = 1 - c if j < 4 else c
        start = pl.multiple_of(core * 256 + lax.rem(x + j % 4, 4) * 64, 64)
        copies.append(
            (start, pltpu.make_async_copy(score.at[pl.ds(start, 64)], held.at[j], sems.at[j]))
        )
    for _, copy in copies:
        copy.start()
    lse = joined(shares[y])
    for b in range(4):
        norm[b * 128 : b * 128 + 128, :] = jnp.transpose(
            jnp.broadcast_to(lse[b : b + 1, :], (128, 128))
        )
    for j, (start, copy) in enumerate(copies):
        copy.wait()
        block = jnp.exp(held[j] - norm[pl.ds(start, 64), 0:1]).astype(BF)
        if j % 4 == 2:
            across[j // 4 * 64 : j // 4 * 64 + 64, :] = block
        else:
            outs[(0, 2, None, 4, 1, 3, None, 5)[j]][...] = block
    copy = pltpu.make_async_copy(across, out_across, sems.at[0])
    copy.start()
    copy.wait()


def responsibilities(at, shares, score):
    return pl.pallas_call(
        resp_kernel,
        in_specs=[scalar(), whole()] + hbm(),
        out_specs=[whole()] * 6 + hbm(),
        scratch_shapes=[
            VMEM((512, 128), F32),
            VMEM((8, 64, 2048), F32),
            pltpu.SemaphoreType.DMA((8,)),
            VMEM((128, 2048), BF),
        ],
        out_shape=[jax.ShapeDtypeStruct((64, 2048), BF)] * 6 + [pltpu.HBM((128, 2048), BF)],
        compiler_params=params(),
        cost_estimate=pl.CostEstimate(flops=1 << 21, bytes_accessed=6 << 20, transcendentals=1 << 20),
    )(at, shares, still(score))


def cut_kernel(at, means, ahead, out, turned):
    del ahead
    for i in range(0, 2048, 128):
        turned[:, i : i + 128] = jnp.transpose(means[i : i + 128, :].astype(F32))
    out[...] = turned[pl.ds(pl.multiple_of(lax.rem(at[3], 4) * 32, 32), 32), :]


def mean_columns(at, means, ahead):
    return pl.pallas_call(
        cut_kernel,
        grid_spec=pltpu.PrefetchScalarGridSpec(
            num_scalar_prefetch=1,
            grid=(1,),
            in_specs=[pl.BlockSpec((2048, 128), lambda i, at: (0, at[3] // 4))] + anywhere(),
            out_specs=pl.BlockSpec((32, 2048), lambda i, at: (0, 0)),
            scratch_shapes=[VMEM((128, 2048), F32)],
        ),
        out_shape=pltpu.HBM((32, 2048), F32),
        compiler_params=params(),
    )(at, still(means), ahead)


def finish_kernel(sent, means, new, counts):
    for y in range(4):
        total = sent[y * 8, :, :].astype(F32)
        for z in range(1, 8):
            total = total + sent[y * 8 + z, :, :].astype(F32)
        count = total[128:132, :] + total[132:136, :]
        counts[y * 4 : y * 4 + 4, :] = count
        for q in range(4):
            cut = slice(y * 512 + q * 128, y * 512 + q * 128 + 128)
            part = total[q * 32 : q * 32 + 32, :] + means[:, cut]
            new[:, cut] = part / (count[q : q + 1, :] + 1.0)


def finish(sent, mean_cols):
    return pl.pallas_call(
        finish_kernel,
        grid=(1,),
        in_specs=[
            pl.BlockSpec((32, 136, 128), lambda i: (0, 0, 0)),
            pl.BlockSpec((32, 2048), lambda i: (0, 0)),
        ],
        out_specs=[
            pl.BlockSpec((32, 2048), lambda i: (0, 0)),
            pl.BlockSpec((16, 128), lambda i: (0, 0)),
        ],
        out_shape=[
            jax.ShapeDtypeStruct((32, 2048), F32),
            jax.ShapeDtypeStruct((16, 128), F32),
        ],
        compiler_params=params(),
    )(sent, still(mean_cols))


def lay_kernel(at, *refs):
    pieces, out, sems = refs[:8], refs[8], refs[9]
    x, c = at[0], at[1]
    copies = []
    for j in range(8):
        core = 1 - c if j < 4 else c
        comp = lax.rem(x + 4 - j % 4, 4) * 2 + core
        spot = out.at[:, pl.ds(pl.multiple_of(comp * 2048, 2048), 2048)]
        piece = pieces[j].at[pl.ds(64, 64)] if j == 6 else pieces[j]
        copies.append(pltpu.make_async_copy(piece, spot, sems.at[j]))
    for copy in copies:
        copy.start()
    for copy in copies:
        copy.wait()


def lay_out(at, pieces):
    return pl.pallas_call(
        lay_kernel,
        in_specs=[scalar()] + [whole()] * 8,
        out_specs=pl.BlockSpec(memory_space=pl.ANY),
        scratch_shapes=[pltpu.SemaphoreType.DMA((8,))],
        out_shape=jax.ShapeDtypeStruct((64, 16384), BF),
        compiler_params=params(),
        cost_estimate=pl.CostEstimate(flops=0, bytes_accessed=4 << 20, transcendentals=0),
    )(at, *pieces)


def body(points, means, log_weights, inv_var):
    x, c, y, h, l = (lax.axis_index(a) for a in "xcyhl")
    at = jnp.stack([x, c, y, y * 8 + h * 2 + l, l]).astype(jnp.int32)

    far = shift(points, "y", 2)
    scaled, bias_row = prepare(means, inv_var, log_weights)

    own = gather_x(at, points, (scaled,), (far,))
    other = shift(own, "c", 1)
    before = shift(own, "y", 1)
    after = shift(own, "y", -1)
    score, share = scores(at, own, other, scaled, bias_row)

    shares = lax.all_to_all(share, ("y", "x", "c"), split_axis=0, concat_axis=0, tiled=True)
    mean_cols = mean_columns(at, means, share)
    far = gather_x(at, far, (mean_cols,), (shares,))
    shares = shares.reshape(4, 8, 4, 128)
    pieces = [own, other]
    for mine in (before, after, far):
        pieces += [mine, shift(mine, "c", 1)]

    blocks = responsibilities(at, shares, score)
    near = [shift(blocks[2], "x", 1), shift(blocks[4], "x", 3)]
    sums = partial_sums(at, shares, scaled, bias_row, pieces, blocks[0])
    sums = hold(sums, *near)
    across = shift(hold(blocks[6], still(sums)), "x", 2)
    mine = [blocks[1], shift(blocks[3], "x", 1), across, shift(blocks[5], "x", 3)]
    sent = lax.all_to_all(sums, ("y", "h", "l"), split_axis=0, concat_axis=0, tiled=True)
    theirs = [shift(b, "c", 1) for b in (blocks[0], near[0], across[:64], near[1])]
    held = theirs + mine
    resp_rows = lay_out(at, held)

    new_means_t, counts = finish(sent, mean_cols)
    counts = counts.reshape(2048)

    lse = joined(lax.dynamic_index_in_dim(shares, y, 0, keepdims=False)).reshape(8, 64)
    own_lse = lax.dynamic_index_in_dim(lse, c * 4 + x, 0, keepdims=False)
    points_f = points.astype(F32)
    const_term = 0.5 * jnp.sum(jnp.log(inv_var)) - 0.5 * 1024 * math.log(2.0 * math.pi)
    loglik = own_lse - 0.5 * jnp.sum(points_f * points_f * inv_var[None, :], axis=1) + const_term
    return (resp_rows, counts, new_means_t, loglik)


def solution(mesh):
    axes = ("y", "h", "l", "x", "c")
    mesh = Mesh(mesh.devices.reshape(4, 4, 2, 4, 2), axes)
    comp, pt = ("x", "c"), ("y", "h", "l")
    return jax.shard_map(
        body,
        mesh=mesh,
        in_specs=(P(axes, None), P(comp, None), P(comp), P()),
        out_specs=(P(axes, None), P(comp), P(pt, comp), P(axes)),
        check_vma=False,
    )
```

```python
import functools
import math

import jax
import jax.numpy as jnp
from jax import lax
from jax.experimental import pallas as pl
from jax.experimental.pallas import tpu as pltpu
from jax.sharding import Mesh
from jax.sharding import PartitionSpec as P

BF = jnp.bfloat16
F32 = jnp.float32
VMEM_LIMIT = 24 * 1024 * 1024
VMEM = pltpu.VMEM
SIZES = {"y": 4, "x": 4, "c": 2}


def shift(value, axis, step):
    n = SIZES[axis]
    return lax.ppermute(value, axis, [(i, (i + step) % n) for i in range(n)])


def still(value):
    return pltpu.with_memory_space_constraint(value, pltpu.HBM)


def params():
    return pltpu.CompilerParams(vmem_limit_bytes=VMEM_LIMIT)


def whole():
    return pl.BlockSpec(memory_space=VMEM)


def scalar():
    return pl.BlockSpec(memory_space=pltpu.SMEM)


def anywhere(n=1):
    return [pl.BlockSpec(memory_space=pl.ANY)] * n


def hbm(n=1):
    return [pl.BlockSpec(memory_space=pltpu.HBM)] * n


def prepare_kernel(means, inv_var, weights, scaled, row):
    values = means[...].astype(F32)
    product = values * inv_var[...]
    scaled[...] = product.astype(BF)
    square = values * product
    norm = functools.reduce(jnp.add, [square[:, i : i + 128] for i in range(0, 1024, 128)])
    norm = 0.5 * jnp.sum(norm, axis=1, keepdims=True)
    for i in range(0, 512, 128):
        row[:, i : i + 128] = weights[:, i : i + 128] - line(norm[i : i + 128])


def prepare(means, inv_var, log_weights):
    return pl.pallas_call(
        prepare_kernel,
        grid=(4,),
        in_specs=[
            pl.BlockSpec((512, 1024), lambda i: (i, 0)),
            pl.BlockSpec((1, 1024), lambda i: (0, 0)),
            pl.BlockSpec((1, 512), lambda i: (0, i)),
        ],
        out_specs=(
            pl.BlockSpec((512, 1024), lambda i: (i, 0)),
            pl.BlockSpec((1, 512), lambda i: (0, i)),
        ),
        out_shape=(
            pltpu.HBM((2048, 1024), BF),
            jax.ShapeDtypeStruct((1, 2048), F32),
        ),
        compiler_params=params(),
        cost_estimate=pl.CostEstimate(flops=6 << 21, bytes_accessed=8 << 20, transcendentals=0),
    )(still(means), still(inv_var.reshape(1, 1024)), still(log_weights.reshape(1, 2048)))


def place_kernel(at, own, before, after, far, *refs):
    out = refs[-1]
    x = at[0]
    for step, piece in ((0, own), (3, before), (1, after), (2, far)):
        slot = lax.rem(x + step, 4)
        out[pl.ds(pl.multiple_of(slot * 64, 64), 64), :] = piece[...]


def gather_x(at, own, ahead, there=()):
    parts = (own, shift(own, "x", 1), shift(own, "x", -1), shift(own, "x", 2))
    return pl.pallas_call(
        place_kernel,
        out_shape=jax.ShapeDtypeStruct((256, 1024), BF),
        in_specs=[scalar()] + [whole()] * 4 + hbm(len(ahead)) + anywhere(len(there)),
        out_specs=whole(),
        compiler_params=params(),
    )(at, *parts, *(still(a) for a in ahead), *there)


def column(row):
    return jnp.transpose(jnp.broadcast_to(row, (128, 128)))[:, 0:1]


def line(col):
    return jnp.transpose(jnp.broadcast_to(col, (128, 128)))[0:1, :]


def score_kernel(at, own, other, scaled, bias, score, share, rows, peak, total):
    step = pl.program_id(0)
    c = at[1]

    @pl.when(step == 0)
    def _():
        rows[pl.ds(pl.multiple_of(c * 256, 256), 256), :] = own[...]
        rows[pl.ds(pl.multiple_of((1 - c) * 256, 256), 256), :] = other[...]
        peak[...] = jnp.full_like(peak, -jnp.inf)
        total[...] = jnp.zeros_like(total)

    for r in range(2):
        cut = slice(r * 256, r * 256 + 256)
        tile = lax.dot_general(
            rows[cut, :], scaled[...], (((1,), (1,)), ((), ())), preferred_element_type=F32
        )
        tile = tile + bias[...]
        score[cut, :] = tile
        lanes = [tile[:, i : i + 128] for i in range(0, tile.shape[1], 128)]
        old = peak[cut, :]
        top = functools.reduce(jnp.maximum, lanes, old)
        added = functools.reduce(jnp.add, [jnp.exp(lane - top) for lane in lanes])
        total[cut, :] = total[cut, :] * jnp.exp(old - top) + added
        peak[cut, :] = top

    @pl.when(step == pl.num_programs(0) - 1)
    def _():
        for b in range(4):
            cut = slice(b * 128, b * 128 + 128)
            top = jnp.max(peak[cut, :], axis=1, keepdims=True)
            mass = jnp.sum(total[cut, :] * jnp.exp(peak[cut, :] - top), axis=1, keepdims=True)
            share[:, b, :] = jnp.broadcast_to(line(top + jnp.log(mass)), (32, 128))


def scores(at, own, other, scaled, bias_row):
    width = 1024
    return pl.pallas_call(
        score_kernel,
        grid=(2048 // width,),
        out_shape=(
            pltpu.HBM((512, 2048), F32),
            jax.ShapeDtypeStruct((32, 4, 128), F32),
        ),
        in_specs=[
            scalar(),
            pl.BlockSpec((256, 1024), lambda i: (0, 0)),
            pl.BlockSpec((256, 1024), lambda i: (0, 0)),
            pl.BlockSpec((width, 1024), lambda i: (i, 0)),
            pl.BlockSpec((1, width), lambda i: (0, i)),
        ],
        out_specs=(
            pl.BlockSpec((512, width), lambda i: (0, i)),
            pl.BlockSpec((32, 4, 128), lambda i: (0, 0, 0)),
        ),
        scratch_shapes=[VMEM((512, 1024), BF), VMEM((512, 128), F32), VMEM((512, 128), F32)],
        compiler_params=params(),
        cost_estimate=pl.CostEstimate(
            flops=2 * 512 * 2048 * 1024, bytes_accessed=9 << 20, transcendentals=1 << 20
        ),
    )(at, own, other, still(scaled), bias_row)


def joined(shares):
    top = jnp.max(shares, axis=0)
    return top + jnp.log(jnp.sum(jnp.exp(shares - top[None]), axis=0))


def hold_kernel(*refs):
    del refs


def hold(value, *first):
    return pl.pallas_call(
        hold_kernel,
        out_shape=pltpu.HBM(value.shape, value.dtype),
        in_specs=hbm() + anywhere(len(first)),
        out_specs=pl.BlockSpec(memory_space=pltpu.HBM),
        input_output_aliases={0: 0},
        compiler_params=params(),
    )(value, *first)


def sums_kernel(at, shares, scaled, bias, *refs):
    pieces = refs[:8]
    sums = refs[9]
    rows, weights, lse, norms, sems = refs[10:]
    copies = [
        pltpu.make_async_copy(piece, rows.at[pl.ds(i * 256, 256)], sems.at[i])
        for i, piece in enumerate(pieces)
    ]
    for copy in copies:
        copy.start()
    y, c = at[2], at[1]
    for yy in range(4):
        lse[pl.ds(yy * 4, 4), :] = joined(shares[yy])
    parts = []
    for i in range(8):
        there = lax.rem(y + (0, 3, 1, 2)[i // 2], 4)
        core = c if i % 2 == 0 else 1 - c
        line_at = there * 4 + core * 2
        parts += [lse[pl.ds(line_at, 1), :], lse[pl.ds(line_at + 1, 1), :]]
    norms[...] = jnp.transpose(jnp.concatenate(parts + [jnp.zeros((112, 128), F32)], axis=0))
    count = jnp.zeros((8, 512), F32)
    for g in range(2):
        for copy in copies[g * 4 : g * 4 + 4]:
            copy.wait()
        score = lax.dot_general(
            rows[g * 1024 : g * 1024 + 1024, :],
            scaled[...],
            (((1,), (1,)), ((), ())),
            preferred_element_type=F32,
        )
        for q in range(8):
            j = g * 8 + q
            shifted = score[q * 128 : q * 128 + 128, :] + (bias[...] - norms[:, j : j + 1])
            weight = jnp.exp(shifted).astype(BF)
            weights[j * 128 : j * 128 + 128, :] = weight
            weight = weight.astype(F32)
            count = count + functools.reduce(
                jnp.add, [weight[t : t + 8, :] for t in range(0, 128, 8)]
            )
    count = jnp.sum(count, axis=0, keepdims=True)
    lines = jnp.concatenate([count[:, b : b + 128] for b in range(0, 512, 128)], axis=0)
    high = lines.astype(BF).astype(F32)
    tail = jnp.concatenate([high, lines - high], axis=0).astype(BF)
    sums[:, 128:136, :] = jnp.broadcast_to(tail[None], (32, 8, 128))
    block = lax.dot_general(
        rows[...], weights[...], (((0,), (0,)), ((), ())), preferred_element_type=F32
    ).astype(BF)
    for q in range(4):
        part = block[:, q * 128 : q * 128 + 128].reshape(32, 32, 128)
        sums[:, q * 32 : q * 32 + 32, :] = part


def partial_sums(at, shares, scaled, bias_row, pieces, first):
    return pl.pallas_call(
        sums_kernel,
        grid_spec=pltpu.PrefetchScalarGridSpec(
            num_scalar_prefetch=1,
            grid=(1,),
            in_specs=[
                pl.BlockSpec((4, 8, 4, 128), lambda i, at: (0, 0, 0, 0)),
                pl.BlockSpec((512, 1024), lambda i, at: (at[2], 0)),
                pl.BlockSpec((1, 512), lambda i, at: (0, at[2])),
            ]
            + anywhere(9),
            out_specs=pl.BlockSpec((32, 136, 128), lambda i, at: (0, 0, 0)),
            scratch_shapes=[
                VMEM((2048, 1024), BF),
                VMEM((2048, 512), BF),
                VMEM((16, 128), F32),
                VMEM((128, 128), F32),
                pltpu.SemaphoreType.DMA((8,)),
            ],
        ),
        out_shape=pltpu.HBM((32, 136, 128), BF),
        compiler_params=params(),
        cost_estimate=pl.CostEstimate(
            flops=4 * 512 * 2048 * 1024, bytes_accessed=8 << 20, transcendentals=1 << 20
        ),
    )(at, shares, still(scaled), bias_row, *pieces, first)


def resp_kernel(at, shares, score, *refs):
    outs, out_across = refs[:6], refs[6]
    norm, held, sems, across = refs[7:]
    x, c, y = at[0], at[1], at[2]
    copies = []
    for j in range(8):
        core = 1 - c if j < 4 else c
        start = pl.multiple_of(core * 256 + lax.rem(x + j % 4, 4) * 64, 64)
        copies.append(
            (start, pltpu.make_async_copy(score.at[pl.ds(start, 64)], held.at[j], sems.at[j]))
        )
    for _, copy in copies:
        copy.start()
    lse = joined(shares[y])
    for b in range(4):
        norm[b * 128 : b * 128 + 128, :] = jnp.transpose(
            jnp.broadcast_to(lse[b : b + 1, :], (128, 128))
        )
    for j, (start, copy) in enumerate(copies):
        copy.wait()
        block = jnp.exp(held[j] - norm[pl.ds(start, 64), 0:1]).astype(BF)
        if j % 4 == 2:
            across[j // 4 * 64 : j // 4 * 64 + 64, :] = block
        else:
            outs[(0, 2, None, 4, 1, 3, None, 5)[j]][...] = block
    copy = pltpu.make_async_copy(across, out_across, sems.at[0])
    copy.start()
    copy.wait()


def responsibilities(at, shares, score):
    return pl.pallas_call(
        resp_kernel,
        in_specs=[scalar(), whole()] + hbm(),
        out_specs=[whole()] * 6 + hbm(),
        scratch_shapes=[
            VMEM((512, 128), F32),
            VMEM((8, 64, 2048), F32),
            pltpu.SemaphoreType.DMA((8,)),
            VMEM((128, 2048), BF),
        ],
        out_shape=[jax.ShapeDtypeStruct((64, 2048), BF)] * 6 + [pltpu.HBM((128, 2048), BF)],
        compiler_params=params(),
        cost_estimate=pl.CostEstimate(flops=1 << 21, bytes_accessed=6 << 20, transcendentals=1 << 20),
    )(at, shares, still(score))


def cut_kernel(at, means, ahead, out, turned):
    del ahead
    for i in range(0, 2048, 128):
        turned[:, i : i + 128] = jnp.transpose(means[i : i + 128, :].astype(F32))
    out[...] = turned[pl.ds(pl.multiple_of(lax.rem(at[3], 4) * 32, 32), 32), :]


def mean_columns(at, means, ahead):
    return pl.pallas_call(
        cut_kernel,
        grid_spec=pltpu.PrefetchScalarGridSpec(
            num_scalar_prefetch=1,
            grid=(1,),
            in_specs=[pl.BlockSpec((2048, 128), lambda i, at: (0, at[3] // 4))] + anywhere(),
            out_specs=pl.BlockSpec((32, 2048), lambda i, at: (0, 0)),
            scratch_shapes=[VMEM((128, 2048), F32)],
        ),
        out_shape=pltpu.HBM((32, 2048), F32),
        compiler_params=params(),
    )(at, still(means), ahead)


def finish_kernel(sent, means, new, counts):
    for y in range(4):
        total = sent[y * 8, :, :].astype(F32)
        for z in range(1, 8):
            total = total + sent[y * 8 + z, :, :].astype(F32)
        count = total[128:132, :] + total[132:136, :]
        counts[y * 4 : y * 4 + 4, :] = count
        for q in range(4):
            cut = slice(y * 512 + q * 128, y * 512 + q * 128 + 128)
            part = total[q * 32 : q * 32 + 32, :] + means[:, cut]
            new[:, cut] = part / (count[q : q + 1, :] + 1.0)


def finish(sent, mean_cols):
    return pl.pallas_call(
        finish_kernel,
        grid=(1,),
        in_specs=[
            pl.BlockSpec((32, 136, 128), lambda i: (0, 0, 0)),
            pl.BlockSpec((32, 2048), lambda i: (0, 0)),
        ],
        out_specs=[
            pl.BlockSpec((32, 2048), lambda i: (0, 0)),
            pl.BlockSpec((16, 128), lambda i: (0, 0)),
        ],
        out_shape=[
            jax.ShapeDtypeStruct((32, 2048), F32),
            jax.ShapeDtypeStruct((16, 128), F32),
        ],
        compiler_params=params(),
    )(sent, still(mean_cols))


def lay_kernel(at, *refs):
    pieces, out, sems = refs[:8], refs[8], refs[9]
    x, c = at[0], at[1]
    copies = []
    for j in range(8):
        core = 1 - c if j < 4 else c
        comp = lax.rem(x + 4 - j % 4, 4) * 2 + core
        spot = out.at[:, pl.ds(pl.multiple_of(comp * 2048, 2048), 2048)]
        piece = pieces[j].at[pl.ds(64, 64)] if j == 6 else pieces[j]
        copies.append(pltpu.make_async_copy(piece, spot, sems.at[j]))
    for copy in copies:
        copy.start()
    for copy in copies:
        copy.wait()


def lay_out(at, pieces):
    return pl.pallas_call(
        lay_kernel,
        in_specs=[scalar()] + [whole()] * 8,
        out_specs=pl.BlockSpec(memory_space=pl.ANY),
        scratch_shapes=[pltpu.SemaphoreType.DMA((8,))],
        out_shape=jax.ShapeDtypeStruct((64, 16384), BF),
        compiler_params=params(),
        cost_estimate=pl.CostEstimate(flops=0, bytes_accessed=4 << 20, transcendentals=0),
    )(at, *pieces)


def body(points, means, log_weights, inv_var):
    x, c, y, h, l = (lax.axis_index(a) for a in "xcyhl")
    at = jnp.stack([x, c, y, y * 8 + h * 2 + l, l]).astype(jnp.int32)

    far = shift(points, "y", 2)
    scaled, bias_row = prepare(means, inv_var, log_weights)

    own = gather_x(at, points, (scaled,), (far,))
    other = shift(own, "c", 1)
    before = shift(own, "y", 1)
    after = shift(own, "y", -1)
    score, share = scores(at, own, other, scaled, bias_row)

    shares = lax.all_to_all(share, ("y", "x", "c"), split_axis=0, concat_axis=0, tiled=True)
    mean_cols = mean_columns(at, means, share)
    far = gather_x(at, far, (mean_cols,), (shares,))
    shares = shares.reshape(4, 8, 4, 128)
    pieces = [own, other]
    for mine in (before, after, far):
        pieces += [mine, shift(mine, "c", 1)]

    blocks = responsibilities(at, shares, score)
    near = [shift(blocks[2], "x", 1), shift(blocks[4], "x", 3)]
    sums = partial_sums(at, shares, scaled, bias_row, pieces, blocks[0])
    sums = hold(sums, *near)
    across = shift(hold(blocks[6], still(sums)), "x", 2)
    mine = [blocks[1], shift(blocks[3], "x", 1), across, shift(blocks[5], "x", 3)]
    sent = lax.all_to_all(sums, ("y", "h", "l"), split_axis=0, concat_axis=0, tiled=True)
    theirs = [shift(b, "c", 1) for b in (blocks[0], near[0], across[:64], near[1])]
    held = theirs + mine
    resp_rows = lay_out(at, held)

    new_means_t, counts = finish(sent, mean_cols)
    counts = counts.reshape(2048)

    lse = joined(lax.dynamic_index_in_dim(shares, y, 0, keepdims=False)).reshape(8, 64)
    own_lse = lax.dynamic_index_in_dim(lse, c * 4 + x, 0, keepdims=False)
    points_f = points.astype(F32)
    const_term = 0.5 * jnp.sum(jnp.log(inv_var)) - 0.5 * 1024 * math.log(2.0 * math.pi)
    loglik = own_lse - 0.5 * jnp.sum(points_f * points_f * inv_var[None, :], axis=1) + const_term
    return (resp_rows, counts, new_means_t, loglik)


def solution(mesh):
    axes = ("y", "h", "l", "x", "c")
    mesh = Mesh(mesh.devices.reshape(4, 4, 2, 4, 2), axes)
    comp, pt = ("x", "c"), ("y", "h", "l")
    return jax.shard_map(
        body,
        mesh=mesh,
        in_specs=(P(axes, None), P(comp, None), P(comp), P()),
        out_specs=(P(axes, None), P(comp), P(pt, comp), P(axes)),
        check_vma=False,
    )
```
